32 devices in a mesh: stream: 4 (over y, x), seq: 8 (over z, core).
Axes of the slice: x: 2, y: 2, z: 4, core: 2. Of those that a mesh axis runs over, the one named last changes fastest.
Arguments:
- conv_input: bfloat16 [4, 32768, 1280], P('stream', 'seq'), may hold values from -6 to 6
- conv_weight: float32 [4, 1280], replicated, may hold values from -3 to 3
- conv_bias: float32 [1280], replicated, may hold values from -1 to 1
- step_size: float32 [4, 16, 32768], P('stream', None, 'seq'), may hold values from 0.0005 to 0.005
- log_decay: float32 [4, 16, 32768], P('stream', None, 'seq'), as said below
- skip_gain: float32 [16], replicated, may hold values from 0.5 to 1.5
- doc_bounds: int32 [4, 32], P('stream'), may hold values from 1 to 32768, as said below
- doc_owner: int32 [4, 32], P('stream'), may hold values from 0 to 3, as said below
Outputs:
- mixed_out: bfloat16 [4, 32768, 1024], P('stream', 'seq')
- handoff_ssm: float32 [4, 8, 4, 2, 16, 64, 128], P('stream', 'seq')
- handoff_conv: bfloat16 [4, 8, 4, 2, 3, 1280], P('stream', 'seq')
The draws below stay inside these ranges and needn't reach their ends.
Inputs may be any that keep to these rules, and one draw needn't show every extreme that they name: `doc_bounds`: each row rises and never falls; the real documents of a stream end at 32768, after which every entry equals 32768. At most 4 real documents have their last position in one run of 4096 positions starting at a multiple of 4096. `doc_owner`: among the real documents whose last positions lie in one such run of one stream, no owner is named more than 2 times. `log_decay`: never positive.
All inputs are finite; a program needn't handle non-finite values.
Results may differ from the reference program's by a relative error of at most 0.006.
Values may be sent and summed in bfloat16 or wider, within the bound.
No kernel may reach another device: no remote copies, remote signals or barrier semaphores. Data moves between devices by JAX's collectives and lax.ppermute only.
A program may use at most 256 MiB of HBM per device.

```python
import math
import jax
import jax.numpy as jnp
from jax import lax

H = 16
P_SIZE = 64
N = 128
CONV = 4
SPAN = 256
EMAX = 4
CAP = 2
TOK_DEV = 4096
CH = 1280
PROMPT_STREAMS = 4
STREAM_LENGTH = 32768
NB = 32
N_STREAM = 4
N_SEQ = 8


def shared_docs(key):
    key_sequence = jax.random.split(jax.random.fold_in(key, 11), 7)
    shard_ids = jnp.arange(N_SEQ)
    run_length = N_SEQ // 2 + 1
    run_start = jax.random.randint(key_sequence[6], (PROMPT_STREAMS, 1), 1, N_SEQ - run_length)
    in_run = (shard_ids[None, :] >= run_start) & (shard_ids[None, :] < run_start + run_length)
    end_counts = jax.random.randint(key_sequence[0], (PROMPT_STREAMS, N_SEQ), 1, EMAX + 1)
    full_shard = run_start - 1
    end_counts = jnp.where(shard_ids[None, :] == full_shard, EMAX, end_counts)
    end_counts = jnp.where(in_run, 0, end_counts)
    pick_keys = jax.random.split(key_sequence[2], PROMPT_STREAMS * N_SEQ)
    offsets = jax.vmap(lambda one_key: jnp.sort(jax.random.permutation(one_key, TOK_DEV)[:EMAX]))(pick_keys)
    offsets = offsets.reshape(PROMPT_STREAMS, N_SEQ, EMAX)
    slot_ids = jnp.arange(EMAX)
    offsets = jnp.where((shard_ids[None, :, None] == N_SEQ - 1) & (slot_ids[None, None, :] == EMAX - 1), TOK_DEV - 1, offsets)
    used = slot_ids[None, None, :] >= EMAX - end_counts[:, :, None]
    end_points = jnp.where(used, shard_ids[None, :, None] * TOK_DEV + offsets + 1, STREAM_LENGTH)
    order_keys = jax.random.split(key_sequence[3], PROMPT_STREAMS * N_SEQ)
    shuffled = jax.vmap(lambda one_key: jax.random.permutation(one_key, EMAX))(order_keys).reshape(PROMPT_STREAMS, N_SEQ, EMAX)
    base_owner = jax.random.randint(key_sequence[4], (PROMPT_STREAMS, N_SEQ), 0, N_STREAM)
    full_owner = jax.random.randint(key_sequence[5], (), 0, N_STREAM)
    base_owner = jnp.where(shard_ids[None, :] == full_shard, full_owner, base_owner)
    owner_of = (base_owner[:, :, None] + shuffled // CAP) % N_STREAM
    flat_ends = end_points.reshape(PROMPT_STREAMS, NB).astype(jnp.int32)
    flat_owner = owner_of.reshape(PROMPT_STREAMS, NB).astype(jnp.int32)
    sorted_ends, sorted_owner = lax.sort((flat_ends, flat_owner), dimension=1, is_stable=True, num_keys=1)
    return (sorted_ends.astype(jnp.int32), sorted_owner.astype(jnp.int32))


def draw_doc_bounds(key, part):
    return shared_docs(key)[0]


def draw_doc_owner(key, part):
    return shared_docs(key)[1]


def draw_log_decay(key, part):
    key_sequence = jax.random.split(jax.random.fold_in(key, 5), 8)
    fast_count = jax.random.randint(key_sequence[0], (), max(1, H // 4), max(2, min(H, 3 * H // 4 + 1)))
    head_order = jax.random.permutation(key_sequence[1], H)
    is_fast = head_order < fast_count
    fast_rate = jnp.exp(jax.random.uniform(key_sequence[2], (H,), jnp.float32, math.log(1.0 / 50.0), math.log(1.0 / 30.0)))
    slow_rate = jax.random.uniform(key_sequence[3], (H,), jnp.float32, 0.05, 0.5) / STREAM_LENGTH
    decay_rate = jnp.where(is_fast, fast_rate, slow_rate)
    shard_factor = jnp.exp(jax.random.uniform(key_sequence[4], (PROMPT_STREAMS, H, N_SEQ), jnp.float32, math.log(0.5), math.log(2.0)))
    shard_factor = jnp.repeat(shard_factor, TOK_DEV, axis=2)
    token_factor = jnp.exp(jax.random.uniform(key_sequence[5], (PROMPT_STREAMS, H, STREAM_LENGTH), jnp.float32, math.log(0.5), math.log(2.0)))
    decay_factors = -decay_rate[None, :, None] * shard_factor * token_factor
    flurry_location = jax.random.randint(key_sequence[6], (PROMPT_STREAMS, 3), 0, STREAM_LENGTH)
    flurry_penalty = jax.random.uniform(key_sequence[7], (PROMPT_STREAMS, 3), jnp.float32, 0.2, 0.4)
    token_positions = jnp.arange(STREAM_LENGTH)
    flurry_discard = jnp.sum(jnp.where(token_positions[None, :, None] == flurry_location[:, None, :], jnp.log1p(-flurry_penalty)[:, None, :], 0.0), axis=2)
    return (decay_factors + flurry_discard[:, None, :]).astype(jnp.float32)


def block_levels(rng, extent, cuts, least, largest):
    def one(axis_at, blocks):
        draws = jax.random.uniform(jax.random.fold_in(jax.random.fold_in(rng, 6), axis_at), (blocks,), jnp.float32, least / len(cuts), largest / len(cuts))
        return jnp.repeat(jnp.exp(draws), extent[axis_at] // blocks).reshape((-1,) + (1,) * (len(extent) - axis_at - 1))

    level = one(*cuts[0])
    for cut in cuts[1:]:
        level = level * one(*cut)
    return level


def noise(stream_key, dims, scale, most, cuts=(), held_as=jnp.bfloat16):
    gain = block_levels(stream_key, dims, cuts, -0.22, 0.18) if cuts else 1.0
    result = jax.random.normal(stream_key, dims, jnp.float32) * scale * gain
    return jnp.minimum(jnp.maximum(result, -most), most).astype(held_as)


def setup_inputs(seed: int = 0) -> dict:
    seeds = jax.random.split(jax.random.key(seed), 9)
    conv_input = noise(seeds[0], (PROMPT_STREAMS, STREAM_LENGTH, CH), 1.0, 6.0, ((0, 4), (1, 8)))
    conv_weight = noise(seeds[1], (CONV, CH), CONV ** -0.5, 3.0, (), jnp.float32)
    conv_bias = jnp.clip(jax.random.uniform(seeds[2], (CH,), jnp.float32, -1.0, 1.0), -1.0, 1.0)
    step_size = jnp.clip(jnp.exp(math.log(0.005) - 2.30258502 * jax.random.uniform(seeds[3], (PROMPT_STREAMS, H, STREAM_LENGTH), jnp.float32) ** block_levels(seeds[3], (PROMPT_STREAMS, H, STREAM_LENGTH), ((0, 4), (2, 8)), -0.2, 0.2)), 0.0005, 0.005)
    log_decay = draw_log_decay(jax.random.fold_in(seeds[8], 71), 0)
    skip_gain = jnp.clip(jax.random.uniform(seeds[5], (H,), jnp.float32, 0.5, 1.5), 0.5, 1.5)
    doc_bounds = draw_doc_bounds(jax.random.fold_in(seeds[8], 71), 0)
    doc_owner = draw_doc_owner(jax.random.fold_in(seeds[8], 71), 0)
    return dict(conv_input=conv_input, conv_weight=conv_weight, conv_bias=conv_bias, step_size=step_size, log_decay=log_decay, skip_gain=skip_gain, doc_bounds=doc_bounds, doc_owner=doc_owner)


def split_product(c_rows, state):
    state_hi = state.astype(jnp.bfloat16)
    state_lo = (state - state_hi.astype(jnp.float32)).astype(jnp.bfloat16)
    c_wide = c_rows.astype(jnp.float32)
    first = jnp.einsum("tn,hpn->thp", c_wide, state_hi.astype(jnp.float32))
    second = jnp.einsum("tn,hpn->thp", c_wide, state_lo.astype(jnp.float32))
    return first + second


def conv_mix(conv_rows, doc_ids, conv_weight, conv_bias):
    values = conv_rows.astype(jnp.float32)
    mixed_sum = conv_bias[None, :] + conv_weight[0][None, :] * values
    for lag_step in range(1, CONV):
        moved_rows = jnp.concatenate([jnp.zeros((lag_step, values.shape[1]), jnp.float32), values[:-lag_step]], 0)
        moved_doc = jnp.concatenate([jnp.full((lag_step,), -1, jnp.int32), doc_ids[:-lag_step]], 0)
        mixed_sum = mixed_sum + conv_weight[lag_step][None, :] * jnp.where((moved_doc == doc_ids)[:, None], moved_rows, 0.0)
    return jax.nn.silu(mixed_sum).astype(jnp.bfloat16)


def span_output(x_span, b_span, c_span, dt_span, cum_decay, doc_span, prev_doc, state_in, skip_gain):
    row_count = doc_span.shape[0]
    head_count = dt_span.shape[0]
    scores = jnp.dot(c_span, b_span.T, preferred_element_type=jnp.float32)
    position = jnp.arange(row_count)
    causal = (position[:, None] >= position[None, :]) & (doc_span[:, None] == doc_span[None, :])
    spread = cum_decay[:, :, None] - cum_decay[:, None, :]
    weights = jnp.where(causal[None], jnp.exp(jnp.where(causal[None], spread, 0.0)) * scores[None] * dt_span[:, None, :], 0.0).astype(jnp.bfloat16)
    head_rows = x_span.reshape(row_count, head_count, -1)
    inner_part = jnp.einsum("hts,shp->thp", weights.astype(jnp.float32), head_rows.astype(jnp.float32))
    entry_gate = jnp.where((doc_span == prev_doc)[None, :], jnp.exp(cum_decay), 0.0)
    outer_part = split_product(c_span, state_in) * entry_gate.T[:, :, None]
    summed = inner_part + outer_part + skip_gain[None, :, None] * head_rows.astype(jnp.float32)
    return summed.reshape(row_count, -1)


def partial_state(x_span, b_span, dt_span, cum_decay, doc_span, last_row, doc_key):
    row_count = doc_span.shape[0]
    head_count = dt_span.shape[0]
    kept_rows = (jnp.arange(row_count) <= last_row) & (doc_span == doc_key)
    scaled = jnp.where(kept_rows[None, :], jnp.exp(cum_decay[:, last_row][:, None] - cum_decay) * dt_span, 0.0)
    loaded = (scaled.T[:, :, None] * x_span.reshape(row_count, head_count, -1).astype(jnp.float32)).astype(jnp.bfloat16)
    return jnp.einsum("shp,sn->hpn", loaded.astype(jnp.float32), b_span.astype(jnp.float32))


def one_stream(conv_rows, step_rows, decay_rows, bound_row, conv_weight, conv_bias, skip_gain):
    width = H * P_SIZE
    position = jnp.arange(STREAM_LENGTH, dtype=jnp.int32)
    doc_ids = jnp.searchsorted(bound_row, position, side="right").astype(jnp.int32)
    activated = conv_mix(conv_rows, doc_ids, conv_weight, conv_bias)
    count = STREAM_LENGTH // SPAN
    x_spans = activated[:, :width].reshape(count, SPAN, width)
    b_spans = activated[:, width:width + N].reshape(count, SPAN, N)
    c_spans = activated[:, width + N:].reshape(count, SPAN, N)
    dt_spans = step_rows.reshape(H, count, SPAN).transpose(1, 0, 2)
    ld_spans = decay_rows.reshape(H, count, SPAN).transpose(1, 0, 2)
    doc_spans = doc_ids.reshape(count, SPAN)
    prev_docs = jnp.concatenate([jnp.full((1,), -1, jnp.int32), doc_spans[:-1, -1]])

    def advance(state_in, item):
        x_span, b_span, c_span, dt_span, ld_span, doc_span, prev_doc = item
        cum_decay = jnp.cumsum(ld_span, axis=1)
        out_rows = span_output(x_span, b_span, c_span, dt_span, cum_decay, doc_span, prev_doc, state_in, skip_gain)
        block_state = partial_state(x_span, b_span, dt_span, cum_decay, doc_span, SPAN - 1, doc_span[-1])
        gate = jnp.where(doc_span[-1] == prev_doc, jnp.exp(cum_decay[:, -1]), 0.0)
        return block_state + gate[:, None, None] * state_in, (out_rows.astype(jnp.bfloat16), state_in)

    start_state = jnp.zeros((H, P_SIZE, N), jnp.float32)
    _, (out_spans, state_stack) = lax.scan(advance, start_state, (x_spans, b_spans, c_spans, dt_spans, ld_spans, doc_spans, prev_docs))
    padded = jnp.concatenate([jnp.zeros((CONV - 1, conv_rows.shape[1]), jnp.bfloat16), conv_rows], 0)

    def finish(doc_index):
        end_pos = bound_row[doc_index]
        start_pos = jnp.where(doc_index > 0, bound_row[jnp.maximum(doc_index - 1, 0)], 0)
        is_real = end_pos > start_pos
        last_pos = jnp.clip(end_pos - 1, 0, STREAM_LENGTH - 1)
        block = last_pos // SPAN
        offset = last_pos % SPAN
        cum_decay = jnp.cumsum(ld_spans[block], axis=1)
        state = partial_state(x_spans[block], b_spans[block], dt_spans[block], cum_decay, doc_spans[block], offset, doc_index)
        state = state + jnp.where(prev_docs[block] == doc_index, jnp.exp(cum_decay[:, offset]), 0.0)[:, None, None] * state_stack[block]
        tail_rows = lax.dynamic_slice_in_dim(padded, last_pos + 1, CONV - 1, 0)
        tail_pos = last_pos - (CONV - 2) + jnp.arange(CONV - 1, dtype=jnp.int32)
        tail = jnp.where((tail_pos >= start_pos)[:, None], tail_rows, jnp.zeros_like(tail_rows))
        return jnp.where(is_real, state, 0.0), tail, is_real, (last_pos // TOK_DEV).astype(jnp.int32)

    finals, tails, real_docs, shard_of = lax.map(finish, jnp.arange(NB, dtype=jnp.int32))
    return out_spans.reshape(STREAM_LENGTH, width), finals, tails, real_docs, shard_of


def reference(conv_input, conv_weight, conv_bias, step_size, log_decay, skip_gain, doc_bounds, doc_owner):
    handoff_ssm = jnp.zeros((N_STREAM, N_SEQ, PROMPT_STREAMS, CAP, H, P_SIZE, N), jnp.float32)
    handoff_conv = jnp.zeros((N_STREAM, N_SEQ, PROMPT_STREAMS, CAP, CONV - 1, H * P_SIZE + 2 * N), jnp.bfloat16)
    outputs = []
    doc_index = jnp.arange(NB, dtype=jnp.int32)
    for stream in range(PROMPT_STREAMS):
        out_rows, finals, tails, real_docs, shard_of = one_stream(conv_input[stream], step_size[stream], log_decay[stream], doc_bounds[stream], conv_weight, conv_bias, skip_gain)
        outputs.append(out_rows)
        owner_row = doc_owner[stream]
        same = real_docs[None, :] & (shard_of[None, :] == shard_of[:, None]) & (owner_row[None, :] == owner_row[:, None]) & (doc_index[None, :] < doc_index[:, None])
        slot_rank = jnp.sum(same.astype(jnp.int32), axis=1).astype(jnp.int32)
        target = jnp.where(real_docs, owner_row, N_STREAM).astype(jnp.int32)
        handoff_ssm = handoff_ssm.at[target, shard_of, stream, slot_rank].set(finals, mode="drop")
        handoff_conv = handoff_conv.at[target, shard_of, stream, slot_rank].set(tails, mode="drop")
    return jnp.stack(outputs), handoff_ssm, handoff_conv
```

```python
import functools

import jax
import jax.numpy as jnp
from jax import lax
from jax.experimental import pallas as pl
from jax.experimental.pallas import tpu as pltpu
from jax.sharding import PartitionSpec as P

P_SIZE = 64
N = 128
EMAX = 4
CAP = 2
CHUNK = 128
BLOCK = 256
FAR = 1 << 30
LOG2E = 1.4426950408889634
PAY = 144
TAIL = 32
VMEM = 56 * 1024 * 1024

F32 = jnp.float32
BF16 = jnp.bfloat16


def shifted(value, axis, steps):
    count = lax.axis_size(axis)
    leading, last = (max(0, -steps), min(count, count - steps))
    return lax.ppermute(value, axis, [(source, source + steps) for source in range(leading, last)])


def iota(shape, axis):
    return lax.broadcasted_iota(jnp.int32, shape, axis)


def outer_dot(left, right):
    return lax.dot_general(left, right, (((0,), (0,)), ((), ())), preferred_element_type=F32)


def halves(value):
    high = value.astype(BF16)
    low = (value - high.astype(F32)).astype(BF16)
    return jnp.concatenate([high, low], axis=0)


def thirds(value):
    high = value.astype(BF16)
    rest = value - high.astype(F32)
    mid = rest.astype(BF16)
    low = (rest - mid.astype(F32)).astype(BF16)
    return jnp.concatenate([high, mid, low], axis=0)


def spread_row(column, rep):
    return jnp.sum(rep * column, axis=0, keepdims=True)


def last_start(meta, place):
    start = meta[0]
    for slot in range(EMAX):
        end = meta[1 + slot]
        start = jnp.where(end <= place, end, start)
    return start


def next_end(meta, place):
    end = FAR
    for slot in reversed(range(EMAX)):
        end = jnp.where(meta[1 + slot] > place, meta[1 + slot], end)
    return end


def starts_of(meta, rows):
    start = jnp.full(rows.shape, meta[0], jnp.int32)
    for slot in range(EMAX):
        end = meta[1 + slot]
        start = jnp.where(rows >= end, end, start)
    return start


def read_docs(bounds, owners, meta, count, anchor, span):
    for slot in range(EMAX):
        meta[1 + slot] = FAR
        meta[5 + slot] = 0
    for owner in range(count.shape[0]):
        count[owner] = 0

    def one(index, carry):
        found, prior, start = carry
        end = bounds[0, index]
        owner = owners[0, index]
        mine = (end > prior) & (end > anchor) & (end <= anchor + span) & (found < EMAX)

        @pl.when(mine)
        def _():
            meta[1 + found] = end - anchor
            rank = count[owner]
            meta[5 + found] = jnp.where(rank < CAP, owner * CAP + rank, -1)
            count[owner] = rank + 1

        return found + mine.astype(jnp.int32), end, jnp.where(end <= anchor, end, start)

    zero = jnp.int32(0)
    _, _, start = lax.fori_loop(0, bounds.shape[1], one, (zero, zero, zero))
    meta[0] = start - anchor


def states_kernel(
    shard_ref, bounds, owners, x_ref, rim_ref, dt_ref, ld_ref, w_ref, bias_ref, rep_ref, rep16_ref, tri_ref,
    act_ref, cum_ref, carry_ref, sin_ref, pay_ref, fin_ref, first_ref, meta,
    state, edge, edge16, total, count,
):
    step = pl.program_id(0)
    heads = dt_ref.shape[0]
    width = rep_ref.shape[1]
    span = pl.num_programs(0) * BLOCK

    @pl.when(step == 0)
    def _():
        read_docs(bounds, owners, meta, count, shard_ref[0] * span, span)
        state[...] = jnp.zeros_like(state)
        total[...] = jnp.zeros_like(total)
        fin_ref[...] = jnp.zeros_like(fin_ref)
        first_ref[...] = jnp.zeros_like(first_ref)
        edge16[...] = rim_ref[...]
        edge[...] = rim_ref[...].astype(F32)[8:]

    for part in range(BLOCK // CHUNK):
        low = part * CHUNK
        rows = slice(low, low + CHUNK)
        begin = step * BLOCK + low
        place = iota((CHUNK, 128), 0) + begin
        back = place - starts_of(meta, place)
        keep = [(back >= lag).astype(F32) for lag in range(1, 4)]
        for tile in range(x_ref.shape[1] // 128):
            cols = slice(tile * 128, tile * 128 + 128)
            here = x_ref[rows, cols].astype(F32)
            wide = jnp.concatenate([edge[:, cols], here], axis=0)
            mixed = bias_ref[:, cols] + w_ref[0:1, cols] * here
            for lag in range(1, 4):
                moved = wide[8 - lag : 8 - lag + CHUNK]
                mixed = mixed + (w_ref[lag : lag + 1, cols] * keep[lag - 1]) * moved
            act_ref[rows, cols] = (mixed + mixed * jnp.tanh(mixed)).astype(BF16)
            edge[:, cols] = here[CHUNK - 8 :]

        summed = jnp.dot(
            thirds(ld_ref[:, rows] * LOG2E), tri_ref[...], preferred_element_type=F32
        )
        cum = summed[:heads] + summed[heads : 2 * heads] + summed[2 * heads :]
        cum_ref[:, rows] = cum
        dt = dt_ref[:, rows]
        lane = iota((heads, CHUNK), 1) + begin
        open_end = jnp.where(meta[0] < 0, meta[1], -1)
        carry_ref[:, rows] = jnp.where(lane < open_end, jnp.exp2(total[...] + cum), 0.0)
        x_act = act_ref[rows, :width]
        b_act = act_ref[rows, width : width + N]
        sin_ref[part] = state[...].astype(BF16)

        def finish(slot, _):
            end = meta[1 + slot]
            start = jnp.where(slot > 0, meta[jnp.maximum(slot, 1)], meta[0])
            at_end = jnp.sum(jnp.where(lane == end - 1, cum, 0.0), axis=1, keepdims=True)
            inside = (lane < end) & (lane >= start)
            weight = jnp.where(inside, jnp.exp2(jnp.minimum(at_end - cum, 0.0)) * dt, 0.0)
            load = (outer_dot(halves(weight), rep16_ref[...]) * x_act.astype(F32)).astype(BF16)
            local = outer_dot(b_act, load)
            through = jnp.where(start < begin, jnp.exp2(at_end), 0.0)
            final = local + spread_row(through, rep_ref[...]) * state[...]
            target = meta[5 + slot]

            @pl.when(target >= 0)
            def _():
                fin_ref[target, :width] = final.T.astype(BF16)

            opened = jnp.where(start < 0, jnp.exp2(total[:, :1] + at_end), 0.0)

            @pl.when(slot == 0)
            def _():
                first_ref[...] = jnp.broadcast_to(
                    spread_row(opened, rep_ref[...]), first_ref.shape
                )

            tail = jnp.zeros((TAIL, 128), F32)
            row = iota((TAIL, CHUNK), 0)
            col = iota((TAIL, CHUNK), 1) + begin
            row16 = iota((TAIL, 16), 0)
            col16 = iota((TAIL, 16), 1) + begin - 16
            for tile in range(x_ref.shape[1] // 128):
                cols = slice(tile * 128, tile * 128 + 128)
                want = end - 3 + row - 3 * tile
                pick = (col == want) & (col >= start) & (row >= 3 * tile) & (row < 3 * tile + 3)
                want16 = end - 3 + row16 - 3 * tile
                pick16 = (col16 == want16) & (col16 >= start) & (row16 >= 3 * tile) & (row16 < 3 * tile + 3)
                tail = tail + jnp.dot(
                    pick.astype(F32).astype(BF16), x_ref[rows, cols], preferred_element_type=F32
                ) + jnp.dot(
                    pick16.astype(F32).astype(BF16), edge16[:, cols], preferred_element_type=F32
                )

            @pl.when(target >= 0)
            def _():
                fin_ref[target, width : width + TAIL] = tail.astype(BF16)

            return 0

        done = jnp.int32(0)
        upto = jnp.int32(0)
        for slot in range(EMAX):
            done = done + (meta[1 + slot] <= begin).astype(jnp.int32)
            upto = upto + (meta[1 + slot] <= begin + CHUNK).astype(jnp.int32)
        lax.fori_loop(done, upto, finish, 0)
        edge16[...] = x_ref[low + CHUNK - 16 : low + CHUNK, :]

        start = last_start(meta, begin + CHUNK - 1)
        last = cum[:, CHUNK - 1 :]
        weight = jnp.where(lane >= start, jnp.exp2(last - cum) * dt, 0.0)
        load = (outer_dot(halves(weight), rep16_ref[...]) * x_act.astype(F32)).astype(BF16)
        through = spread_row(jnp.where(start < begin, jnp.exp2(last), 0.0), rep_ref[...])
        state[...] = through * state[...] + outer_dot(b_act, load)
        total[...] = total[...] + last

    @pl.when(step == pl.num_programs(0) - 1)
    def _():
        start = last_start(meta, span - 1)
        gate = spread_row(jnp.where(start < 0, jnp.exp2(total[:, :1]), 0.0), rep_ref[...])
        gate = jnp.broadcast_to(gate, (16, width))
        high = gate.astype(BF16).astype(F32)
        pay_ref[:N] = state[...].astype(BF16)
        pay_ref[N:] = jnp.where(iota((16, width), 0) == 0, high, gate - high).astype(BF16)


def output_kernel(meta, act_ref, dt_ref, cum_ref, sin_ref, gain_ref, rep16_ref, out_ref):
    step = pl.program_id(0)
    heads = dt_ref.shape[0]
    width = out_ref.shape[1]
    for part in range(BLOCK // CHUNK):
        low = part * CHUNK
        rows = slice(low, low + CHUNK)
        begin = step * BLOCK + low
        cum = cum_ref[:, rows]
        back = cum - jnp.log2(dt_ref[:, rows])
        ahead = cum.T
        b_act = act_ref[rows, width : width + N]
        c_act = act_ref[rows, width + N : width + 2 * N]
        place = iota((CHUNK, CHUNK), 0) + begin
        other = iota((CHUNK, CHUNK), 1) + begin
        scores = lax.dot_general(c_act, b_act, (((1,), (1,)), ((), ())), preferred_element_type=F32)
        scores = jnp.where((other <= place) & (other >= starts_of(meta, place)), scores, 0.0)
        lane = iota((heads, CHUNK), 1) + begin
        before = jnp.where(last_start(meta, begin) < begin, next_end(meta, begin), -1)
        entry = halves(jnp.where(lane < before, jnp.exp2(cum), 0.0))
        left_half = iota((CHUNK, 128), 1) < P_SIZE
        for pair in range(heads // 2):
            cols = slice(pair * 128, pair * 128 + 128)
            mixes = []
            for head in (2 * pair, 2 * pair + 1):
                spread = jnp.minimum(ahead[:, head : head + 1] - back[head : head + 1, :], 0.0)
                mixes.append((jnp.exp2(spread) * scores).astype(BF16))
            x_act = act_ref[rows, cols]
            zero = jnp.zeros_like(x_act)
            split = jnp.concatenate(
                [jnp.where(left_half, x_act, zero), jnp.where(left_half, zero, x_act)], axis=0
            )
            inner = jnp.dot(jnp.concatenate(mixes, axis=1), split, preferred_element_type=F32)
            outer = jnp.dot(c_act, sin_ref[part, :, cols], preferred_element_type=F32)
            scale = outer_dot(entry, rep16_ref[:, cols])
            value = inner + scale * outer + gain_ref[:, cols] * x_act.astype(F32)
            out_ref[rows, cols] = value.astype(BF16)


def carry_kernel(shard_ref, meta, gathered, first_ref, fin_in, carried_ref, fin_ref, held):
    del meta
    width = first_ref.shape[1]
    held[...] = jnp.zeros_like(held)

    def one(index, _):
        gates = gathered[index, N:].astype(F32)
        held[...] = (gates[0:1] + gates[1:2]) * held[...] + gathered[index, :N].astype(F32)
        return 0

    lax.fori_loop(0, shard_ref[0], one, 0)
    carried_ref[...] = held[...].astype(BF16)
    fin_ref[0, :width] = (
        fin_in[0, :width].astype(F32) + (first_ref[0:1] * held[...]).T
    ).astype(BF16)
    fin_ref[0, width:] = fin_in[0, width:]


def correct_kernel(meta, base_ref, c_ref, carry_ref, carried_ref, rep16_ref, out_ref):
    step = pl.program_id(0)
    touched = (meta[0] < 0) & (meta[1] > step * BLOCK)

    @pl.when(touched)
    def _():
        entry = halves(carry_ref[...])
        width = out_ref.shape[1]
        for tile in range(width // 256):
            cols = slice(tile * 256, tile * 256 + 256)
            outer = jnp.dot(c_ref[...], carried_ref[:, cols], preferred_element_type=F32)
            scale = outer_dot(entry, rep16_ref[:, cols])
            out_ref[:, cols] = (base_ref[:, cols].astype(F32) + scale * outer).astype(BF16)

    @pl.when(jnp.logical_not(touched))
    def _():
        out_ref[...] = base_ref[...]


def params():
    return pltpu.CompilerParams(vmem_limit_bytes=VMEM, dimension_semantics=("arbitrary",))


def whole(shape):
    return pl.BlockSpec(shape, lambda *_: (0,) * len(shape))


def on_device(
    conv_input, conv_weight, conv_bias, step_size, log_decay, skip_gain, doc_bounds, doc_owner
):
    span, channels = conv_input.shape[1:]
    heads = step_size.shape[1]
    width = heads * P_SIZE
    steps = span // BLOCK
    chunks = span // CHUNK
    owners = lax.axis_size("stream")
    slots = owners * CAP
    rows = width + TAIL
    shard = lax.axis_index("seq").astype(jnp.int32).reshape(1)
    rows_in = conv_input[0]
    rim = shifted(rows_in[span - 16 :], "seq", 1)
    rep = (jnp.arange(width)[None, :] // P_SIZE == jnp.arange(heads)[:, None]).astype(F32)
    rep16 = jnp.concatenate([rep, rep], 0).astype(BF16)
    ticks = jnp.arange(CHUNK)
    tri = (ticks[:, None] <= ticks[None, :]).astype(BF16)
    smem = pl.BlockSpec(memory_space=pltpu.SMEM)
    per_head = pl.BlockSpec((heads, BLOCK), lambda i, *_: (0, i))
    act, cum, carry, sin, pay, fin, first, meta = pl.pallas_call(
        states_kernel,
        grid=(steps,),
        in_specs=[
            smem, smem, smem,
            pl.BlockSpec((BLOCK, channels), lambda i: (i, 0)),
            whole((16, channels)),
            per_head, per_head,
            whole((4, channels)), whole((1, channels)),
            whole((heads, width)), whole((2 * heads, width)), whole((CHUNK, CHUNK)),
        ],
        out_specs=[
            pl.BlockSpec((BLOCK, channels), lambda i: (i, 0)),
            per_head, per_head,
            pl.BlockSpec((BLOCK // CHUNK, N, width), lambda i: (i, 0, 0)),
            whole((PAY, width)), whole((slots, rows, N)), whole((8, width)),
            smem,
        ],
        out_shape=[
            jax.ShapeDtypeStruct((span, channels), BF16),
            jax.ShapeDtypeStruct((heads, span), F32),
            jax.ShapeDtypeStruct((heads, span), F32),
            jax.ShapeDtypeStruct((chunks, N, width), BF16),
            jax.ShapeDtypeStruct((PAY, width), BF16),
            jax.ShapeDtypeStruct((slots, rows, N), BF16),
            jax.ShapeDtypeStruct((8, width), F32),
            jax.ShapeDtypeStruct((16,), jnp.int32),
        ],
        scratch_shapes=[
            pltpu.VMEM((N, width), F32),
            pltpu.VMEM((8, channels), F32),
            pltpu.VMEM((16, channels), BF16),
            pltpu.VMEM((heads, CHUNK), F32),
            pltpu.SMEM((owners,), jnp.int32),
        ],
        compiler_params=params(),
        cost_estimate=pl.CostEstimate(
            flops=2 * span * width * N * 2, bytes_accessed=40 << 20, transcendentals=span * channels
        ),
        name="states",
    )(
        shard, doc_bounds, doc_owner, rows_in, rim, step_size[0], log_decay[0],
        conv_weight * 0.5, conv_bias[None] * 0.5, rep, rep16, tri,
    )

    gathered = lax.all_gather(pay[None], "seq", axis=0, tiled=True)

    gain = jnp.repeat(skip_gain, P_SIZE)[None]
    prefetch = functools.partial(pltpu.PrefetchScalarGridSpec, num_scalar_prefetch=1)
    base = pl.pallas_call(
        output_kernel,
        grid_spec=prefetch(
            grid=(steps,),
            in_specs=[
                pl.BlockSpec((BLOCK, channels), lambda i, *_: (i, 0)),
                per_head, per_head,
                pl.BlockSpec((BLOCK // CHUNK, N, width), lambda i, *_: (i, 0, 0)),
                whole((1, width)), whole((2 * heads, width)),
            ],
            out_specs=pl.BlockSpec((BLOCK, width), lambda i, *_: (i, 0)),
        ),
        out_shape=jax.ShapeDtypeStruct((span, width), BF16),
        compiler_params=params(),
        cost_estimate=pl.CostEstimate(
            flops=2 * span * width * N * 4, bytes_accessed=30 << 20, transcendentals=span * CHUNK * heads
        ),
        name="outputs",
    )(meta, act, step_size[0], cum, sin, gain, rep16)

    carried, fin = pl.pallas_call(
        carry_kernel,
        grid_spec=pltpu.PrefetchScalarGridSpec(
            num_scalar_prefetch=2,
            grid=(1,),
            in_specs=[
                whole(gathered.shape), whole((8, width)),
                pl.BlockSpec((1, rows, N), lambda i, shard_ref, meta: (meta[5], 0, 0)),
            ],
            out_specs=[
                whole((N, width)),
                pl.BlockSpec((1, rows, N), lambda i, shard_ref, meta: (meta[5], 0, 0)),
            ],
            scratch_shapes=[pltpu.VMEM((N, width), F32)],
        ),
        out_shape=[
            jax.ShapeDtypeStruct((N, width), BF16),
            jax.ShapeDtypeStruct((slots, rows, N), BF16),
        ],
        input_output_aliases={4: 1},
        compiler_params=params(),
        name="carry",
    )(shard, meta, gathered, first, fin)

    got = lax.all_to_all(
        fin.reshape(owners, CAP, rows, N), "stream", split_axis=0, concat_axis=0, tiled=True
    )

    out = pl.pallas_call(
        correct_kernel,
        grid_spec=prefetch(
            grid=(steps,),
            in_specs=[
                pl.BlockSpec((BLOCK, width), lambda i, *_: (i, 0)),
                pl.BlockSpec((BLOCK, N), lambda i, *_: (i, width // N + 1)),
                per_head,
                whole((N, width)), whole((2 * heads, width)),
            ],
            out_specs=pl.BlockSpec((BLOCK, width), lambda i, *_: (i, 0)),
        ),
        out_shape=jax.ShapeDtypeStruct((span, width), BF16),
        input_output_aliases={1: 0},
        compiler_params=params(),
        cost_estimate=pl.CostEstimate(
            flops=2 * span * width * N, bytes_accessed=18 << 20, transcendentals=0
        ),
        name="correct",
    )(meta, base, act, carry, carried, rep16)

    ssm = got[:, :, :width].astype(F32).reshape(1, 1, owners, CAP, heads, P_SIZE, N)
    tiles = channels // N
    conv = got[:, :, width : width + 3 * tiles].reshape(owners, CAP, tiles, 3, N)
    conv = conv.transpose(0, 1, 3, 2, 4).reshape(1, 1, owners, CAP, 3, channels)
    return out[None], ssm, conv


def solution(mesh):
    in_specs = (
        P("stream", "seq", None),
        P(),
        P(),
        P("stream", None, "seq"),
        P("stream", None, "seq"),
        P(),
        P("stream", None),
        P("stream", None),
    )
    out_specs = (
        P("stream", "seq", None),
        P("stream", "seq", None, None, None, None, None),
        P("stream", "seq", None, None, None, None),
    )
    return jax.shard_map(
        on_device, mesh=mesh, in_specs=in_specs, out_specs=out_specs, check_vma=False
    )
```

```python
import functools

import jax
import jax.numpy as jnp
import numpy as np
from jax import lax
from jax.experimental import pallas as pl
from jax.experimental.pallas import tpu as pltpu
from jax.sharding import PartitionSpec as P

P_SIZE = 64
N = 128
EMAX = 4
CAP = 2
CHUNK = 128
BLOCK = 512
FAR = 1 << 30
LOG2E = 1.4426950408889634
PAY = 144
TAIL = 32
VMEM = 56 * 1024 * 1024

F32 = jnp.float32
BF16 = jnp.bfloat16


def shifted(value, axis, steps):
    count = lax.axis_size(axis)
    leading, last = (max(0, -steps), min(count, count - steps))
    return lax.ppermute(value, axis, [(source, source + steps) for source in range(leading, last)])


def iota(shape, axis):
    return lax.broadcasted_iota(jnp.int32, shape, axis)


def outer_dot(left, right):
    return lax.dot_general(left, right, (((0,), (0,)), ((), ())), preferred_element_type=F32)


def halves(value):
    high = value.astype(BF16)
    low = (value - high.astype(F32)).astype(BF16)
    return jnp.concatenate([high, low], axis=0)


def thirds(value):
    high = value.astype(BF16)
    rest = value - high.astype(F32)
    mid = rest.astype(BF16)
    low = (rest - mid.astype(F32)).astype(BF16)
    return jnp.concatenate([high, mid, low], axis=0)


def spread_row(column, rep):
    return jnp.sum(rep * column, axis=0, keepdims=True)


def last_start(meta, place):
    start = meta[0]
    for slot in range(EMAX):
        end = meta[1 + slot]
        start = jnp.where(end <= place, end, start)
    return start


def next_end(meta, place):
    end = FAR
    for slot in reversed(range(EMAX)):
        end = jnp.where(meta[1 + slot] > place, meta[1 + slot], end)
    return end


def starts_of(meta, rows):
    start = jnp.full(rows.shape, meta[0], jnp.int32)
    for slot in range(EMAX):
        end = meta[1 + slot]
        start = jnp.where(rows >= end, end, start)
    return start


def read_docs(bounds, owners, meta, count, anchor, span):
    for slot in range(EMAX):
        meta[1 + slot] = FAR
        meta[5 + slot] = 0
    for owner in range(count.shape[0]):
        count[owner] = 0

    def one(index, carry):
        found, prior, start = carry
        end = bounds[0, index]
        owner = owners[0, index]
        mine = (end > prior) & (end > anchor) & (end <= anchor + span) & (found < EMAX)

        @pl.when(mine)
        def _():
            meta[1 + found] = end - anchor
            rank = count[owner]
            meta[5 + found] = jnp.where(rank < CAP, owner * CAP + rank, -1)
            count[owner] = rank + 1

        return found + mine.astype(jnp.int32), end, jnp.where(end <= anchor, end, start)

    zero = jnp.int32(0)
    _, _, start = lax.fori_loop(0, bounds.shape[1], one, (zero, zero, zero))
    meta[0] = start - anchor


def conv_rows(x_ref, edge16, moves, weights, act_ref, part, choice):
    low = part * CHUNK
    rows = slice(low, low + CHUNK)
    pick = moves[choice]
    for tile in range(x_ref.shape[1] // 256):
        cols = slice(tile * 256, tile * 256 + 256)
        if part:
            wide = x_ref[low - 16 : low + CHUNK, cols]
        else:
            wide = jnp.concatenate([edge16[:, cols], x_ref[rows, cols]], axis=0)
        moved = jnp.dot(pick, wide, preferred_element_type=F32)
        moved = moved.reshape(CHUNK // 8, 3, 8, 256)
        mixed = weights[4:5, cols] + weights[0:1, cols] * x_ref[rows, cols].astype(F32)
        for lag in range(1, 4):
            mixed = mixed + weights[lag : lag + 1, cols] * moved[:, lag - 1].reshape(CHUNK, 256)
        act_ref[rows, cols] = (mixed + mixed * jnp.tanh(mixed)).astype(BF16)


def states_kernel(
    shard_ref, bounds, owners, x_ref, rim_ref, dt_ref, ld_ref, w_ref, bias_ref,
    rep_ref, rep16_ref, tri_ref, move_ref, slot_ref,
    act_ref, cum_ref, carry_ref, sin_ref, pay_ref, fin_ref, first_ref, meta,
    state, edge16, total, totals, weights, moves, count,
):
    step = pl.program_id(0)
    heads = dt_ref.shape[0]
    width = rep_ref.shape[1]
    span = pl.num_programs(0) * BLOCK
    parts = BLOCK // CHUNK
    first = step * BLOCK

    @pl.when(step == 0)
    def _():
        read_docs(bounds, owners, meta, count, shard_ref[0] * span, span)
        state[...] = jnp.zeros_like(state)
        total[...] = jnp.zeros_like(total)
        fin_ref[...] = jnp.zeros_like(fin_ref)
        first_ref[...] = jnp.zeros_like(first_ref)
        edge16[...] = rim_ref[...]
        weights[0:4] = 0.5 * w_ref[...]
        weights[4:5] = 0.5 * bias_ref[...]
        moves[0] = move_ref[...]

    choices = []
    for part in range(parts):
        begin = first + part * CHUNK
        near = (meta[0] > begin - 3) & (meta[0] < begin + CHUNK)
        for slot in range(EMAX):
            near = near | ((meta[1 + slot] > begin - 3) & (meta[1 + slot] < begin + CHUNK))

        @pl.when(near)
        def _():
            tick = slot_ref[...] // 4 + begin
            kept = (tick - starts_of(meta, tick) >= slot_ref[...] % 4).astype(F32)
            moves[1 + part, :, :128] = (kept * move_ref[:, :128].astype(F32)).astype(BF16)
            moves[1 + part, :, 128:] = (kept[:, :16] * move_ref[:, 128:].astype(F32)).astype(BF16)

        choices.append(jnp.where(near, 1 + part, 0))

    conv_rows(x_ref, edge16, moves, weights, act_ref, 0, choices[0])
    running = total[...]
    for part in range(parts):
        low = part * CHUNK
        rows = slice(low, low + CHUNK)
        begin = first + low
        if part + 1 < parts:
            conv_rows(x_ref, edge16, moves, weights, act_ref, part + 1, choices[part + 1])
        summed = jnp.dot(
            thirds(ld_ref[:, rows] * LOG2E), tri_ref[...], preferred_element_type=F32
        )
        cum = summed[:heads] + summed[heads : 2 * heads] + summed[2 * heads :]
        cum_ref[:, rows] = cum
        lane = iota((heads, CHUNK), 1) + begin
        open_end = jnp.where(meta[0] < 0, meta[1], -1)
        carry_ref[:, rows] = jnp.where(lane < open_end, jnp.exp2(running + cum), 0.0)
        totals[part] = running
        start = last_start(meta, begin + CHUNK - 1)
        last = cum[:, CHUNK - 1 :]
        weight = jnp.where(lane >= start, jnp.exp2(last - cum) * dt_ref[:, rows], 0.0)
        weight = weight.T.astype(BF16)
        through = spread_row(jnp.where(start < begin, jnp.exp2(last), 0.0), rep_ref[...])
        b_turned = act_ref[rows, width : width + N].T
        for tile in range(width // 256):
            cols = slice(tile * 256, tile * 256 + 256)
            held = state[:, cols]
            sin_ref[part, :, cols] = held.astype(BF16)
            scale = jnp.dot(weight, rep16_ref[:heads, cols], preferred_element_type=F32)
            load = scale.astype(BF16) * act_ref[rows, cols]
            grown = jnp.dot(b_turned, load, preferred_element_type=F32)
            state[:, cols] = through[:, cols] * held + grown
        running = running + last
    total[...] = running

    def finish(slot, _):
        end = meta[1 + slot]
        start = jnp.where(slot > 0, meta[jnp.maximum(slot, 1)], meta[0])
        part = (end - 1 - first) // CHUNK
        low = pl.multiple_of(part * CHUNK, CHUNK)
        begin = first + low
        lane = iota((heads, CHUNK), 1) + begin
        cum = cum_ref[:, pl.ds(low, CHUNK)]
        at_end = jnp.sum(jnp.where(lane == end - 1, cum, 0.0), axis=1, keepdims=True)
        inside = (lane < end) & (lane >= start)
        weight = jnp.exp2(jnp.minimum(at_end - cum, 0.0)) * dt_ref[:, pl.ds(low, CHUNK)]
        weight = jnp.where(inside, weight, 0.0).T.astype(BF16)
        scale = jnp.dot(weight, rep16_ref[:heads], preferred_element_type=F32)
        load = scale.astype(BF16) * act_ref[pl.ds(low, CHUNK), :width]
        local = outer_dot(act_ref[pl.ds(low, CHUNK), width : width + N], load)
        through = spread_row(jnp.where(start < begin, jnp.exp2(at_end), 0.0), rep_ref[...])
        final = local + through * sin_ref[part].astype(F32)
        target = meta[5 + slot]
        opened = jnp.where(start < 0, jnp.exp2(totals[part][:, :1] + at_end), 0.0)

        @pl.when(slot == 0)
        def _():
            first_ref[...] = jnp.broadcast_to(spread_row(opened, rep_ref[...]), first_ref.shape)

        tail = jnp.zeros((TAIL, 128), F32)
        row = iota((TAIL, CHUNK), 0)
        col = iota((TAIL, CHUNK), 1) + begin
        row16 = iota((TAIL, 16), 0)
        col16 = iota((TAIL, 16), 1) + begin - 16
        before = pl.multiple_of(jnp.maximum(low - 16, 0), 16)
        for tile in range(x_ref.shape[1] // 128):
            cols = slice(tile * 128, tile * 128 + 128)
            mine = (row >= 3 * tile) & (row < 3 * tile + 3)
            pick = (col == end - 3 + row - 3 * tile) & (col >= start) & mine
            mine16 = (row16 >= 3 * tile) & (row16 < 3 * tile + 3)
            pick16 = (col16 == end - 3 + row16 - 3 * tile) & (col16 >= start) & mine16
            rim = jnp.where(low > 0, x_ref[pl.ds(before, 16), cols].astype(F32), edge16[:, cols].astype(F32))
            tail = tail + jnp.dot(
                pick.astype(F32).astype(BF16), x_ref[pl.ds(low, CHUNK), cols], preferred_element_type=F32
            ) + jnp.dot(
                pick16.astype(F32).astype(BF16), rim.astype(BF16), preferred_element_type=F32
            )

        @pl.when(target >= 0)
        def _():
            fin_ref[target, :width] = final.T.astype(BF16)
            fin_ref[target, width : width + TAIL] = tail.astype(BF16)

        return 0

    done = jnp.int32(0)
    upto = jnp.int32(0)
    for slot in range(EMAX):
        done = done + (meta[1 + slot] <= first).astype(jnp.int32)
        upto = upto + (meta[1 + slot] <= first + BLOCK).astype(jnp.int32)
    lax.fori_loop(done, upto, finish, 0)
    edge16[...] = x_ref[BLOCK - 16 :, :]

    @pl.when(step == pl.num_programs(0) - 1)
    def _():
        start = last_start(meta, span - 1)
        gate = spread_row(jnp.where(start < 0, jnp.exp2(total[:, :1]), 0.0), rep_ref[...])
        gate = jnp.broadcast_to(gate, (16, width))
        high = gate.astype(BF16).astype(F32)
        pay_ref[:N] = state[...].astype(BF16)
        pay_ref[N:] = jnp.where(iota((16, width), 0) == 0, high, gate - high).astype(BF16)


def output_kernel(meta, act_ref, dt_ref, cum_ref, sin_ref, gain_ref, rep16_ref, out_ref):
    step = pl.program_id(0)
    heads = dt_ref.shape[0]
    width = out_ref.shape[1]
    for part in range(BLOCK // CHUNK):
        low = part * CHUNK
        rows = slice(low, low + CHUNK)
        begin = step * BLOCK + low
        cum = cum_ref[:, rows]
        back = cum - jnp.log2(dt_ref[:, rows])
        ahead = cum.T
        b_act = act_ref[rows, width : width + N]
        c_act = act_ref[rows, width + N : width + 2 * N]
        place = iota((CHUNK, CHUNK), 0) + begin
        other = iota((CHUNK, CHUNK), 1) + begin
        scores = lax.dot_general(c_act, b_act, (((1,), (1,)), ((), ())), preferred_element_type=F32)
        scores = jnp.where((other <= place) & (other >= starts_of(meta, place)), scores, 0.0)
        lane = iota((heads, CHUNK), 1) + begin
        before = jnp.where(last_start(meta, begin) < begin, next_end(meta, begin), -1)
        entry = jnp.where(lane < before, jnp.exp2(cum), 0.0)
        entry = jnp.concatenate([entry, entry - entry.astype(BF16).astype(F32)], axis=0).T.astype(BF16)
        left_half = iota((CHUNK, 128), 1) < P_SIZE
        for quad in range(heads // 4):
            cols = slice(quad * 256, quad * 256 + 256)
            outer = jnp.dot(c_act, sin_ref[part, :, cols], preferred_element_type=F32)
            scale = jnp.dot(entry, rep16_ref[:, cols], preferred_element_type=F32)
            sums = []
            for pair in (2 * quad, 2 * quad + 1):
                mixes = []
                for head in (2 * pair, 2 * pair + 1):
                    spread = jnp.minimum(ahead[:, head : head + 1] - back[head : head + 1, :], 0.0)
                    mixes.append((jnp.exp2(spread) * scores).astype(BF16))
                x_pair = act_ref[rows, pair * 128 : pair * 128 + 128]
                zero = jnp.zeros_like(x_pair)
                split = jnp.concatenate(
                    [jnp.where(left_half, x_pair, zero), jnp.where(left_half, zero, x_pair)], axis=0
                )
                sums.append(
                    jnp.dot(jnp.concatenate(mixes, axis=1), split, preferred_element_type=F32)
                )
            inner = jnp.concatenate(sums, axis=1)
            value = inner + scale * outer + gain_ref[:, cols] * act_ref[rows, cols].astype(F32)
            out_ref[rows, cols] = value.astype(BF16)


def carry_kernel(shard_ref, meta, gathered, first_ref, fin_in, carried_ref, fin_ref, held):
    del meta
    width = first_ref.shape[1]
    held[...] = jnp.zeros_like(held)

    def one(index, _):
        gates = gathered[index, N:].astype(F32)
        held[...] = (gates[0:1] + gates[1:2]) * held[...] + gathered[index, :N].astype(F32)
        return 0

    lax.fori_loop(0, shard_ref[0], one, 0)
    carried_ref[...] = held[...].astype(BF16)
    fin_ref[0, :width] = (
        fin_in[0, :width].astype(F32) + (first_ref[0:1] * held[...]).T
    ).astype(BF16)
    fin_ref[0, width:] = fin_in[0, width:]


def correct_kernel(meta, base_ref, c_ref, carry_ref, carried_ref, rep16_ref, out_ref):
    step = pl.program_id(0)
    touched = (meta[0] < 0) & (meta[1] > step * BLOCK)

    @pl.when(touched)
    def _():
        entry = carry_ref[...]
        entry = jnp.concatenate([entry, entry - entry.astype(BF16).astype(F32)], axis=0).T.astype(BF16)
        width = out_ref.shape[1]
        for tile in range(width // 256):
            cols = slice(tile * 256, tile * 256 + 256)
            for part in range(BLOCK // CHUNK):
                rows = slice(part * CHUNK, part * CHUNK + CHUNK)
                outer = jnp.dot(c_ref[rows, :], carried_ref[:, cols], preferred_element_type=F32)
                scale = jnp.dot(entry[rows], rep16_ref[:, cols], preferred_element_type=F32)
                out_ref[rows, cols] = (base_ref[rows, cols].astype(F32) + scale * outer).astype(BF16)

    @pl.when(jnp.logical_not(touched))
    def _():
        out_ref[...] = base_ref[...]


def params():
    return pltpu.CompilerParams(vmem_limit_bytes=VMEM, dimension_semantics=("arbitrary",))


def whole(shape):
    return pl.BlockSpec(shape, lambda *_: (0,) * len(shape))


def on_device(
    conv_input, conv_weight, conv_bias, step_size, log_decay, skip_gain, doc_bounds, doc_owner
):
    span, channels = conv_input.shape[1:]
    heads = step_size.shape[1]
    width = heads * P_SIZE
    steps = span // BLOCK
    chunks = span // CHUNK
    owners = lax.axis_size("stream")
    slots = owners * CAP
    rows = width + TAIL
    shard = lax.axis_index("seq").astype(jnp.int32).reshape(1)
    rows_in = conv_input[0]
    rim = shifted(rows_in[span - 16 :], "seq", 1)
    rep = (np.arange(width)[None, :] // P_SIZE == np.arange(heads)[:, None]).astype(np.float32)
    rep16 = np.concatenate([rep, rep], 0).astype(BF16)
    ticks = np.arange(CHUNK)
    tri = (ticks[:, None] <= ticks[None, :]).astype(BF16)
    order = np.arange(3 * CHUNK)
    tick, lag = 8 * (order // 24) + order % 8, order % 24 // 8 + 1
    source = np.arange(CHUNK + 16)
    move = (source[None, :] - 16 == (tick - lag)[:, None]).astype(BF16)
    slot = np.broadcast_to((4 * tick + lag)[:, None], (3 * CHUNK, 128)).astype(np.int32)
    smem = pl.BlockSpec(memory_space=pltpu.SMEM)
    per_head = pl.BlockSpec((heads, BLOCK), lambda i, *_: (0, i))
    act, cum, carry, sin, pay, fin, first, meta = pl.pallas_call(
        states_kernel,
        grid=(steps,),
        in_specs=[
            smem, smem, smem,
            pl.BlockSpec((BLOCK, channels), lambda i: (i, 0)),
            whole((16, channels)),
            per_head, per_head,
            whole((4, channels)), whole((1, channels)),
            whole((heads, width)), whole((2 * heads, width)), whole((CHUNK, CHUNK)),
            whole(move.shape), whole(slot.shape),
        ],
        out_specs=[
            pl.BlockSpec((BLOCK, channels), lambda i: (i, 0)),
            per_head, per_head,
            pl.BlockSpec((BLOCK // CHUNK, N, width), lambda i: (i, 0, 0)),
            whole((PAY, width)), whole((slots, rows, N)), whole((8, width)),
            smem,
        ],
        out_shape=[
            jax.ShapeDtypeStruct((span, channels), BF16),
            jax.ShapeDtypeStruct((heads, span), F32),
            jax.ShapeDtypeStruct((heads, span), F32),
            jax.ShapeDtypeStruct((chunks, N, width), BF16),
            jax.ShapeDtypeStruct((PAY, width), BF16),
            jax.ShapeDtypeStruct((slots, rows, N), BF16),
            jax.ShapeDtypeStruct((8, width), F32),
            jax.ShapeDtypeStruct((16,), jnp.int32),
        ],
        scratch_shapes=[
            pltpu.VMEM((N, width), F32),
            pltpu.VMEM((16, channels), BF16),
            pltpu.VMEM((heads, CHUNK), F32),
            pltpu.VMEM((BLOCK // CHUNK, heads, CHUNK), F32),
            pltpu.VMEM((8, channels), F32),
            pltpu.VMEM((1 + BLOCK // CHUNK,) + move.shape, BF16),
            pltpu.SMEM((owners,), jnp.int32),
        ],
        compiler_params=params(),
        cost_estimate=pl.CostEstimate(
            flops=2 * span * width * N * 2, bytes_accessed=40 << 20, transcendentals=span * channels
        ),
        name="states",
    )(
        shard, doc_bounds, doc_owner, rows_in, rim, step_size[0], log_decay[0],
        conv_weight, conv_bias[None], rep, rep16, tri, move, slot,
    )

    gathered = lax.all_gather(pay[None], "seq", axis=0, tiled=True)

    gain = jnp.repeat(skip_gain, P_SIZE)[None]
    prefetch = functools.partial(pltpu.PrefetchScalarGridSpec, num_scalar_prefetch=1)
    base = pl.pallas_call(
        output_kernel,
        grid_spec=prefetch(
            grid=(steps,),
            in_specs=[
                pl.BlockSpec((BLOCK, channels), lambda i, *_: (i, 0)),
                per_head, per_head,
                pl.BlockSpec((BLOCK // CHUNK, N, width), lambda i, *_: (i, 0, 0)),
                whole((1, width)), whole((2 * heads, width)),
            ],
            out_specs=pl.BlockSpec((BLOCK, width), lambda i, *_: (i, 0)),
        ),
        out_shape=jax.ShapeDtypeStruct((span, width), BF16),
        compiler_params=params(),
        cost_estimate=pl.CostEstimate(
            flops=2 * span * width * N * 4, bytes_accessed=30 << 20, transcendentals=span * CHUNK * heads
        ),
        name="outputs",
    )(meta, act, step_size[0], cum, sin, gain, rep16)

    gathered, base = lax.optimization_barrier((gathered, base))
    carried, fin = pl.pallas_call(
        carry_kernel,
        grid_spec=pltpu.PrefetchScalarGridSpec(
            num_scalar_prefetch=2,
            grid=(1,),
            in_specs=[
                whole(gathered.shape), whole((8, width)),
                pl.BlockSpec((1, rows, N), lambda i, shard_ref, meta: (meta[5], 0, 0)),
            ],
            out_specs=[
                whole((N, width)),
                pl.BlockSpec((1, rows, N), lambda i, shard_ref, meta: (meta[5], 0, 0)),
            ],
            scratch_shapes=[pltpu.VMEM((N, width), F32)],
        ),
        out_shape=[
            jax.ShapeDtypeStruct((N, width), BF16),
            jax.ShapeDtypeStruct((slots, rows, N), BF16),
        ],
        input_output_aliases={4: 1},
        compiler_params=params(),
        name="carry",
    )(shard, meta, gathered, first, fin)

    got = lax.all_to_all(
        fin.reshape(owners, CAP, rows, N), "stream", split_axis=0, concat_axis=0, tiled=True
    )

    out = pl.pallas_call(
        correct_kernel,
        grid_spec=prefetch(
            grid=(steps,),
            in_specs=[
                pl.BlockSpec((BLOCK, width), lambda i, *_: (i, 0)),
                pl.BlockSpec((BLOCK, N), lambda i, *_: (i, width // N + 1)),
                per_head,
                whole((N, width)), whole((2 * heads, width)),
            ],
            out_specs=pl.BlockSpec((BLOCK, width), lambda i, *_: (i, 0)),
        ),
        out_shape=jax.ShapeDtypeStruct((span, width), BF16),
        input_output_aliases={1: 0},
        compiler_params=params(),
        cost_estimate=pl.CostEstimate(
            flops=2 * span * width * N, bytes_accessed=18 << 20, transcendentals=0
        ),
        name="correct",
    )(meta, base, act, carry, carried, rep16)

    ssm = got[:, :, :width].astype(F32).reshape(1, 1, owners, CAP, heads, P_SIZE, N)
    tiles = channels // N
    conv = got[:, :, width : width + 3 * tiles].reshape(owners, CAP, tiles, 3, N)
    conv = conv.transpose(0, 1, 3, 2, 4).reshape(1, 1, owners, CAP, 3, channels)
    return out[None], ssm, conv


def solution(mesh):
    in_specs = (
        P("stream", "seq", None),
        P(),
        P(),
        P("stream", None, "seq"),
        P("stream", None, "seq"),
        P(),
        P("stream", None),
        P("stream", None),
    )
    out_specs = (
        P("stream", "seq", None),
        P("stream", "seq", None, None, None, None, None),
        P("stream", "seq", None, None, None, None),
    )
    return jax.shard_map(
        on_device, mesh=mesh, in_specs=in_specs, out_specs=out_specs, check_vma=False
    )
```

```python
import functools

import jax
import jax.numpy as jnp
import numpy as np
from jax import lax
from jax.experimental import pallas as pl
from jax.experimental.pallas import tpu as pltpu
from jax.sharding import PartitionSpec as P

P_SIZE = 64
N = 128
EMAX = 4
CAP = 2
CHUNK = 128
BLOCK = 512
FAR = 1 << 30
LOG2E = 1.4426950408889634
PAY = 144
TAIL = 32
VMEM = 56 * 1024 * 1024

F32 = jnp.float32
BF16 = jnp.bfloat16


def shifted(value, axis, steps):
    count = lax.axis_size(axis)
    leading, last = (max(0, -steps), min(count, count - steps))
    return lax.ppermute(value, axis, [(source, source + steps) for source in range(leading, last)])


def iota(shape, axis):
    return lax.broadcasted_iota(jnp.int32, shape, axis)


def outer_dot(left, right):
    return lax.dot_general(left, right, (((0,), (0,)), ((), ())), preferred_element_type=F32)


def halves(value):
    high = value.astype(BF16)
    low = (value - high.astype(F32)).astype(BF16)
    return jnp.concatenate([high, low], axis=0)


def thirds(value):
    high = value.astype(BF16)
    rest = value - high.astype(F32)
    mid = rest.astype(BF16)
    low = (rest - mid.astype(F32)).astype(BF16)
    return jnp.concatenate([high, mid, low], axis=0)


def spread_row(column, rep):
    return jnp.sum(rep * column, axis=0, keepdims=True)


def last_start(meta, place):
    start = meta[0]
    for slot in range(EMAX):
        end = meta[1 + slot]
        start = jnp.where(end <= place, end, start)
    return start


def next_end(meta, place):
    end = FAR
    for slot in reversed(range(EMAX)):
        end = jnp.where(meta[1 + slot] > place, meta[1 + slot], end)
    return end


def starts_of(meta, rows):
    start = jnp.full(rows.shape, meta[0], jnp.int32)
    for slot in range(EMAX):
        end = meta[1 + slot]
        start = jnp.where(rows >= end, end, start)
    return start


def read_docs(bounds, owners, meta, count, anchor, span):
    for slot in range(EMAX):
        meta[1 + slot] = FAR
        meta[5 + slot] = 0
    for owner in range(count.shape[0]):
        count[owner] = 0

    def one(index, carry):
        found, prior, start = carry
        end = bounds[0, index]
        owner = owners[0, index]
        mine = (end > prior) & (end > anchor) & (end <= anchor + span) & (found < EMAX)

        @pl.when(mine)
        def _():
            meta[1 + found] = end - anchor
            rank = count[owner]
            meta[5 + found] = jnp.where(rank < CAP, owner * CAP + rank, -1)
            count[owner] = rank + 1

        return found + mine.astype(jnp.int32), end, jnp.where(end <= anchor, end, start)

    zero = jnp.int32(0)
    _, _, start = lax.fori_loop(0, bounds.shape[1], one, (zero, zero, zero))
    meta[0] = start - anchor


def conv_rows(x_ref, edge16, moves, weights, act_ref, part, choice):
    low = part * CHUNK
    rows = slice(low, low + CHUNK)
    pick = moves[choice]
    for tile in range(x_ref.shape[1] // 256):
        cols = slice(tile * 256, tile * 256 + 256)
        if part:
            wide = x_ref[low - 16 : low + CHUNK, cols]
        else:
            wide = jnp.concatenate([edge16[:, cols], x_ref[rows, cols]], axis=0)
        moved = jnp.dot(pick, wide, preferred_element_type=F32)
        moved = moved.reshape(CHUNK // 8, 3, 8, 256)
        mixed = weights[4:5, cols] + weights[0:1, cols] * x_ref[rows, cols].astype(F32)
        for lag in range(1, 4):
            mixed = mixed + weights[lag : lag + 1, cols] * moved[:, lag - 1].reshape(CHUNK, 256)
        act_ref[rows, cols] = (mixed + mixed * jnp.tanh(mixed)).astype(BF16)


def states_kernel(
    shard_ref, bounds, owners, x_ref, rim_ref, dt_ref, ld_ref, w_ref, bias_ref,
    rep_ref, rep16_ref, tri_ref, move_ref, slot_ref,
    act_ref, cum_ref, carry_ref, sin_ref, pay_ref, fin_ref, first_ref, meta,
    state, edge16, total, totals, weights, moves, count,
):
    step = pl.program_id(0)
    heads = dt_ref.shape[0]
    width = rep_ref.shape[1]
    span = pl.num_programs(0) * BLOCK
    parts = BLOCK // CHUNK
    first = step * BLOCK

    @pl.when(step == 0)
    def _():
        read_docs(bounds, owners, meta, count, shard_ref[0] * span, span)
        state[...] = jnp.zeros_like(state)
        total[...] = jnp.zeros_like(total)
        fin_ref[...] = jnp.zeros_like(fin_ref)
        first_ref[...] = jnp.zeros_like(first_ref)
        edge16[...] = rim_ref[...]
        weights[0:4] = 0.5 * w_ref[...]
        weights[4:5] = 0.5 * bias_ref[...]
        moves[0] = move_ref[...]

    choices = []
    for part in range(parts):
        begin = first + part * CHUNK
        near = (meta[0] > begin - 3) & (meta[0] < begin + CHUNK)
        for slot in range(EMAX):
            near = near | ((meta[1 + slot] > begin - 3) & (meta[1 + slot] < begin + CHUNK))

        @pl.when(near)
        def _():
            tick = slot_ref[...] // 4 + begin
            kept = (tick - starts_of(meta, tick) >= slot_ref[...] % 4).astype(F32)
            moves[1 + part, :, :128] = (kept * move_ref[:, :128].astype(F32)).astype(BF16)
            moves[1 + part, :, 128:] = (kept[:, :16] * move_ref[:, 128:].astype(F32)).astype(BF16)

        choices.append(jnp.where(near, 1 + part, 0))

    conv_rows(x_ref, edge16, moves, weights, act_ref, 0, choices[0])
    running = total[...]
    for part in range(parts):
        low = part * CHUNK
        rows = slice(low, low + CHUNK)
        begin = first + low
        if part + 1 < parts:
            conv_rows(x_ref, edge16, moves, weights, act_ref, part + 1, choices[part + 1])
        summed = jnp.dot(
            thirds(ld_ref[:, rows] * LOG2E), tri_ref[...], preferred_element_type=F32
        )
        cum = summed[:heads] + summed[heads : 2 * heads] + summed[2 * heads :]
        cum_ref[:, rows] = cum
        lane = iota((heads, CHUNK), 1) + begin
        open_end = jnp.where(meta[0] < 0, meta[1], -1)
        carry_ref[:, rows] = jnp.where(lane < open_end, jnp.exp2(running + cum), 0.0)
        totals[part] = running
        start = last_start(meta, begin + CHUNK - 1)
        last = cum[:, CHUNK - 1 :]
        weight = jnp.where(lane >= start, jnp.exp2(last - cum) * dt_ref[:, rows], 0.0)
        weight = weight.T.astype(BF16)
        through = spread_row(jnp.where(start < begin, jnp.exp2(last), 0.0), rep_ref[...])
        b_turned = act_ref[rows, width : width + N].T
        for tile in range(width // 256):
            cols = slice(tile * 256, tile * 256 + 256)
            held = state[:, cols]
            sin_ref[part, :, cols] = held.astype(BF16)
            scale = jnp.dot(weight, rep16_ref[:heads, cols], preferred_element_type=F32)
            load = scale.astype(BF16) * act_ref[rows, cols]
            grown = jnp.dot(b_turned, load, preferred_element_type=F32)
            state[:, cols] = through[:, cols] * held + grown
        running = running + last
    total[...] = running

    def finish(slot, _):
        end = meta[1 + slot]
        start = jnp.where(slot > 0, meta[jnp.maximum(slot, 1)], meta[0])
        part = (end - 1 - first) // CHUNK
        low = pl.multiple_of(part * CHUNK, CHUNK)
        begin = first + low
        lane = iota((heads, CHUNK), 1) + begin
        cum = cum_ref[:, pl.ds(low, CHUNK)]
        at_end = jnp.sum(jnp.where(lane == end - 1, cum, 0.0), axis=1, keepdims=True)
        inside = (lane < end) & (lane >= start)
        weight = jnp.exp2(jnp.minimum(at_end - cum, 0.0)) * dt_ref[:, pl.ds(low, CHUNK)]
        weight = jnp.where(inside, weight, 0.0).T.astype(BF16)
        scale = jnp.dot(weight, rep16_ref[:heads], preferred_element_type=F32)
        load = scale.astype(BF16) * act_ref[pl.ds(low, CHUNK), :width]
        local = outer_dot(act_ref[pl.ds(low, CHUNK), width : width + N], load)
        through = spread_row(jnp.where(start < begin, jnp.exp2(at_end), 0.0), rep_ref[...])
        final = local + through * sin_ref[part].astype(F32)
        target = meta[5 + slot]
        opened = jnp.where(start < 0, jnp.exp2(totals[part][:, :1] + at_end), 0.0)

        @pl.when(slot == 0)
        def _():
            first_ref[...] = jnp.broadcast_to(spread_row(opened, rep_ref[...]), first_ref.shape)

        tail = jnp.zeros((TAIL, 128), F32)
        row = iota((TAIL, CHUNK), 0)
        col = iota((TAIL, CHUNK), 1) + begin
        row16 = iota((TAIL, 16), 0)
        col16 = iota((TAIL, 16), 1) + begin - 16
        before = pl.multiple_of(jnp.maximum(low - 16, 0), 16)
        for tile in range(x_ref.shape[1] // 128):
            cols = slice(tile * 128, tile * 128 + 128)
            mine = (row >= 3 * tile) & (row < 3 * tile + 3)
            pick = (col == end - 3 + row - 3 * tile) & (col >= start) & mine
            mine16 = (row16 >= 3 * tile) & (row16 < 3 * tile + 3)
            pick16 = (col16 == end - 3 + row16 - 3 * tile) & (col16 >= start) & mine16
            rim = jnp.where(low > 0, x_ref[pl.ds(before, 16), cols].astype(F32), edge16[:, cols].astype(F32))
            tail = tail + jnp.dot(
                pick.astype(F32).astype(BF16), x_ref[pl.ds(low, CHUNK), cols], preferred_element_type=F32
            ) + jnp.dot(
                pick16.astype(F32).astype(BF16), rim.astype(BF16), preferred_element_type=F32
            )

        @pl.when(target >= 0)
        def _():
            fin_ref[target, :width] = final.T.astype(BF16)
            fin_ref[target, width : width + TAIL] = tail.astype(BF16)

        return 0

    done = jnp.int32(0)
    upto = jnp.int32(0)
    for slot in range(EMAX):
        done = done + (meta[1 + slot] <= first).astype(jnp.int32)
        upto = upto + (meta[1 + slot] <= first + BLOCK).astype(jnp.int32)
    lax.fori_loop(done, upto, finish, 0)
    edge16[...] = x_ref[BLOCK - 16 :, :]

    @pl.when(step == pl.num_programs(0) - 1)
    def _():
        start = last_start(meta, span - 1)
        gate = spread_row(jnp.where(start < 0, jnp.exp2(total[:, :1]), 0.0), rep_ref[...])
        gate = jnp.broadcast_to(gate, (16, width))
        high = gate.astype(BF16).astype(F32)
        pay_ref[:N] = state[...].astype(BF16)
        pay_ref[N:] = jnp.where(iota((16, width), 0) == 0, high, gate - high).astype(BF16)


def output_kernel(origin, held, meta, act_ref, dt_ref, cum_ref, sin_ref, gain_ref, rep16_ref, *refs):
    out_ref = refs[held]
    step = origin + pl.program_id(0)
    heads = dt_ref.shape[0]
    width = out_ref.shape[1]
    for part in range(BLOCK // CHUNK):
        low = part * CHUNK
        rows = slice(low, low + CHUNK)
        begin = step * BLOCK + low
        cum = cum_ref[:, rows]
        back = cum - jnp.log2(dt_ref[:, rows])
        ahead = cum.T
        b_act = act_ref[rows, width : width + N]
        c_act = act_ref[rows, width + N : width + 2 * N]
        place = iota((CHUNK, CHUNK), 0) + begin
        other = iota((CHUNK, CHUNK), 1) + begin
        scores = lax.dot_general(c_act, b_act, (((1,), (1,)), ((), ())), preferred_element_type=F32)
        scores = jnp.where((other <= place) & (other >= starts_of(meta, place)), scores, 0.0)
        lane = iota((heads, CHUNK), 1) + begin
        before = jnp.where(last_start(meta, begin) < begin, next_end(meta, begin), -1)
        entry = jnp.where(lane < before, jnp.exp2(cum), 0.0)
        entry = jnp.concatenate([entry, entry - entry.astype(BF16).astype(F32)], axis=0).T.astype(BF16)
        left_half = iota((CHUNK, 128), 1) < P_SIZE
        for quad in range(heads // 4):
            cols = slice(quad * 256, quad * 256 + 256)
            outer = jnp.dot(c_act, sin_ref[part, :, cols], preferred_element_type=F32)
            scale = jnp.dot(entry, rep16_ref[:, cols], preferred_element_type=F32)
            sums = []
            for pair in (2 * quad, 2 * quad + 1):
                mixes = []
                for head in (2 * pair, 2 * pair + 1):
                    spread = jnp.minimum(ahead[:, head : head + 1] - back[head : head + 1, :], 0.0)
                    mixes.append((jnp.exp2(spread) * scores).astype(BF16))
                x_pair = act_ref[rows, pair * 128 : pair * 128 + 128]
                zero = jnp.zeros_like(x_pair)
                split = jnp.concatenate(
                    [jnp.where(left_half, x_pair, zero), jnp.where(left_half, zero, x_pair)], axis=0
                )
                sums.append(
                    jnp.dot(jnp.concatenate(mixes, axis=1), split, preferred_element_type=F32)
                )
            inner = jnp.concatenate(sums, axis=1)
            value = inner + scale * outer + gain_ref[:, cols] * act_ref[rows, cols].astype(F32)
            out_ref[rows, cols] = value.astype(BF16)


def gates_of(pay_ref, cols):
    gates = pay_ref[N:, cols].astype(F32)
    return gates[0:1] + gates[1:2]


def pair_kernel(shard_ref, own_ref, got_ref, half_ref):
    side = half_ref.shape[1]

    def join(early, late, cols):
        after = gates_of(late, cols)
        gate = jnp.broadcast_to(after * gates_of(early, cols), (PAY - N, side))
        high = gate.astype(BF16).astype(F32)
        half_ref[:N] = (late[:N, cols].astype(F32) + after * early[:N, cols].astype(F32)).astype(BF16)
        half_ref[N:] = jnp.where(iota((PAY - N, side), 0) == 0, high, gate - high).astype(BF16)

    @pl.when(shard_ref[0] % 2 == 0)
    def _():
        join(own_ref, got_ref, slice(0, side))

    @pl.when(shard_ref[0] % 2 == 1)
    def _():
        join(got_ref, own_ref, slice(side, 2 * side))


def prefix_kernel(shard_ref, gathered, prefix_ref, held):
    held[...] = jnp.zeros_like(held)

    def one(index, _):
        gates = gathered[index, N:].astype(F32)
        held[...] = (gates[0:1] + gates[1:2]) * held[...] + gathered[index, :N].astype(F32)
        return 0

    lax.fori_loop(0, shard_ref[0] // 2, one, 0)
    prefix_ref[...] = held[...].astype(BF16)


def carry_kernel(shard_ref, meta, mine_ref, other_ref, early_ref, first_ref, carried_ref, send_ref):
    side = mine_ref.shape[1]
    lower, upper = slice(0, side), slice(side, 2 * side)

    @pl.when(shard_ref[0] % 2 == 0)
    def _():
        carried_ref[:, lower] = mine_ref[...]
        carried_ref[:, upper] = other_ref[...]

    @pl.when(shard_ref[0] % 2 == 1)
    def _():
        for cols, part in ((lower, other_ref), (upper, mine_ref)):
            carried_ref[:, cols] = (
                early_ref[:N, cols].astype(F32) + gates_of(early_ref, cols) * part[...].astype(F32)
            ).astype(BF16)

    send_ref[...] = jnp.zeros_like(send_ref)
    send_ref[meta[5] // CAP] = (first_ref[0:1] * carried_ref[...].astype(F32)).T.astype(BF16)


def correct_kernel(meta, base_ref, c_ref, carry_ref, carried_ref, rep16_ref, out_ref):
    step = pl.program_id(0)
    touched = (meta[0] < 0) & (meta[1] > step * BLOCK)

    @pl.when(touched)
    def _():
        entry = carry_ref[...]
        entry = jnp.concatenate([entry, entry - entry.astype(BF16).astype(F32)], axis=0).T.astype(BF16)
        width = out_ref.shape[1]
        for tile in range(width // 256):
            cols = slice(tile * 256, tile * 256 + 256)
            outer = jnp.dot(c_ref[...], carried_ref[:, cols], preferred_element_type=F32)
            scale = jnp.dot(entry, rep16_ref[:, cols], preferred_element_type=F32)
            out_ref[:, cols] = (base_ref[:, cols].astype(F32) + scale * outer).astype(BF16)

    @pl.when(jnp.logical_not(touched))
    def _():
        out_ref[...] = base_ref[...]


def params():
    return pltpu.CompilerParams(vmem_limit_bytes=VMEM, dimension_semantics=("arbitrary",))


def whole(shape):
    return pl.BlockSpec(shape, lambda *_: (0,) * len(shape))


def on_device(
    conv_input, conv_weight, conv_bias, step_size, log_decay, skip_gain, doc_bounds, doc_owner
):
    span, channels = conv_input.shape[1:]
    heads = step_size.shape[1]
    width = heads * P_SIZE
    steps = span // BLOCK
    chunks = span // CHUNK
    owners = lax.axis_size("stream")
    slots = owners * CAP
    rows = width + TAIL
    shard = lax.axis_index("seq").astype(jnp.int32).reshape(1)
    rows_in = conv_input[0]
    rim = shifted(rows_in[span - 16 :], "seq", 1)
    rep = (np.arange(width)[None, :] // P_SIZE == np.arange(heads)[:, None]).astype(np.float32)
    rep16 = np.concatenate([rep, rep], 0).astype(BF16)
    ticks = np.arange(CHUNK)
    tri = (ticks[:, None] <= ticks[None, :]).astype(BF16)
    order = np.arange(3 * CHUNK)
    tick, lag = 8 * (order // 24) + order % 8, order % 24 // 8 + 1
    source = np.arange(CHUNK + 16)
    move = (source[None, :] - 16 == (tick - lag)[:, None]).astype(BF16)
    slot = np.broadcast_to((4 * tick + lag)[:, None], (3 * CHUNK, 128)).astype(np.int32)
    smem = pl.BlockSpec(memory_space=pltpu.SMEM)
    per_head = pl.BlockSpec((heads, BLOCK), lambda i, *_: (0, i))
    act, cum, carry, sin, pay, fin, first, meta = pl.pallas_call(
        states_kernel,
        grid=(steps,),
        in_specs=[
            smem, smem, smem,
            pl.BlockSpec((BLOCK, channels), lambda i: (i, 0)),
            whole((16, channels)),
            per_head, per_head,
            whole((4, channels)), whole((1, channels)),
            whole((heads, width)), whole((2 * heads, width)), whole((CHUNK, CHUNK)),
            whole(move.shape), whole(slot.shape),
        ],
        out_specs=[
            pl.BlockSpec((BLOCK, channels), lambda i: (i, 0)),
            per_head, per_head,
            pl.BlockSpec((BLOCK // CHUNK, N, width), lambda i: (i, 0, 0)),
            whole((PAY, width)), whole((slots, rows, N)), whole((8, width)),
            smem,
        ],
        out_shape=[
            jax.ShapeDtypeStruct((span, channels), BF16),
            jax.ShapeDtypeStruct((heads, span), F32),
            jax.ShapeDtypeStruct((heads, span), F32),
            jax.ShapeDtypeStruct((chunks, N, width), BF16),
            jax.ShapeDtypeStruct((PAY, width), BF16),
            jax.ShapeDtypeStruct((slots, rows, N), BF16),
            jax.ShapeDtypeStruct((8, width), F32),
            jax.ShapeDtypeStruct((16,), jnp.int32),
        ],
        scratch_shapes=[
            pltpu.VMEM((N, width), F32),
            pltpu.VMEM((16, channels), BF16),
            pltpu.VMEM((heads, CHUNK), F32),
            pltpu.VMEM((BLOCK // CHUNK, heads, CHUNK), F32),
            pltpu.VMEM((8, channels), F32),
            pltpu.VMEM((1 + BLOCK // CHUNK,) + move.shape, BF16),
            pltpu.SMEM((owners,), jnp.int32),
        ],
        compiler_params=params(),
        cost_estimate=pl.CostEstimate(
            flops=2 * span * width * N * 2, bytes_accessed=40 << 20, transcendentals=span * channels
        ),
        name="states",
    )(
        shard, doc_bounds, doc_owner, rows_in, rim, step_size[0], log_decay[0],
        conv_weight, conv_bias[None], rep, rep16, tri, move, slot,
    )

    gain = jnp.repeat(skip_gain, P_SIZE)[None]
    prefetch = functools.partial(pltpu.PrefetchScalarGridSpec, num_scalar_prefetch=1)

    def outputs(first, last, base):
        hold = [] if base is None else [base]
        return pl.pallas_call(
            functools.partial(output_kernel, first, bool(hold)),
            grid_spec=prefetch(
                grid=(last - first,),
                in_specs=[
                    pl.BlockSpec((BLOCK, channels), lambda i, *_: (first + i, 0)),
                    pl.BlockSpec((heads, BLOCK), lambda i, *_: (0, first + i)),
                    pl.BlockSpec((heads, BLOCK), lambda i, *_: (0, first + i)),
                    pl.BlockSpec((BLOCK // CHUNK, N, width), lambda i, *_: (first + i, 0, 0)),
                    whole((1, width)), whole((2 * heads, width)),
                ] + [pl.BlockSpec(memory_space=pl.ANY)] * len(hold),
                out_specs=pl.BlockSpec((BLOCK, width), lambda i, *_: (first + i, 0)),
            ),
            out_shape=jax.ShapeDtypeStruct((span, width), BF16),
            input_output_aliases={7: 0} if hold else {},
            compiler_params=params(),
            cost_estimate=pl.CostEstimate(
                flops=2 * (last - first) * BLOCK * width * N * 4,
                bytes_accessed=(last - first) * (4 << 20),
                transcendentals=(last - first) * BLOCK * CHUNK * heads,
            ),
            name="outputs",
        )(meta, act, step_size[0], cum, sin, gain, rep16, *hold)

    side = width // 2
    count = lax.axis_size("seq")
    pairs = [(index, index ^ 1) for index in range(count)]
    early = lax.ppermute(pay, "seq", pairs)
    base = outputs(0, 1, None)
    early, base = lax.optimization_barrier((early, base))
    half = pl.pallas_call(
        pair_kernel,
        in_specs=[smem, whole((PAY, width)), whole((PAY, width))],
        out_specs=whole((PAY, side)),
        out_shape=jax.ShapeDtypeStruct((PAY, side), BF16),
        compiler_params=pltpu.CompilerParams(vmem_limit_bytes=VMEM),
        name="pair",
    )(shard, pay, early)
    half, fin = lax.optimization_barrier((half, fin))
    gathered = lax.all_gather(
        half[None], "seq", axis=0, tiled=True,
        axis_index_groups=[list(range(0, count, 2)), list(range(1, count, 2))],
    )
    got = lax.all_to_all(
        fin.reshape(owners, CAP, rows, N), "stream", split_axis=0, concat_axis=0, tiled=True
    )
    base = outputs(1, steps - 2, base)
    gathered, base = lax.optimization_barrier((gathered, base))
    mine = pl.pallas_call(
        prefix_kernel,
        in_specs=[smem, whole(gathered.shape)],
        out_specs=whole((N, side)),
        out_shape=jax.ShapeDtypeStruct((N, side), BF16),
        scratch_shapes=[pltpu.VMEM((N, side), F32)],
        compiler_params=pltpu.CompilerParams(vmem_limit_bytes=VMEM),
        name="prefix",
    )(shard, gathered)
    other = lax.ppermute(mine, "seq", pairs)
    base = outputs(steps - 2, steps, base)
    other, base = lax.optimization_barrier((other, base))
    carried, send = pl.pallas_call(
        carry_kernel,
        in_specs=[smem, smem, whole((N, side)), whole((N, side)), whole((PAY, width)), whole((8, width))],
        out_specs=[whole((N, width)), whole((owners, width, N))],
        out_shape=[
            jax.ShapeDtypeStruct((N, width), BF16),
            jax.ShapeDtypeStruct((owners, width, N), BF16),
        ],
        compiler_params=pltpu.CompilerParams(vmem_limit_bytes=VMEM),
        name="carry",
    )(shard, meta, mine, other, early, first)
    more = lax.all_to_all(send, "stream", split_axis=0, concat_axis=0, tiled=True)

    out = pl.pallas_call(
        correct_kernel,
        grid_spec=prefetch(
            grid=(steps,),
            in_specs=[
                pl.BlockSpec((BLOCK, width), lambda i, *_: (i, 0)),
                pl.BlockSpec((BLOCK, N), lambda i, *_: (i, width // N + 1)),
                per_head,
                whole((N, width)), whole((2 * heads, width)),
            ],
            out_specs=pl.BlockSpec((BLOCK, width), lambda i, *_: (i, 0)),
        ),
        out_shape=jax.ShapeDtypeStruct((span, width), BF16),
        input_output_aliases={1: 0},
        compiler_params=params(),
        cost_estimate=pl.CostEstimate(
            flops=2 * span * width * N, bytes_accessed=18 << 20, transcendentals=0
        ),
        name="correct",
    )(meta, base, act, carry, carried, rep16)

    more = jnp.concatenate([more[:, None], jnp.zeros((owners, CAP - 1, width, N), BF16)], axis=1)
    ssm = got[:, :, :width].astype(F32) + more.astype(F32)
    ssm = ssm.reshape(1, 1, owners, CAP, heads, P_SIZE, N)
    tiles = channels // N
    conv = got[:, :, width : width + 3 * tiles].reshape(owners, CAP, tiles, 3, N)
    conv = conv.transpose(0, 1, 3, 2, 4).reshape(1, 1, owners, CAP, 3, channels)
    return out[None], ssm, conv


def solution(mesh):
    in_specs = (
        P("stream", "seq", None),
        P(),
        P(),
        P("stream", None, "seq"),
        P("stream", None, "seq"),
        P(),
        P("stream", None),
        P("stream", None),
    )
    out_specs = (
        P("stream", "seq", None),
        P("stream", "seq", None, None, None, None, None),
        P("stream", "seq", None, None, None, None),
    )
    return jax.shard_map(
        on_device, mesh=mesh, in_specs=in_specs, out_specs=out_specs, check_vma=False
    )
```

```python
import functools

import jax
import jax.numpy as jnp
import numpy as np
from jax import lax
from jax.experimental import pallas as pl
from jax.experimental.pallas import tpu as pltpu
from jax.sharding import PartitionSpec as P

P_SIZE = 64
N = 128
EMAX = 4
CAP = 2
CHUNK = 128
BLOCK = 512
FAR = 1 << 30
LOG2E = 1.4426950408889634
PAY = 144
TAIL = 32
MIB = 1024 * 1024

F32 = jnp.float32
BF16 = jnp.bfloat16


def shifted(value, axis, steps):
    count = lax.axis_size(axis)
    leading, last = (max(0, -steps), min(count, count - steps))
    return lax.ppermute(value, axis, [(source, source + steps) for source in range(leading, last)])


def iota(shape, axis):
    return lax.broadcasted_iota(jnp.int32, shape, axis)


def outer_dot(left, right):
    return lax.dot_general(left, right, (((0,), (0,)), ((), ())), preferred_element_type=F32)


def halves(value):
    high = value.astype(BF16)
    low = (value - high.astype(F32)).astype(BF16)
    return jnp.concatenate([high, low], axis=0)


def thirds(value):
    high = value.astype(BF16)
    rest = value - high.astype(F32)
    mid = rest.astype(BF16)
    low = (rest - mid.astype(F32)).astype(BF16)
    return jnp.concatenate([high, mid, low], axis=0)


def spread_row(column, rep):
    return jnp.sum(rep * column, axis=0, keepdims=True)


def last_start(meta, place):
    start = meta[0]
    for slot in range(EMAX):
        end = meta[1 + slot]
        start = jnp.where(end <= place, end, start)
    return start


def next_end(meta, place):
    end = FAR
    for slot in reversed(range(EMAX)):
        end = jnp.where(meta[1 + slot] > place, meta[1 + slot], end)
    return end


def starts_of(meta, rows):
    start = jnp.full(rows.shape, meta[0], jnp.int32)
    for slot in range(EMAX):
        end = meta[1 + slot]
        start = jnp.where(rows >= end, end, start)
    return start


def read_docs(bounds, owners, meta, count, anchor, span):
    for slot in range(EMAX):
        meta[1 + slot] = FAR
        meta[5 + slot] = 0
    for owner in range(count.shape[0]):
        count[owner] = 0

    def one(index, carry):
        found, prior, start = carry
        end = bounds[0, index]
        owner = owners[0, index]
        mine = (end > prior) & (end > anchor) & (end <= anchor + span) & (found < EMAX)

        @pl.when(mine)
        def _():
            meta[1 + found] = end - anchor
            rank = count[owner]
            meta[5 + found] = jnp.where(rank < CAP, owner * CAP + rank, -1)
            count[owner] = rank + 1

        return found + mine.astype(jnp.int32), end, jnp.where(end <= anchor, end, start)

    zero = jnp.int32(0)
    _, _, start = lax.fori_loop(0, bounds.shape[1], one, (zero, zero, zero))
    meta[0] = start - anchor


def conv_rows(x_ref, edge16, moves, weights, act_ref, first, part, choice):
    low = part * CHUNK
    rows = slice(low, low + CHUNK)
    pick = moves[choice]
    for tile in range(x_ref.shape[1] // 256):
        cols = slice(tile * 256, tile * 256 + 256)
        if part:
            wide = x_ref[low - 16 : low + CHUNK, cols]
        else:
            wide = jnp.concatenate([edge16[:, cols], x_ref[rows, cols]], axis=0)
        moved = jnp.dot(pick, wide, preferred_element_type=F32)
        moved = moved.reshape(CHUNK // 8, 3, 8, 256)
        mixed = weights[4:5, cols] + weights[0:1, cols] * x_ref[rows, cols].astype(F32)
        for lag in range(1, 4):
            mixed = mixed + weights[lag : lag + 1, cols] * moved[:, lag - 1].reshape(CHUNK, 256)
        act_ref[pl.ds(first + low, CHUNK), cols] = (mixed + mixed * jnp.tanh(mixed)).astype(BF16)


def states_kernel(
    shard_ref, bounds, owners, x_ref, rim_ref, dt_ref, ld_ref, w_ref, bias_ref,
    rep_ref, rep16_ref, tri_ref, move_ref, slot_ref,
    act_ref, cum_ref, carry_ref, sin_ref, pay_ref, fin_ref, first_ref, meta,
    state, edge16, total, totals, weights, moves, count,
):
    step = pl.program_id(0)
    heads = dt_ref.shape[0]
    width = rep_ref.shape[1]
    span = pl.num_programs(0) * BLOCK
    parts = BLOCK // CHUNK
    first = pl.multiple_of(step * BLOCK, BLOCK)

    @pl.when(step == 0)
    def _():
        read_docs(bounds, owners, meta, count, shard_ref[0] * span, span)
        state[...] = jnp.zeros_like(state)
        total[...] = jnp.zeros_like(total)
        fin_ref[...] = jnp.zeros_like(fin_ref)
        first_ref[...] = jnp.zeros_like(first_ref)
        edge16[...] = rim_ref[...]
        weights[0:4] = 0.5 * w_ref[...]
        weights[4:5] = 0.5 * bias_ref[...]
        moves[0] = move_ref[...]

    choices = []
    for part in range(parts):
        begin = first + part * CHUNK
        near = (meta[0] > begin - 3) & (meta[0] < begin + CHUNK)
        for slot in range(EMAX):
            near = near | ((meta[1 + slot] > begin - 3) & (meta[1 + slot] < begin + CHUNK))

        @pl.when(near)
        def _():
            tick = slot_ref[...] // 4 + begin
            kept = (tick - starts_of(meta, tick) >= slot_ref[...] % 4).astype(F32)
            moves[1 + part, :, :128] = (kept * move_ref[:, :128].astype(F32)).astype(BF16)
            moves[1 + part, :, 128:] = (kept[:, :16] * move_ref[:, 128:].astype(F32)).astype(BF16)

        choices.append(jnp.where(near, 1 + part, 0))

    conv_rows(x_ref, edge16, moves, weights, act_ref, first, 0, choices[0])
    running = total[...]
    for part in range(parts):
        low = part * CHUNK
        rows = slice(low, low + CHUNK)
        begin = first + low
        if part + 1 < parts:
            conv_rows(x_ref, edge16, moves, weights, act_ref, first, part + 1, choices[part + 1])
        summed = jnp.dot(
            thirds(ld_ref[:, rows] * LOG2E), tri_ref[...], preferred_element_type=F32
        )
        cum = summed[:heads] + summed[heads : 2 * heads] + summed[2 * heads :]
        there = pl.ds(begin, CHUNK)
        cum_ref[:, there] = cum
        lane = iota((heads, CHUNK), 1) + begin
        open_end = jnp.where(meta[0] < 0, meta[1], -1)
        carry_ref[:, there] = jnp.where(lane < open_end, jnp.exp2(running + cum), 0.0)
        totals[part] = running
        start = last_start(meta, begin + CHUNK - 1)
        last = cum[:, CHUNK - 1 :]
        weight = jnp.where(lane >= start, jnp.exp2(last - cum) * dt_ref[:, rows], 0.0)
        weight = weight.T.astype(BF16)
        through = spread_row(jnp.where(start < begin, jnp.exp2(last), 0.0), rep_ref[...])
        b_turned = act_ref[there, width : width + N].T
        for tile in range(width // 256):
            cols = slice(tile * 256, tile * 256 + 256)
            held = state[:, cols]
            sin_ref[part, :, cols] = held.astype(BF16)
            scale = jnp.dot(weight, rep16_ref[:heads, cols], preferred_element_type=F32)
            load = scale.astype(BF16) * act_ref[there, cols]
            grown = jnp.dot(b_turned, load, preferred_element_type=F32)
            state[:, cols] = through[:, cols] * held + grown
        running = running + last
    total[...] = running

    def finish(slot, _):
        end = meta[1 + slot]
        start = jnp.where(slot > 0, meta[jnp.maximum(slot, 1)], meta[0])
        part = (end - 1 - first) // CHUNK
        low = pl.multiple_of(part * CHUNK, CHUNK)
        begin = first + low
        lane = iota((heads, CHUNK), 1) + begin
        there = pl.ds(pl.multiple_of(begin, CHUNK), CHUNK)
        cum = cum_ref[:, there]
        at_end = jnp.sum(jnp.where(lane == end - 1, cum, 0.0), axis=1, keepdims=True)
        inside = (lane < end) & (lane >= start)
        weight = jnp.exp2(jnp.minimum(at_end - cum, 0.0)) * dt_ref[:, pl.ds(low, CHUNK)]
        weight = jnp.where(inside, weight, 0.0).T.astype(BF16)
        scale = jnp.dot(weight, rep16_ref[:heads], preferred_element_type=F32)
        load = scale.astype(BF16) * act_ref[there, :width]
        local = outer_dot(act_ref[there, width : width + N], load)
        through = spread_row(jnp.where(start < begin, jnp.exp2(at_end), 0.0), rep_ref[...])
        final = local + through * sin_ref[part].astype(F32)
        target = meta[5 + slot]
        opened = jnp.where(start < 0, jnp.exp2(totals[part][:, :1] + at_end), 0.0)

        @pl.when(slot == 0)
        def _():
            first_ref[...] = jnp.broadcast_to(spread_row(opened, rep_ref[...]), first_ref.shape)

        tail = jnp.zeros((TAIL, 128), F32)
        row = iota((TAIL, CHUNK), 0)
        col = iota((TAIL, CHUNK), 1) + begin
        row16 = iota((TAIL, 16), 0)
        col16 = iota((TAIL, 16), 1) + begin - 16
        before = pl.multiple_of(jnp.maximum(low - 16, 0), 16)
        for tile in range(x_ref.shape[1] // 128):
            cols = slice(tile * 128, tile * 128 + 128)
            mine = (row >= 3 * tile) & (row < 3 * tile + 3)
            pick = (col == end - 3 + row - 3 * tile) & (col >= start) & mine
            mine16 = (row16 >= 3 * tile) & (row16 < 3 * tile + 3)
            pick16 = (col16 == end - 3 + row16 - 3 * tile) & (col16 >= start) & mine16
            rim = jnp.where(low > 0, x_ref[pl.ds(before, 16), cols].astype(F32), edge16[:, cols].astype(F32))
            tail = tail + jnp.dot(
                pick.astype(F32).astype(BF16), x_ref[pl.ds(low, CHUNK), cols], preferred_element_type=F32
            ) + jnp.dot(
                pick16.astype(F32).astype(BF16), rim.astype(BF16), preferred_element_type=F32
            )

        @pl.when(target >= 0)
        def _():
            fin_ref[target, :width] = final.T.astype(BF16)
            fin_ref[target, width : width + TAIL] = tail.astype(BF16)

        return 0

    done = jnp.int32(0)
    upto = jnp.int32(0)
    for slot in range(EMAX):
        done = done + (meta[1 + slot] <= first).astype(jnp.int32)
        upto = upto + (meta[1 + slot] <= first + BLOCK).astype(jnp.int32)
    lax.fori_loop(done, upto, finish, 0)
    edge16[...] = x_ref[BLOCK - 16 :, :]

    @pl.when(step == pl.num_programs(0) - 1)
    def _():
        start = last_start(meta, span - 1)
        gate = spread_row(jnp.where(start < 0, jnp.exp2(total[:, :1]), 0.0), rep_ref[...])
        gate = jnp.broadcast_to(gate, (16, width))
        high = gate.astype(BF16).astype(F32)
        pay_ref[:N] = state[...].astype(BF16)
        pay_ref[N:] = jnp.where(iota((16, width), 0) == 0, high, gate - high).astype(BF16)


def output_kernel(origin, held, meta, act_ref, dt_ref, cum_ref, sin_ref, gain_ref, rep16_ref, *refs):
    out_ref = refs[held]
    step = origin + pl.program_id(0)
    heads = dt_ref.shape[0]
    width = out_ref.shape[1]
    parts = BLOCK // CHUNK
    for part in range(parts):
        begin = pl.multiple_of(step * BLOCK + part * CHUNK, CHUNK)
        rows = pl.ds(begin, CHUNK)
        here = slice(part * CHUNK, part * CHUNK + CHUNK)
        cum = cum_ref[:, rows]
        back = cum - jnp.log2(dt_ref[:, here])
        ahead = cum.T
        b_act = act_ref[rows, width : width + N]
        c_act = act_ref[rows, width + N : width + 2 * N]
        place = iota((CHUNK, CHUNK), 0) + begin
        other = iota((CHUNK, CHUNK), 1) + begin
        scores = lax.dot_general(c_act, b_act, (((1,), (1,)), ((), ())), preferred_element_type=F32)
        scores = jnp.where((other <= place) & (other >= starts_of(meta, place)), scores, 0.0)
        lane = iota((heads, CHUNK), 1) + begin
        before = jnp.where(last_start(meta, begin) < begin, next_end(meta, begin), -1)
        entry = jnp.where(lane < before, jnp.exp2(cum), 0.0)
        entry = jnp.concatenate([entry, entry - entry.astype(BF16).astype(F32)], axis=0).T.astype(BF16)
        left_half = iota((CHUNK, 128), 1) < P_SIZE
        for quad in range(heads // 4):
            cols = slice(quad * 256, quad * 256 + 256)
            outer = jnp.dot(c_act, sin_ref[part, :, cols], preferred_element_type=F32)
            scale = jnp.dot(entry, rep16_ref[:, cols], preferred_element_type=F32)
            sums = []
            for pair in (2 * quad, 2 * quad + 1):
                mixes = []
                for head in (2 * pair, 2 * pair + 1):
                    spread = jnp.minimum(ahead[:, head : head + 1] - back[head : head + 1, :], 0.0)
                    mixes.append((jnp.exp2(spread) * scores).astype(BF16))
                x_pair = act_ref[rows, pair * 128 : pair * 128 + 128]
                zero = jnp.zeros_like(x_pair)
                split = jnp.concatenate(
                    [jnp.where(left_half, x_pair, zero), jnp.where(left_half, zero, x_pair)], axis=0
                )
                sums.append(
                    jnp.dot(jnp.concatenate(mixes, axis=1), split, preferred_element_type=F32)
                )
            inner = jnp.concatenate(sums, axis=1)
            value = inner + scale * outer + gain_ref[:, cols] * act_ref[rows, cols].astype(F32)
            out_ref[rows, cols] = value.astype(BF16)


def gates_of(pay_ref, cols):
    gates = pay_ref[N:, cols].astype(F32)
    return gates[0:1] + gates[1:2]


def pair_kernel(shard_ref, own_ref, got_ref, half_ref):
    side = half_ref.shape[1]

    def join(early, late, cols):
        after = gates_of(late, cols)
        gate = jnp.broadcast_to(after * gates_of(early, cols), (PAY - N, side))
        high = gate.astype(BF16).astype(F32)
        half_ref[:N] = (late[:N, cols].astype(F32) + after * early[:N, cols].astype(F32)).astype(BF16)
        half_ref[N:] = jnp.where(iota((PAY - N, side), 0) == 0, high, gate - high).astype(BF16)

    @pl.when(shard_ref[0] % 2 == 0)
    def _():
        join(own_ref, got_ref, slice(0, side))

    @pl.when(shard_ref[0] % 2 == 1)
    def _():
        join(got_ref, own_ref, slice(side, 2 * side))


def prefix_kernel(*refs):
    prefix_ref = refs[-1]
    side = prefix_ref.shape[1]
    total = jnp.zeros((N, side), F32)
    for ref in refs[:-1]:
        total = gates_of(ref, slice(0, side)) * total + ref[:N].astype(F32)
    prefix_ref[...] = total.astype(BF16)


def carry_kernel(shard_ref, stream_ref, meta, mine_ref, other_ref, early_ref, first_ref, carried_ref, *sends):
    side = mine_ref.shape[1]
    lower, upper = slice(0, side), slice(side, 2 * side)

    @pl.when(shard_ref[0] % 2 == 0)
    def _():
        carried_ref[:, lower] = mine_ref[...]
        carried_ref[:, upper] = other_ref[...]

    @pl.when(shard_ref[0] % 2 == 1)
    def _():
        for cols, part in ((lower, other_ref), (upper, mine_ref)):
            carried_ref[:, cols] = (
                early_ref[:N, cols].astype(F32) + gates_of(early_ref, cols) * part[...].astype(F32)
            ).astype(BF16)

    value = (first_ref[0:1] * carried_ref[...].astype(F32)).T.astype(BF16)
    apart = (meta[5] // CAP) ^ stream_ref[0]
    for index, ref in enumerate(sends):
        ref[...] = jnp.where(apart == index, value, jnp.zeros_like(value))


def correct_kernel(meta, base_ref, act_ref, carry_ref, carried_ref, rep16_ref, out_ref):
    width = out_ref.shape[1]
    begin = pl.multiple_of(pl.program_id(0) * BLOCK, BLOCK)
    rows = pl.ds(begin, BLOCK)
    touched = (meta[0] < 0) & (meta[1] > begin)

    @pl.when(touched)
    def _():
        entry = carry_ref[:, rows]
        entry = jnp.concatenate([entry, entry - entry.astype(BF16).astype(F32)], axis=0).T.astype(BF16)
        c_act = act_ref[rows, width + N : width + 2 * N]
        for tile in range(width // 256):
            cols = slice(tile * 256, tile * 256 + 256)
            outer = jnp.dot(c_act, carried_ref[:, cols], preferred_element_type=F32)
            scale = jnp.dot(entry, rep16_ref[:, cols], preferred_element_type=F32)
            out_ref[:, cols] = (base_ref[rows, cols].astype(F32) + scale * outer).astype(BF16)

    @pl.when(jnp.logical_not(touched))
    def _():
        out_ref[...] = base_ref[rows, :]


def params(mib):
    return pltpu.CompilerParams(vmem_limit_bytes=mib * MIB)


def whole(shape):
    return pl.BlockSpec(shape, lambda *_: (0,) * len(shape))


def on_device(
    conv_input, conv_weight, conv_bias, step_size, log_decay, skip_gain, doc_bounds, doc_owner
):
    span, channels = conv_input.shape[1:]
    heads = step_size.shape[1]
    width = heads * P_SIZE
    steps = span // BLOCK
    chunks = span // CHUNK
    owners = lax.axis_size("stream")
    slots = owners * CAP
    rows = width + TAIL
    shard = lax.axis_index("seq").astype(jnp.int32).reshape(1)
    rows_in = conv_input[0]
    rim = shifted(rows_in[span - 16 :], "seq", 1)
    rep = (np.arange(width)[None, :] // P_SIZE == np.arange(heads)[:, None]).astype(np.float32)
    rep16 = np.concatenate([rep, rep], 0).astype(BF16)
    ticks = np.arange(CHUNK)
    tri = (ticks[:, None] <= ticks[None, :]).astype(BF16)
    order = np.arange(3 * CHUNK)
    tick, lag = 8 * (order // 24) + order % 8, order % 24 // 8 + 1
    source = np.arange(CHUNK + 16)
    move = (source[None, :] - 16 == (tick - lag)[:, None]).astype(BF16)
    slot = np.broadcast_to((4 * tick + lag)[:, None], (3 * CHUNK, 128)).astype(np.int32)
    smem = pl.BlockSpec(memory_space=pltpu.SMEM)
    resident = pl.BlockSpec(memory_space=pltpu.VMEM)
    stream = lax.axis_index("stream").astype(jnp.int32).reshape(1)
    per_head = pl.BlockSpec((heads, BLOCK), lambda i, *_: (0, i))
    act, cum, carry, sin, pay, fin, first, meta = pl.pallas_call(
        states_kernel,
        grid=(steps,),
        in_specs=[
            smem, smem, smem,
            pl.BlockSpec((BLOCK, channels), lambda i: (i, 0)),
            whole((16, channels)),
            per_head, per_head,
            whole((4, channels)), whole((1, channels)),
            whole((heads, width)), whole((2 * heads, width)), whole((CHUNK, CHUNK)),
            whole(move.shape), whole(slot.shape),
        ],
        out_specs=[
            resident, resident, resident,
            pl.BlockSpec((BLOCK // CHUNK, N, width), lambda i: (i, 0, 0)),
            whole((PAY, width)), whole((slots, rows, N)), whole((8, width)),
            smem,
        ],
        out_shape=[
            pltpu.VMEM((span, channels), BF16),
            pltpu.VMEM((heads, span), F32),
            pltpu.VMEM((heads, span), F32),
            jax.ShapeDtypeStruct((chunks, N, width), BF16),
            jax.ShapeDtypeStruct((PAY, width), BF16),
            jax.ShapeDtypeStruct((slots, rows, N), BF16),
            jax.ShapeDtypeStruct((8, width), F32),
            jax.ShapeDtypeStruct((16,), jnp.int32),
        ],
        scratch_shapes=[
            pltpu.VMEM((N, width), F32),
            pltpu.VMEM((16, channels), BF16),
            pltpu.VMEM((heads, CHUNK), F32),
            pltpu.VMEM((BLOCK // CHUNK, heads, CHUNK), F32),
            pltpu.VMEM((8, channels), F32),
            pltpu.VMEM((1 + BLOCK // CHUNK,) + move.shape, BF16),
            pltpu.SMEM((owners,), jnp.int32),
        ],
        compiler_params=params(18),
        cost_estimate=pl.CostEstimate(
            flops=2 * span * width * N * 2, bytes_accessed=40 << 20, transcendentals=span * channels
        ),
        name="states",
    )(
        shard, doc_bounds, doc_owner, rows_in, rim, step_size[0], log_decay[0],
        conv_weight, conv_bias[None], rep, rep16, tri, move, slot,
    )

    gain = jnp.repeat(skip_gain, P_SIZE)[None]
    prefetch = functools.partial(pltpu.PrefetchScalarGridSpec, num_scalar_prefetch=1)

    def outputs(first, last, base):
        hold = [] if base is None else [base]
        return pl.pallas_call(
            functools.partial(output_kernel, first, bool(hold)),
            grid_spec=prefetch(
                grid=(last - first,),
                in_specs=[
                    resident,
                    pl.BlockSpec((heads, BLOCK), lambda i, *_: (0, first + i)),
                    resident,
                    pl.BlockSpec((BLOCK // CHUNK, N, width), lambda i, *_: (first + i, 0, 0)),
                    whole((1, width)), whole((2 * heads, width)),
                ] + [resident] * len(hold),
                out_specs=resident,
            ),
            out_shape=pltpu.VMEM((span, width), BF16),
            input_output_aliases={7: 0} if hold else {},
            compiler_params=params(10),
            cost_estimate=pl.CostEstimate(
                flops=2 * (last - first) * BLOCK * width * N * 4,
                bytes_accessed=(last - first) * (4 << 20),
                transcendentals=(last - first) * BLOCK * CHUNK * heads,
            ),
            name="outputs",
        )(meta, act, step_size[0], cum, sin, gain, rep16, *hold)

    side = width // 2
    count = lax.axis_size("seq")
    pairs = [(index, index ^ 1) for index in range(count)]
    early = lax.ppermute(pay, "seq", pairs)
    base = outputs(0, 1, None)
    early, base = lax.optimization_barrier((early, base))
    half = pl.pallas_call(
        pair_kernel,
        in_specs=[smem, whole((PAY, width)), whole((PAY, width))],
        out_specs=whole((PAY, side)),
        out_shape=jax.ShapeDtypeStruct((PAY, side), BF16),
        compiler_params=params(8),
        name="pair",
    )(shard, pay, early)
    half, fin = lax.optimization_barrier((half, fin))
    chips = count // 2
    behind = [shifted(half, "seq", 2 * far) for far in range(chips - 1, 0, -1)]
    got = lax.all_to_all(
        fin.reshape(owners, CAP, rows, N), "stream", split_axis=0, concat_axis=0, tiled=True
    )
    base = outputs(1, steps - 2, base)
    *behind, base = lax.optimization_barrier((*behind, base))
    mine = pl.pallas_call(
        prefix_kernel,
        in_specs=[whole((PAY, side))] * len(behind),
        out_specs=whole((N, side)),
        out_shape=jax.ShapeDtypeStruct((N, side), BF16),
        compiler_params=params(8),
        name="prefix",
    )(*behind)
    other = lax.ppermute(mine, "seq", pairs)
    base = outputs(steps - 2, steps, base)
    other, base, got = lax.optimization_barrier((other, base, got))
    carried, *send = pl.pallas_call(
        carry_kernel,
        in_specs=[smem, smem, smem, whole((N, side)), whole((N, side)), whole((PAY, width)), whole((8, width))],
        out_specs=[whole((N, width))] + [whole((width, N))] * owners,
        out_shape=[jax.ShapeDtypeStruct((N, width), BF16)]
        + [jax.ShapeDtypeStruct((width, N), BF16)] * owners,
        compiler_params=params(8),
        name="carry",
    )(shard, stream, meta, mine, other, early, first)
    more = [send[0]]
    for apart in range(1, owners):
        swap = [(index, index ^ apart) for index in range(owners)]
        more.append(lax.ppermute(send[apart], "stream", swap))

    out = pl.pallas_call(
        correct_kernel,
        grid_spec=prefetch(
            grid=(steps,),
            in_specs=[
                resident, resident, resident,
                whole((N, width)), whole((2 * heads, width)),
            ],
            out_specs=pl.BlockSpec((BLOCK, width), lambda i, *_: (i, 0)),
        ),
        out_shape=jax.ShapeDtypeStruct((span, width), BF16),
        compiler_params=params(10),
        cost_estimate=pl.CostEstimate(
            flops=2 * span * width * N, bytes_accessed=18 << 20, transcendentals=0
        ),
        name="correct",
    )(meta, base, act, carry, carried, rep16)

    apart = (jnp.arange(owners) ^ stream)[:, None, None]
    extra = jnp.zeros((owners, width, N), F32)
    for index in range(owners):
        extra = jnp.where(apart == index, more[index][None].astype(F32), extra)
    ranks = jnp.arange(CAP)[None, :, None, None]
    ssm = got[:, :, :width].astype(F32) + jnp.where(ranks == 0, extra[:, None], 0.0)
    ssm = ssm.reshape(1, 1, owners, CAP, heads, P_SIZE, N)
    tiles = channels // N
    conv = got[:, :, width : width + 3 * tiles].reshape(owners, CAP, tiles, 3, N)
    conv = conv.transpose(0, 1, 3, 2, 4).reshape(1, 1, owners, CAP, 3, channels)
    return out[None], ssm, conv


def solution(mesh):
    in_specs = (
        P("stream", "seq", None),
        P(),
        P(),
        P("stream", None, "seq"),
        P("stream", None, "seq"),
        P(),
        P("stream", None),
        P("stream", None),
    )
    out_specs = (
        P("stream", "seq", None),
        P("stream", "seq", None, None, None, None, None),
        P("stream", "seq", None, None, None, None),
    )
    return jax.shard_map(
        on_device, mesh=mesh, in_specs=in_specs, out_specs=out_specs, check_vma=False
    )
```

```python
import functools

import jax
import jax.numpy as jnp
import numpy as np
from jax import lax
from jax.experimental import pallas as pl
from jax.experimental.pallas import tpu as pltpu
from jax.sharding import PartitionSpec as P

P_SIZE = 64
N = 128
EMAX = 4
CAP = 2
CHUNK = 128
BLOCK = 512
FAR = 1 << 30
LOG2E = 1.4426950408889634
PAY = 144
TAIL = 32
MIB = 1024 * 1024

F32 = jnp.float32
BF16 = jnp.bfloat16


def shifted(value, axis, steps):
    count = lax.axis_size(axis)
    leading, last = (max(0, -steps), min(count, count - steps))
    return lax.ppermute(value, axis, [(source, source + steps) for source in range(leading, last)])


def iota(shape, axis):
    return lax.broadcasted_iota(jnp.int32, shape, axis)


def outer_dot(left, right):
    return lax.dot_general(left, right, (((0,), (0,)), ((), ())), preferred_element_type=F32)


def halves(value):
    high = value.astype(BF16)
    low = (value - high.astype(F32)).astype(BF16)
    return jnp.concatenate([high, low], axis=0)


def thirds(value):
    high = value.astype(BF16)
    rest = value - high.astype(F32)
    mid = rest.astype(BF16)
    low = (rest - mid.astype(F32)).astype(BF16)
    return jnp.concatenate([high, mid, low], axis=0)


def spread_row(column, rep):
    return jnp.sum(rep * column, axis=0, keepdims=True)


def last_start(meta, place):
    start = meta[0]
    for slot in range(EMAX):
        end = meta[1 + slot]
        start = jnp.where(end <= place, end, start)
    return start


def next_end(meta, place):
    end = FAR
    for slot in reversed(range(EMAX)):
        end = jnp.where(meta[1 + slot] > place, meta[1 + slot], end)
    return end


def starts_of(meta, rows):
    start = jnp.full(rows.shape, meta[0], jnp.int32)
    for slot in range(EMAX):
        end = meta[1 + slot]
        start = jnp.where(rows >= end, end, start)
    return start


def read_docs(bounds, owners, meta, count, anchor, span):
    for slot in range(EMAX):
        meta[1 + slot] = FAR
        meta[5 + slot] = 0
    for owner in range(count.shape[0]):
        count[owner] = 0

    def one(index, carry):
        found, prior, start = carry
        end = bounds[0, index]
        owner = owners[0, index]
        mine = (end > prior) & (end > anchor) & (end <= anchor + span) & (found < EMAX)

        @pl.when(mine)
        def _():
            meta[1 + found] = end - anchor
            rank = count[owner]
            meta[5 + found] = jnp.where(rank < CAP, owner * CAP + rank, -1)
            count[owner] = rank + 1

        return found + mine.astype(jnp.int32), end, jnp.where(end <= anchor, end, start)

    zero = jnp.int32(0)
    _, _, start = lax.fori_loop(0, bounds.shape[1], one, (zero, zero, zero))
    meta[0] = start - anchor


def conv_kernel(
    shard_ref, bounds, owners, x_ref, rim_ref, w_ref, bias_ref, move_ref, slot_ref,
    act_ref, tail_ref, meta,
    edge16, weights, moves, count,
):
    step = pl.program_id(0)
    span = pl.num_programs(0) * BLOCK
    parts = BLOCK // CHUNK
    first = step * BLOCK

    @pl.when(step == 0)
    def _():
        read_docs(bounds, owners, meta, count, shard_ref[0] * span, span)
        tail_ref[...] = jnp.zeros_like(tail_ref)
        edge16[...] = rim_ref[...]
        weights[0:4] = 0.5 * w_ref[...]
        weights[4:5] = 0.5 * bias_ref[...]
        moves[0] = move_ref[...]

    choices = []
    for part in range(parts):
        begin = first + part * CHUNK
        near = (meta[0] > begin - 3) & (meta[0] < begin + CHUNK)
        for slot in range(EMAX):
            near = near | ((meta[1 + slot] > begin - 3) & (meta[1 + slot] < begin + CHUNK))

        @pl.when(near)
        def _():
            tick = slot_ref[...] // 4 + begin
            kept = (tick - starts_of(meta, tick) >= slot_ref[...] % 4).astype(F32)
            moves[1 + part, :, :128] = (kept * move_ref[:, :128].astype(F32)).astype(BF16)
            moves[1 + part, :, 128:] = (kept[:, :16] * move_ref[:, 128:].astype(F32)).astype(BF16)

        choices.append(jnp.where(near, 1 + part, 0))

    for part in range(parts):
        low = part * CHUNK
        rows = slice(low, low + CHUNK)
        pick = moves[choices[part]]
        for tile in range(x_ref.shape[1] // 256):
            cols = slice(tile * 256, tile * 256 + 256)
            if part:
                wide = x_ref[low - 16 : low + CHUNK, cols]
            else:
                wide = jnp.concatenate([edge16[:, cols], x_ref[rows, cols]], axis=0)
            moved = jnp.dot(pick, wide, preferred_element_type=F32)
            moved = moved.reshape(CHUNK // 8, 3, 8, 256)
            mixed = weights[4:5, cols] + weights[0:1, cols] * x_ref[rows, cols].astype(F32)
            for lag in range(1, 4):
                mixed = mixed + weights[lag : lag + 1, cols] * moved[:, lag - 1].reshape(CHUNK, 256)
            act_ref[rows, cols] = (mixed + mixed * jnp.tanh(mixed)).astype(BF16)

    def finish(slot, _):
        end = meta[1 + slot]
        start = jnp.where(slot > 0, meta[jnp.maximum(slot, 1)], meta[0])
        low = pl.multiple_of((end - 1 - first) // CHUNK * CHUNK, CHUNK)
        begin = first + low
        target = meta[5 + slot]
        tail = jnp.zeros((TAIL, 128), F32)
        row = iota((TAIL, CHUNK), 0)
        col = iota((TAIL, CHUNK), 1) + begin
        row16 = iota((TAIL, 16), 0)
        col16 = iota((TAIL, 16), 1) + begin - 16
        before = pl.multiple_of(jnp.maximum(low - 16, 0), 16)
        for tile in range(x_ref.shape[1] // 128):
            cols = slice(tile * 128, tile * 128 + 128)
            mine = (row >= 3 * tile) & (row < 3 * tile + 3)
            pick = (col == end - 3 + row - 3 * tile) & (col >= start) & mine
            mine16 = (row16 >= 3 * tile) & (row16 < 3 * tile + 3)
            pick16 = (col16 == end - 3 + row16 - 3 * tile) & (col16 >= start) & mine16
            rim = jnp.where(low > 0, x_ref[pl.ds(before, 16), cols].astype(F32), edge16[:, cols].astype(F32))
            tail = tail + jnp.dot(
                pick.astype(F32).astype(BF16), x_ref[pl.ds(low, CHUNK), cols], preferred_element_type=F32
            ) + jnp.dot(
                pick16.astype(F32).astype(BF16), rim.astype(BF16), preferred_element_type=F32
            )

        @pl.when(target >= 0)
        def _():
            tail_ref[target] = tail.astype(BF16)

        return 0

    lax.fori_loop(*ended(meta, first), finish, 0)
    edge16[...] = x_ref[BLOCK - 16 :, :]


def ended(meta, first):
    done = jnp.int32(0)
    upto = jnp.int32(0)
    for slot in range(EMAX):
        done = done + (meta[1 + slot] <= first).astype(jnp.int32)
        upto = upto + (meta[1 + slot] <= first + BLOCK).astype(jnp.int32)
    return done, upto


def states_kernel(
    meta, act_ref, dt_ref, ld_ref, rep_ref, rep16_ref, tri_ref, tail_ref,
    cum_ref, carry_ref, sin_ref, pay_ref, fin_ref, first_ref,
    state, total, totals,
):
    step = pl.program_id(0)
    heads = dt_ref.shape[0]
    width = rep_ref.shape[1]
    span = pl.num_programs(0) * BLOCK
    parts = BLOCK // CHUNK
    first = step * BLOCK

    @pl.when(step == 0)
    def _():
        state[...] = jnp.zeros_like(state)
        total[...] = jnp.zeros_like(total)
        fin_ref[:, :width] = jnp.zeros_like(fin_ref[:, :width])
        fin_ref[:, width:] = tail_ref[...]
        first_ref[...] = jnp.zeros_like(first_ref)

    running = total[...]
    for part in range(parts):
        low = part * CHUNK
        rows = slice(low, low + CHUNK)
        begin = first + low
        summed = jnp.dot(
            thirds(ld_ref[:, rows] * LOG2E), tri_ref[...], preferred_element_type=F32
        )
        cum = summed[:heads] + summed[heads : 2 * heads] + summed[2 * heads :]
        cum_ref[:, rows] = cum
        lane = iota((heads, CHUNK), 1) + begin
        open_end = jnp.where(meta[0] < 0, meta[1], -1)
        carry_ref[:, rows] = jnp.where(lane < open_end, jnp.exp2(running + cum), 0.0)
        totals[part] = running
        start = last_start(meta, begin + CHUNK - 1)
        last = cum[:, CHUNK - 1 :]
        weight = jnp.where(lane >= start, jnp.exp2(last - cum) * dt_ref[:, rows], 0.0)
        weight = weight.T.astype(BF16)
        through = spread_row(jnp.where(start < begin, jnp.exp2(last), 0.0), rep_ref[...])
        b_turned = act_ref[rows, width : width + N].T
        for tile in range(width // 256):
            cols = slice(tile * 256, tile * 256 + 256)
            held = state[:, cols]
            sin_ref[part, :, cols] = held.astype(BF16)
            scale = jnp.dot(weight, rep16_ref[:heads, cols], preferred_element_type=F32)
            load = scale.astype(BF16) * act_ref[rows, cols]
            grown = jnp.dot(b_turned, load, preferred_element_type=F32)
            state[:, cols] = through[:, cols] * held + grown
        running = running + last
    total[...] = running

    def finish(slot, _):
        end = meta[1 + slot]
        start = jnp.where(slot > 0, meta[jnp.maximum(slot, 1)], meta[0])
        part = (end - 1 - first) // CHUNK
        low = pl.multiple_of(part * CHUNK, CHUNK)
        begin = first + low
        lane = iota((heads, CHUNK), 1) + begin
        cum = cum_ref[:, pl.ds(low, CHUNK)]
        at_end = jnp.sum(jnp.where(lane == end - 1, cum, 0.0), axis=1, keepdims=True)
        inside = (lane < end) & (lane >= start)
        weight = jnp.exp2(jnp.minimum(at_end - cum, 0.0)) * dt_ref[:, pl.ds(low, CHUNK)]
        weight = jnp.where(inside, weight, 0.0).T.astype(BF16)
        scale = jnp.dot(weight, rep16_ref[:heads], preferred_element_type=F32)
        load = scale.astype(BF16) * act_ref[pl.ds(low, CHUNK), :width]
        local = outer_dot(act_ref[pl.ds(low, CHUNK), width : width + N], load)
        through = spread_row(jnp.where(start < begin, jnp.exp2(at_end), 0.0), rep_ref[...])
        final = local + through * sin_ref[part].astype(F32)
        target = meta[5 + slot]
        opened = jnp.where(start < 0, jnp.exp2(totals[part][:, :1] + at_end), 0.0)

        @pl.when(slot == 0)
        def _():
            first_ref[...] = jnp.broadcast_to(spread_row(opened, rep_ref[...]), first_ref.shape)

        @pl.when(target >= 0)
        def _():
            fin_ref[target, :width] = final.T.astype(BF16)

        return 0

    lax.fori_loop(*ended(meta, first), finish, 0)

    @pl.when(step == pl.num_programs(0) - 1)
    def _():
        start = last_start(meta, span - 1)
        gate = spread_row(jnp.where(start < 0, jnp.exp2(total[:, :1]), 0.0), rep_ref[...])
        gate = jnp.broadcast_to(gate, (PAY - N, width))
        high = gate.astype(BF16).astype(F32)
        pay_ref[:N] = state[...].astype(BF16)
        pay_ref[N:] = jnp.where(iota((PAY - N, width), 0) == 0, high, gate - high).astype(BF16)


def output_kernel(origin, held, meta, act_ref, dt_ref, cum_ref, sin_ref, gain_ref, rep16_ref, *refs):
    out_ref = refs[held]
    step = origin + pl.program_id(0)
    heads = dt_ref.shape[0]
    width = out_ref.shape[1]
    parts = BLOCK // CHUNK
    for part in range(parts):
        begin = step * BLOCK + part * CHUNK
        rows = slice(part * CHUNK, part * CHUNK + CHUNK)
        cum = cum_ref[:, rows]
        back = cum - jnp.log2(dt_ref[:, rows])
        ahead = cum.T
        b_act = act_ref[rows, width : width + N]
        c_act = act_ref[rows, width + N : width + 2 * N]
        place = iota((CHUNK, CHUNK), 0) + begin
        other = iota((CHUNK, CHUNK), 1) + begin
        scores = lax.dot_general(c_act, b_act, (((1,), (1,)), ((), ())), preferred_element_type=F32)
        scores = jnp.where((other <= place) & (other >= starts_of(meta, place)), scores, 0.0)
        lane = iota((heads, CHUNK), 1) + begin
        before = jnp.where(last_start(meta, begin) < begin, next_end(meta, begin), -1)
        entry = jnp.where(lane < before, jnp.exp2(cum), 0.0)
        entry = jnp.concatenate([entry, entry - entry.astype(BF16).astype(F32)], axis=0).T.astype(BF16)
        left_half = iota((CHUNK, 128), 1) < P_SIZE
        for quad in range(heads // 4):
            cols = slice(quad * 256, quad * 256 + 256)
            outer = jnp.dot(c_act, sin_ref[part, :, cols], preferred_element_type=F32)
            scale = jnp.dot(entry, rep16_ref[:, cols], preferred_element_type=F32)
            sums = []
            for pair in (2 * quad, 2 * quad + 1):
                mixes = []
                for head in (2 * pair, 2 * pair + 1):
                    spread = jnp.minimum(ahead[:, head : head + 1] - back[head : head + 1, :], 0.0)
                    mixes.append((jnp.exp2(spread) * scores).astype(BF16))
                x_pair = act_ref[rows, pair * 128 : pair * 128 + 128]
                zero = jnp.zeros_like(x_pair)
                split = jnp.concatenate(
                    [jnp.where(left_half, x_pair, zero), jnp.where(left_half, zero, x_pair)], axis=0
                )
                sums.append(
                    jnp.dot(jnp.concatenate(mixes, axis=1), split, preferred_element_type=F32)
                )
            inner = jnp.concatenate(sums, axis=1)
            value = inner + scale * outer + gain_ref[:, cols] * act_ref[rows, cols].astype(F32)
            out_ref[rows, cols] = value.astype(BF16)


def gates_of(pay_ref, cols):
    gates = pay_ref[N:, cols].astype(F32)
    return gates[0:1] + gates[1:2]


def pair_kernel(shard_ref, own_ref, got_ref, half_ref):
    side = half_ref.shape[1]

    def join(early, late, cols):
        after = gates_of(late, cols)
        gate = jnp.broadcast_to(after * gates_of(early, cols), (PAY - N, side))
        high = gate.astype(BF16).astype(F32)
        half_ref[:N] = (late[:N, cols].astype(F32) + after * early[:N, cols].astype(F32)).astype(BF16)
        half_ref[N:] = jnp.where(iota((PAY - N, side), 0) == 0, high, gate - high).astype(BF16)

    @pl.when(shard_ref[0] % 2 == 0)
    def _():
        join(own_ref, got_ref, slice(0, side))

    @pl.when(shard_ref[0] % 2 == 1)
    def _():
        join(got_ref, own_ref, slice(side, 2 * side))


def prefix_kernel(*refs):
    prefix_ref = refs[-1]
    side = prefix_ref.shape[1]
    total = jnp.zeros((N, side), F32)
    for ref in refs[:-1]:
        total = gates_of(ref, slice(0, side)) * total + ref[:N].astype(F32)
    prefix_ref[...] = total.astype(BF16)


def carry_kernel(shard_ref, stream_ref, meta, mine_ref, other_ref, early_ref, first_ref, carried_ref, *sends):
    side = mine_ref.shape[1]
    lower, upper = slice(0, side), slice(side, 2 * side)

    @pl.when(shard_ref[0] % 2 == 0)
    def _():
        carried_ref[:, lower] = mine_ref[...]
        carried_ref[:, upper] = other_ref[...]

    @pl.when(shard_ref[0] % 2 == 1)
    def _():
        for cols, part in ((lower, other_ref), (upper, mine_ref)):
            carried_ref[:, cols] = (
                early_ref[:N, cols].astype(F32) + gates_of(early_ref, cols) * part[...].astype(F32)
            ).astype(BF16)

    value = (first_ref[0:1] * carried_ref[...].astype(F32)).T.astype(BF16)
    apart = (meta[5] // CAP) ^ stream_ref[0]
    for index, ref in enumerate(sends):
        ref[...] = jnp.where(apart == index, value, jnp.zeros_like(value))


def correct_kernel(meta, base_ref, c_ref, carry_ref, carried_ref, rep16_ref, out_ref):
    width = out_ref.shape[1]
    touched = (meta[0] < 0) & (meta[1] > pl.program_id(0) * BLOCK)

    @pl.when(touched)
    def _():
        entry = carry_ref[...]
        entry = jnp.concatenate([entry, entry - entry.astype(BF16).astype(F32)], axis=0).T.astype(BF16)
        for tile in range(width // 256):
            cols = slice(tile * 256, tile * 256 + 256)
            outer = jnp.dot(c_ref[...], carried_ref[:, cols], preferred_element_type=F32)
            scale = jnp.dot(entry, rep16_ref[:, cols], preferred_element_type=F32)
            out_ref[:, cols] = (base_ref[:, cols].astype(F32) + scale * outer).astype(BF16)

    @pl.when(jnp.logical_not(touched))
    def _():
        out_ref[...] = base_ref[...]


def params(mib):
    return pltpu.CompilerParams(vmem_limit_bytes=mib * MIB)


def whole(shape):
    return pl.BlockSpec(shape, lambda *_: (0,) * len(shape))


def on_device(
    conv_input, conv_weight, conv_bias, step_size, log_decay, skip_gain, doc_bounds, doc_owner
):
    span, channels = conv_input.shape[1:]
    heads = step_size.shape[1]
    width = heads * P_SIZE
    steps = span // BLOCK
    chunks = span // CHUNK
    owners = lax.axis_size("stream")
    slots = owners * CAP
    rows = width + TAIL
    shard = lax.axis_index("seq").astype(jnp.int32).reshape(1)
    rows_in = conv_input[0]
    rim = shifted(rows_in[span - 16 :], "seq", 1)
    rep = (np.arange(width)[None, :] // P_SIZE == np.arange(heads)[:, None]).astype(np.float32)
    rep16 = np.concatenate([rep, rep], 0).astype(BF16)
    ticks = np.arange(CHUNK)
    tri = (ticks[:, None] <= ticks[None, :]).astype(BF16)
    order = np.arange(3 * CHUNK)
    tick, lag = 8 * (order // 24) + order % 8, order % 24 // 8 + 1
    source = np.arange(CHUNK + 16)
    move = (source[None, :] - 16 == (tick - lag)[:, None]).astype(BF16)
    slot = np.broadcast_to((4 * tick + lag)[:, None], (3 * CHUNK, 128)).astype(np.int32)
    smem = pl.BlockSpec(memory_space=pltpu.SMEM)
    stream = lax.axis_index("stream").astype(jnp.int32).reshape(1)
    per_head = pl.BlockSpec((heads, BLOCK), lambda i, *_: (0, i))
    prefetch = functools.partial(pltpu.PrefetchScalarGridSpec, num_scalar_prefetch=1)
    by_rows = pl.BlockSpec((BLOCK, channels), lambda i, *_: (i, 0))
    act, tails, meta = pl.pallas_call(
        conv_kernel,
        grid=(steps,),
        in_specs=[
            smem, smem, smem, by_rows, whole((16, channels)),
            whole((4, channels)), whole((1, channels)), whole(move.shape), whole(slot.shape),
        ],
        out_specs=[by_rows, whole((slots, TAIL, N)), smem],
        out_shape=[
            jax.ShapeDtypeStruct((span, channels), BF16),
            jax.ShapeDtypeStruct((slots, TAIL, N), BF16),
            jax.ShapeDtypeStruct((16,), jnp.int32),
        ],
        scratch_shapes=[
            pltpu.VMEM((16, channels), BF16),
            pltpu.VMEM((8, channels), F32),
            pltpu.VMEM((1 + BLOCK // CHUNK,) + move.shape, BF16),
            pltpu.SMEM((owners,), jnp.int32),
        ],
        compiler_params=params(48),
        cost_estimate=pl.CostEstimate(
            flops=2 * span * channels * 400, bytes_accessed=21 << 20, transcendentals=span * channels
        ),
        name="conv",
    )(shard, doc_bounds, doc_owner, rows_in, rim, conv_weight, conv_bias[None], move, slot)
    cum, carry, sin, pay, fin, first = pl.pallas_call(
        states_kernel,
        grid_spec=prefetch(
            grid=(steps,),
            in_specs=[
                by_rows, per_head, per_head,
                whole((heads, width)), whole((2 * heads, width)), whole((CHUNK, CHUNK)),
                whole((slots, TAIL, N)),
            ],
            out_specs=[
                per_head, per_head,
                pl.BlockSpec((BLOCK // CHUNK, N, width), lambda i, *_: (i, 0, 0)),
                whole((PAY, width)), whole((slots, rows, N)), whole((8, width)),
            ],
            scratch_shapes=[
                pltpu.VMEM((N, width), F32),
                pltpu.VMEM((heads, CHUNK), F32),
                pltpu.VMEM((BLOCK // CHUNK, heads, CHUNK), F32),
            ],
        ),
        out_shape=[
            jax.ShapeDtypeStruct((heads, span), F32),
            jax.ShapeDtypeStruct((heads, span), F32),
            jax.ShapeDtypeStruct((chunks, N, width), BF16),
            jax.ShapeDtypeStruct((PAY, width), BF16),
            jax.ShapeDtypeStruct((slots, rows, N), BF16),
            jax.ShapeDtypeStruct((8, width), F32),
        ],
        compiler_params=params(48),
        cost_estimate=pl.CostEstimate(
            flops=2 * span * width * N * 2, bytes_accessed=22 << 20, transcendentals=span * heads
        ),
        name="states",
    )(meta, act, step_size[0], log_decay[0], rep, rep16, tri, tails)

    gain = jnp.repeat(skip_gain, P_SIZE)[None]

    def outputs(first, last, base):
        hold = [] if base is None else [base]
        return pl.pallas_call(
            functools.partial(output_kernel, first, bool(hold)),
            grid_spec=prefetch(
                grid=(last - first,),
                in_specs=[
                    pl.BlockSpec((BLOCK, channels), lambda i, *_: (first + i, 0)),
                    pl.BlockSpec((heads, BLOCK), lambda i, *_: (0, first + i)),
                    pl.BlockSpec((heads, BLOCK), lambda i, *_: (0, first + i)),
                    pl.BlockSpec((BLOCK // CHUNK, N, width), lambda i, *_: (first + i, 0, 0)),
                    whole((1, width)), whole((2 * heads, width)),
                ] + [pl.BlockSpec(memory_space=pl.ANY)] * len(hold),
                out_specs=pl.BlockSpec((BLOCK, width), lambda i, *_: (first + i, 0)),
            ),
            out_shape=jax.ShapeDtypeStruct((span, width), BF16),
            input_output_aliases={7: 0} if hold else {},
            compiler_params=params(48),
            cost_estimate=pl.CostEstimate(
                flops=2 * (last - first) * BLOCK * width * N * 4,
                bytes_accessed=(last - first) * (4 << 20),
                transcendentals=(last - first) * BLOCK * CHUNK * heads,
            ),
            name="outputs",
        )(meta, act, step_size[0], cum, sin, gain, rep16, *hold)

    side = width // 2
    count = lax.axis_size("seq")
    pairs = [(index, index ^ 1) for index in range(count)]
    early = lax.ppermute(pay, "seq", pairs)
    base = outputs(0, 1, None)
    early, base = lax.optimization_barrier((early, base))
    half = pl.pallas_call(
        pair_kernel,
        in_specs=[smem, whole((PAY, width)), whole((PAY, width))],
        out_specs=whole((PAY, side)),
        out_shape=jax.ShapeDtypeStruct((PAY, side), BF16),
        compiler_params=params(48),
        name="pair",
    )(shard, pay, early)
    half, fin = lax.optimization_barrier((half, fin))
    chips = count // 2
    behind = [shifted(half, "seq", 2 * far) for far in range(chips - 1, 0, -1)]
    got = lax.all_to_all(
        fin.reshape(owners, CAP, rows, N), "stream", split_axis=0, concat_axis=0, tiled=True
    )
    base = outputs(1, steps - 2, base)
    *behind, base = lax.optimization_barrier((*behind, base))
    mine = pl.pallas_call(
        prefix_kernel,
        in_specs=[whole((PAY, side))] * len(behind),
        out_specs=whole((N, side)),
        out_shape=jax.ShapeDtypeStruct((N, side), BF16),
        compiler_params=params(48),
        name="prefix",
    )(*behind)
    other = lax.ppermute(mine, "seq", pairs)
    base = outputs(steps - 2, steps, base)
    other, base, got = lax.optimization_barrier((other, base, got))
    carried, *send = pl.pallas_call(
        carry_kernel,
        in_specs=[smem, smem, smem, whole((N, side)), whole((N, side)), whole((PAY, width)), whole((8, width))],
        out_specs=[whole((N, width))] + [whole((width, N))] * owners,
        out_shape=[jax.ShapeDtypeStruct((N, width), BF16)]
        + [jax.ShapeDtypeStruct((width, N), BF16)] * owners,
        compiler_params=params(48),
        name="carry",
    )(shard, stream, meta, mine, other, early, first)
    more = [send[0]]
    for apart in range(1, owners):
        swap = [(index, index ^ apart) for index in range(owners)]
        more.append(lax.ppermute(send[apart], "stream", swap))

    out = pl.pallas_call(
        correct_kernel,
        grid_spec=prefetch(
            grid=(steps,),
            in_specs=[
                pl.BlockSpec((BLOCK, width), lambda i, *_: (i, 0)),
                pl.BlockSpec((BLOCK, N), lambda i, *_: (i, width // N + 1)),
                per_head,
                whole((N, width)), whole((2 * heads, width)),
            ],
            out_specs=pl.BlockSpec((BLOCK, width), lambda i, *_: (i, 0)),
        ),
        out_shape=jax.ShapeDtypeStruct((span, width), BF16),
        input_output_aliases={1: 0},
        compiler_params=params(48),
        cost_estimate=pl.CostEstimate(
            flops=2 * span * width * N, bytes_accessed=18 << 20, transcendentals=0
        ),
        name="correct",
    )(meta, base, act, carry, carried, rep16)

    apart = (jnp.arange(owners) ^ stream)[:, None, None]
    extra = jnp.zeros((owners, width, N), F32)
    for index in range(owners):
        extra = jnp.where(apart == index, more[index][None].astype(F32), extra)
    ranks = jnp.arange(CAP)[None, :, None, None]
    ssm = got[:, :, :width].astype(F32) + jnp.where(ranks == 0, extra[:, None], 0.0)
    ssm = ssm.reshape(1, 1, owners, CAP, heads, P_SIZE, N)
    tiles = channels // N
    conv = got[:, :, width : width + 3 * tiles].reshape(owners, CAP, tiles, 3, N)
    conv = conv.transpose(0, 1, 3, 2, 4).reshape(1, 1, owners, CAP, 3, channels)
    return out[None], ssm, conv


def solution(mesh):
    in_specs = (
        P("stream", "seq", None),
        P(),
        P(),
        P("stream", None, "seq"),
        P("stream", None, "seq"),
        P(),
        P("stream", None),
        P("stream", None),
    )
    out_specs = (
        P("stream", "seq", None),
        P("stream", "seq", None, None, None, None, None),
        P("stream", "seq", None, None, None, None),
    )
    return jax.shard_map(
        on_device, mesh=mesh, in_specs=in_specs, out_specs=out_specs, check_vma=False
    )
```

```python
import functools

import jax
import jax.numpy as jnp
import numpy as np
from jax import lax
from jax.experimental import pallas as pl
from jax.experimental.pallas import tpu as pltpu
from jax.sharding import PartitionSpec as P

P_SIZE = 64
N = 128
EMAX = 4
CAP = 2
CHUNK = 128
BLOCK = 512
FAR = 1 << 30
LOG2E = 1.4426950408889634
PAY = 144
TAIL = 32
MIB = 1024 * 1024

F32 = jnp.float32
BF16 = jnp.bfloat16


def shifted(value, axis, steps):
    count = lax.axis_size(axis)
    leading, last = (max(0, -steps), min(count, count - steps))
    return lax.ppermute(value, axis, [(source, source + steps) for source in range(leading, last)])


def iota(shape, axis):
    return lax.broadcasted_iota(jnp.int32, shape, axis)


def outer_dot(left, right):
    return lax.dot_general(left, right, (((0,), (0,)), ((), ())), preferred_element_type=F32)


def halves(value):
    high = value.astype(BF16)
    low = (value - high.astype(F32)).astype(BF16)
    return jnp.concatenate([high, low], axis=0)


def thirds(value):
    high = value.astype(BF16)
    rest = value - high.astype(F32)
    mid = rest.astype(BF16)
    low = (rest - mid.astype(F32)).astype(BF16)
    return jnp.concatenate([high, mid, low], axis=0)


def spread_row(column, rep):
    return jnp.sum(rep * column, axis=0, keepdims=True)


def last_start(meta, place):
    start = meta[0]
    for slot in range(EMAX):
        end = meta[1 + slot]
        start = jnp.where(end <= place, end, start)
    return start


def next_end(meta, place):
    end = FAR
    for slot in reversed(range(EMAX)):
        end = jnp.where(meta[1 + slot] > place, meta[1 + slot], end)
    return end


def starts_of(meta, rows):
    start = jnp.full(rows.shape, meta[0], jnp.int32)
    for slot in range(EMAX):
        end = meta[1 + slot]
        start = jnp.where(rows >= end, end, start)
    return start


def read_docs(bounds, owners, meta, count, anchor, span):
    for slot in range(EMAX):
        meta[1 + slot] = FAR
        meta[5 + slot] = 0
    for owner in range(count.shape[0]):
        count[owner] = 0

    def one(index, carry):
        found, prior, start = carry
        end = bounds[0, index]
        owner = owners[0, index]
        mine = (end > prior) & (end > anchor) & (end <= anchor + span) & (found < EMAX)

        @pl.when(mine)
        def _():
            meta[1 + found] = end - anchor
            rank = count[owner]
            meta[5 + found] = jnp.where(rank < CAP, owner * CAP + rank, -1)
            count[owner] = rank + 1

        return found + mine.astype(jnp.int32), end, jnp.where(end <= anchor, end, start)

    zero = jnp.int32(0)
    _, _, start = lax.fori_loop(0, bounds.shape[1], one, (zero, zero, zero))
    meta[0] = start - anchor


def conv_kernel(
    shard_ref, bounds, owners, x_ref, rim_ref, w_ref, bias_ref, move_ref, slot_ref,
    act_ref, rest_ref, tail_ref, meta,
    edge16, weights, moves, count,
):
    step = pl.program_id(0)
    span = pl.num_programs(0) * BLOCK
    parts = BLOCK // CHUNK
    first = step * BLOCK

    @pl.when(step == 0)
    def _():
        read_docs(bounds, owners, meta, count, shard_ref[0] * span, span)
        tail_ref[...] = jnp.zeros_like(tail_ref)
        edge16[...] = rim_ref[...]
        weights[0:4] = 0.5 * w_ref[...]
        weights[4:5] = 0.5 * bias_ref[...]
        moves[0] = move_ref[...]

    choices = []
    for part in range(parts):
        begin = first + part * CHUNK
        near = (meta[0] > begin - 3) & (meta[0] < begin + CHUNK)
        for slot in range(EMAX):
            near = near | ((meta[1 + slot] > begin - 3) & (meta[1 + slot] < begin + CHUNK))

        @pl.when(near)
        def _():
            tick = slot_ref[...] // 4 + begin
            kept = (tick - starts_of(meta, tick) >= slot_ref[...] % 4).astype(F32)
            moves[1 + part, :, :128] = (kept * move_ref[:, :128].astype(F32)).astype(BF16)
            moves[1 + part, :, 128:] = (kept[:, :16] * move_ref[:, 128:].astype(F32)).astype(BF16)

        choices.append(jnp.where(near, 1 + part, 0))

    for part in range(parts):
        low = part * CHUNK
        rows = slice(low, low + CHUNK)
        pick = moves[choices[part]]
        for tile in range(x_ref.shape[1] // 256):
            cols = slice(tile * 256, tile * 256 + 256)
            if part:
                wide = x_ref[low - 16 : low + CHUNK, cols]
            else:
                wide = jnp.concatenate([edge16[:, cols], x_ref[rows, cols]], axis=0)
            moved = jnp.dot(pick, wide, preferred_element_type=F32)
            moved = moved.reshape(CHUNK // 8, 3, 8, 256)
            mixed = weights[4:5, cols] + weights[0:1, cols] * x_ref[rows, cols].astype(F32)
            for lag in range(1, 4):
                mixed = mixed + weights[lag : lag + 1, cols] * moved[:, lag - 1].reshape(CHUNK, 256)
            value = (mixed + mixed * jnp.tanh(mixed)).astype(BF16)
            if tile * 256 < act_ref.shape[1]:
                act_ref[rows, cols] = value
            else:
                rest_ref[rows, :] = value

    def finish(slot, _):
        end = meta[1 + slot]
        start = jnp.where(slot > 0, meta[jnp.maximum(slot, 1)], meta[0])
        low = pl.multiple_of((end - 1 - first) // CHUNK * CHUNK, CHUNK)
        begin = first + low
        target = meta[5 + slot]
        tail = jnp.zeros((TAIL, 128), F32)
        row = iota((TAIL, CHUNK), 0)
        col = iota((TAIL, CHUNK), 1) + begin
        row16 = iota((TAIL, 16), 0)
        col16 = iota((TAIL, 16), 1) + begin - 16
        before = pl.multiple_of(jnp.maximum(low - 16, 0), 16)
        for tile in range(x_ref.shape[1] // 128):
            cols = slice(tile * 128, tile * 128 + 128)
            mine = (row >= 3 * tile) & (row < 3 * tile + 3)
            pick = (col == end - 3 + row - 3 * tile) & (col >= start) & mine
            mine16 = (row16 >= 3 * tile) & (row16 < 3 * tile + 3)
            pick16 = (col16 == end - 3 + row16 - 3 * tile) & (col16 >= start) & mine16
            rim = jnp.where(low > 0, x_ref[pl.ds(before, 16), cols].astype(F32), edge16[:, cols].astype(F32))
            tail = tail + jnp.dot(
                pick.astype(F32).astype(BF16), x_ref[pl.ds(low, CHUNK), cols], preferred_element_type=F32
            ) + jnp.dot(
                pick16.astype(F32).astype(BF16), rim.astype(BF16), preferred_element_type=F32
            )

        @pl.when(target >= 0)
        def _():
            tail_ref[target] = tail.astype(BF16)

        return 0

    lax.fori_loop(*ended(meta, first), finish, 0)
    edge16[...] = x_ref[BLOCK - 16 :, :]


def ended(meta, first):
    done = jnp.int32(0)
    upto = jnp.int32(0)
    for slot in range(EMAX):
        done = done + (meta[1 + slot] <= first).astype(jnp.int32)
        upto = upto + (meta[1 + slot] <= first + BLOCK).astype(jnp.int32)
    return done, upto


def states_kernel(
    meta, act_ref, b_ref, dt_ref, ld_ref, rep_ref, rep16_ref, tri_ref, tail_ref,
    cum_ref, carry_ref, sin_ref, pay_ref, fin_ref, first_ref,
    state, total, totals,
):
    step = pl.program_id(0)
    heads = dt_ref.shape[0]
    width = rep_ref.shape[1]
    span = pl.num_programs(0) * BLOCK
    parts = BLOCK // CHUNK
    first = step * BLOCK

    @pl.when(step == 0)
    def _():
        state[...] = jnp.zeros_like(state)
        total[...] = jnp.zeros_like(total)
        fin_ref[:, :width] = jnp.zeros_like(fin_ref[:, :width])
        fin_ref[:, width:] = tail_ref[...]
        first_ref[...] = jnp.zeros_like(first_ref)

    spans = [slice(part * CHUNK, part * CHUNK + CHUNK) for part in range(parts)]
    pieces = jnp.concatenate([thirds(ld_ref[:, rows] * LOG2E) for rows in spans], axis=0)
    summed = jnp.dot(pieces, tri_ref[...], preferred_element_type=F32)
    open_end = jnp.where(meta[0] < 0, meta[1], -1)
    running = total[...]
    weights = []
    throughs = []
    for part, rows in enumerate(spans):
        begin = first + part * CHUNK
        at = 3 * heads * part
        cum = summed[at : at + heads] + summed[at + heads : at + 2 * heads] + summed[at + 2 * heads : at + 3 * heads]
        cum_ref[:, rows] = cum
        lane = iota((heads, CHUNK), 1) + begin
        carry_ref[:, rows] = jnp.where(lane < open_end, jnp.exp2(running + cum), 0.0)
        totals[part] = running
        start = last_start(meta, begin + CHUNK - 1)
        last = cum[:, CHUNK - 1 :]
        weight = jnp.where(lane >= start, jnp.exp2(last - cum) * dt_ref[:, rows], 0.0)
        weights.append(weight.T.astype(BF16))
        throughs.append(spread_row(jnp.where(start < begin, jnp.exp2(last), 0.0), rep_ref[...]))
        running = running + last
    total[...] = running
    weight = jnp.concatenate(weights, axis=0)
    turned = [b_ref[rows, :].T for rows in spans]
    for tile in range(width // 256):
        cols = slice(tile * 256, tile * 256 + 256)
        scale = jnp.dot(weight, rep16_ref[:heads, cols], preferred_element_type=F32)
        load = scale.astype(BF16) * act_ref[:, cols]
        held = state[:, cols]
        for part, rows in enumerate(spans):
            sin_ref[part, :, cols] = held.astype(BF16)
            grown = jnp.dot(turned[part], load[rows], preferred_element_type=F32)
            held = throughs[part][:, cols] * held + grown
        state[:, cols] = held

    def finish(slot, _):
        end = meta[1 + slot]
        start = jnp.where(slot > 0, meta[jnp.maximum(slot, 1)], meta[0])
        part = (end - 1 - first) // CHUNK
        low = pl.multiple_of(part * CHUNK, CHUNK)
        begin = first + low
        lane = iota((heads, CHUNK), 1) + begin
        cum = cum_ref[:, pl.ds(low, CHUNK)]
        at_end = jnp.sum(jnp.where(lane == end - 1, cum, 0.0), axis=1, keepdims=True)
        inside = (lane < end) & (lane >= start)
        weight = jnp.exp2(jnp.minimum(at_end - cum, 0.0)) * dt_ref[:, pl.ds(low, CHUNK)]
        weight = jnp.where(inside, weight, 0.0).T.astype(BF16)
        scale = jnp.dot(weight, rep16_ref[:heads], preferred_element_type=F32)
        load = scale.astype(BF16) * act_ref[pl.ds(low, CHUNK), :]
        local = outer_dot(b_ref[pl.ds(low, CHUNK), :], load)
        through = spread_row(jnp.where(start < begin, jnp.exp2(at_end), 0.0), rep_ref[...])
        final = local + through * sin_ref[part].astype(F32)
        target = meta[5 + slot]
        opened = jnp.where(start < 0, jnp.exp2(totals[part][:, :1] + at_end), 0.0)

        @pl.when(slot == 0)
        def _():
            first_ref[...] = jnp.broadcast_to(spread_row(opened, rep_ref[...]), first_ref.shape)

        @pl.when(target >= 0)
        def _():
            fin_ref[target, :width] = final.T.astype(BF16)

        return 0

    lax.fori_loop(*ended(meta, first), finish, 0)

    @pl.when(step == pl.num_programs(0) - 1)
    def _():
        start = last_start(meta, span - 1)
        gate = spread_row(jnp.where(start < 0, jnp.exp2(total[:, :1]), 0.0), rep_ref[...])
        gate = jnp.broadcast_to(gate, (PAY - N, width))
        high = gate.astype(BF16).astype(F32)
        pay_ref[:N] = state[...].astype(BF16)
        pay_ref[N:] = jnp.where(iota((PAY - N, width), 0) == 0, high, gate - high).astype(BF16)


def output_kernel(origin, late, meta, act_ref, rest_ref, dt_ref, cum_ref, sin_ref, gain_ref, rep16_ref, *refs):
    out_ref = refs[-1]
    step = origin + pl.program_id(0)
    heads = dt_ref.shape[0]
    width = out_ref.shape[1]
    parts = BLOCK // CHUNK
    for part in range(parts):
        begin = step * BLOCK + part * CHUNK
        rows = slice(part * CHUNK, part * CHUNK + CHUNK)
        cum = cum_ref[:, rows]
        back = cum - jnp.log2(dt_ref[:, rows])
        ahead = cum.T
        b_act = rest_ref[rows, :N]
        c_act = rest_ref[rows, N:]
        place = iota((CHUNK, CHUNK), 0) + begin
        other = iota((CHUNK, CHUNK), 1) + begin
        scores = lax.dot_general(c_act, b_act, (((1,), (1,)), ((), ())), preferred_element_type=F32)
        scores = jnp.where((other <= place) & (other >= starts_of(meta, place)), scores, 0.0)
        lane = iota((heads, CHUNK), 1) + begin
        before = jnp.where(last_start(meta, begin) < begin, next_end(meta, begin), -1)
        entry = jnp.where(lane < before, jnp.exp2(cum), 0.0)
        entry = jnp.concatenate([entry, entry - entry.astype(BF16).astype(F32)], axis=0).T.astype(BF16)
        if late:
            extra = refs[0][:, rows]
            extra = jnp.concatenate([extra, extra - extra.astype(BF16).astype(F32)], axis=0).T.astype(BF16)
        left_half = iota((CHUNK, 128), 1) < P_SIZE
        for quad in range(heads // 4):
            cols = slice(quad * 256, quad * 256 + 256)
            outer = jnp.dot(c_act, sin_ref[part, :, cols], preferred_element_type=F32)
            scale = jnp.dot(entry, rep16_ref[:, cols], preferred_element_type=F32)
            sums = []
            for pair in (2 * quad, 2 * quad + 1):
                mixes = []
                for head in (2 * pair, 2 * pair + 1):
                    spread = jnp.minimum(ahead[:, head : head + 1] - back[head : head + 1, :], 0.0)
                    mixes.append((jnp.exp2(spread) * scores).astype(BF16))
                x_pair = act_ref[rows, pair * 128 : pair * 128 + 128]
                zero = jnp.zeros_like(x_pair)
                split = jnp.concatenate(
                    [jnp.where(left_half, x_pair, zero), jnp.where(left_half, zero, x_pair)], axis=0
                )
                sums.append(
                    jnp.dot(jnp.concatenate(mixes, axis=1), split, preferred_element_type=F32)
                )
            inner = jnp.concatenate(sums, axis=1)
            value = inner + scale * outer + gain_ref[:, cols] * act_ref[rows, cols].astype(F32)
            if late:
                outer = jnp.dot(c_act, refs[1][:, cols], preferred_element_type=F32)
                scale = jnp.dot(extra, rep16_ref[:, cols], preferred_element_type=F32)
                value = value + scale * outer
            out_ref[rows, cols] = value.astype(BF16)


def gates_of(pay_ref, cols):
    gates = pay_ref[N:, cols].astype(F32)
    return gates[0:1] + gates[1:2]


def pair_kernel(shard_ref, own_ref, got_ref, half_ref):
    side = half_ref.shape[1]

    def join(early, late, cols):
        after = gates_of(late, cols)
        gate = jnp.broadcast_to(after * gates_of(early, cols), (PAY - N, side))
        high = gate.astype(BF16).astype(F32)
        half_ref[:N] = (late[:N, cols].astype(F32) + after * early[:N, cols].astype(F32)).astype(BF16)
        half_ref[N:] = jnp.where(iota((PAY - N, side), 0) == 0, high, gate - high).astype(BF16)

    @pl.when(shard_ref[0] % 2 == 0)
    def _():
        join(own_ref, got_ref, slice(0, side))

    @pl.when(shard_ref[0] % 2 == 1)
    def _():
        join(got_ref, own_ref, slice(side, 2 * side))


def prefix_kernel(*refs):
    prefix_ref = refs[-1]
    side = prefix_ref.shape[1]
    total = jnp.zeros((N, side), F32)
    for ref in refs[:-1]:
        total = gates_of(ref, slice(0, side)) * total + ref[:N].astype(F32)
    prefix_ref[...] = total.astype(BF16)


def carry_kernel(shard_ref, stream_ref, meta, mine_ref, other_ref, early_ref, first_ref, carried_ref, *sends):
    side = mine_ref.shape[1]
    lower, upper = slice(0, side), slice(side, 2 * side)

    @pl.when(shard_ref[0] % 2 == 0)
    def _():
        carried_ref[:, lower] = mine_ref[...]
        carried_ref[:, upper] = other_ref[...]

    @pl.when(shard_ref[0] % 2 == 1)
    def _():
        for cols, part in ((lower, other_ref), (upper, mine_ref)):
            carried_ref[:, cols] = (
                early_ref[:N, cols].astype(F32) + gates_of(early_ref, cols) * part[...].astype(F32)
            ).astype(BF16)

    value = (first_ref[0:1] * carried_ref[...].astype(F32)).T.astype(BF16)
    apart = (meta[5] // CAP) ^ stream_ref[0]
    for index, ref in enumerate(sends):
        ref[...] = jnp.where(apart == index, value, jnp.zeros_like(value))


def correct_kernel(meta, base_ref, c_ref, carry_ref, carried_ref, rep16_ref, out_ref):
    width = out_ref.shape[1]
    touched = (meta[0] < 0) & (meta[1] > pl.program_id(0) * BLOCK)

    @pl.when(touched)
    def _():
        entry = carry_ref[...]
        entry = jnp.concatenate([entry, entry - entry.astype(BF16).astype(F32)], axis=0).T.astype(BF16)
        for tile in range(width // 256):
            cols = slice(tile * 256, tile * 256 + 256)
            outer = jnp.dot(c_ref[...], carried_ref[:, cols], preferred_element_type=F32)
            scale = jnp.dot(entry, rep16_ref[:, cols], preferred_element_type=F32)
            out_ref[:, cols] = (base_ref[:, cols].astype(F32) + scale * outer).astype(BF16)

    @pl.when(jnp.logical_not(touched))
    def _():
        out_ref[...] = base_ref[...]


def params(mib):
    return pltpu.CompilerParams(vmem_limit_bytes=mib * MIB)


def whole(shape):
    return pl.BlockSpec(shape, lambda *_: (0,) * len(shape))


def on_device(
    conv_input, conv_weight, conv_bias, step_size, log_decay, skip_gain, doc_bounds, doc_owner
):
    span, channels = conv_input.shape[1:]
    heads = step_size.shape[1]
    width = heads * P_SIZE
    steps = span // BLOCK
    chunks = span // CHUNK
    owners = lax.axis_size("stream")
    slots = owners * CAP
    rows = width + TAIL
    shard = lax.axis_index("seq").astype(jnp.int32).reshape(1)
    rows_in = conv_input[0]
    rim = shifted(rows_in[span - 16 :], "seq", 1)
    rep = (np.arange(width)[None, :] // P_SIZE == np.arange(heads)[:, None]).astype(np.float32)
    rep16 = np.concatenate([rep, rep], 0).astype(BF16)
    ticks = np.arange(CHUNK)
    tri = (ticks[:, None] <= ticks[None, :]).astype(BF16)
    order = np.arange(3 * CHUNK)
    tick, lag = 8 * (order // 24) + order % 8, order % 24 // 8 + 1
    source = np.arange(CHUNK + 16)
    move = (source[None, :] - 16 == (tick - lag)[:, None]).astype(BF16)
    slot = np.broadcast_to((4 * tick + lag)[:, None], (3 * CHUNK, 128)).astype(np.int32)
    smem = pl.BlockSpec(memory_space=pltpu.SMEM)
    stream = lax.axis_index("stream").astype(jnp.int32).reshape(1)
    per_head = pl.BlockSpec((heads, BLOCK), lambda i, *_: (0, i))
    prefetch = functools.partial(pltpu.PrefetchScalarGridSpec, num_scalar_prefetch=1)
    by_rows = pl.BlockSpec((BLOCK, channels), lambda i, *_: (i, 0))
    by_width = pl.BlockSpec((BLOCK, width), lambda i, *_: (i, 0))
    by_rest = pl.BlockSpec((BLOCK, 2 * N), lambda i, *_: (i, 0))
    act, rest, tails, meta = pl.pallas_call(
        conv_kernel,
        grid=(steps,),
        in_specs=[
            smem, smem, smem, by_rows, whole((16, channels)),
            whole((4, channels)), whole((1, channels)), whole(move.shape), whole(slot.shape),
        ],
        out_specs=[by_width, by_rest, whole((slots, TAIL, N)), smem],
        out_shape=[
            jax.ShapeDtypeStruct((span, width), BF16),
            jax.ShapeDtypeStruct((span, 2 * N), BF16),
            jax.ShapeDtypeStruct((slots, TAIL, N), BF16),
            jax.ShapeDtypeStruct((16,), jnp.int32),
        ],
        scratch_shapes=[
            pltpu.VMEM((16, channels), BF16),
            pltpu.VMEM((8, channels), F32),
            pltpu.VMEM((1 + BLOCK // CHUNK,) + move.shape, BF16),
            pltpu.SMEM((owners,), jnp.int32),
        ],
        compiler_params=params(60),
        cost_estimate=pl.CostEstimate(
            flops=2 * span * channels * 400, bytes_accessed=21 << 20, transcendentals=span * channels
        ),
        name="conv",
    )(shard, doc_bounds, doc_owner, rows_in, rim, conv_weight, conv_bias[None], move, slot)
    cum, carry, sin, pay, fin, first = pl.pallas_call(
        states_kernel,
        grid_spec=prefetch(
            grid=(steps,),
            in_specs=[
                by_width, pl.BlockSpec((BLOCK, N), lambda i, *_: (i, 0)), per_head, per_head,
                whole((heads, width)), whole((2 * heads, width)), whole((CHUNK, CHUNK)),
                whole((slots, TAIL, N)),
            ],
            out_specs=[
                per_head, per_head,
                pl.BlockSpec((BLOCK // CHUNK, N, width), lambda i, *_: (i, 0, 0)),
                whole((PAY, width)), whole((slots, rows, N)), whole((8, width)),
            ],
            scratch_shapes=[
                pltpu.VMEM((N, width), F32),
                pltpu.VMEM((heads, CHUNK), F32),
                pltpu.VMEM((BLOCK // CHUNK, heads, CHUNK), F32),
            ],
        ),
        out_shape=[
            jax.ShapeDtypeStruct((heads, span), F32),
            jax.ShapeDtypeStruct((heads, span), F32),
            jax.ShapeDtypeStruct((chunks, N, width), BF16),
            jax.ShapeDtypeStruct((PAY, width), BF16),
            jax.ShapeDtypeStruct((slots, rows, N), BF16),
            jax.ShapeDtypeStruct((8, width), F32),
        ],
        compiler_params=params(60),
        cost_estimate=pl.CostEstimate(
            flops=2 * span * width * N * 2, bytes_accessed=22 << 20, transcendentals=span * heads
        ),
        name="states",
    )(meta, act, rest, step_size[0], log_decay[0], rep, rep16, tri, tails)

    gain = jnp.repeat(skip_gain, P_SIZE)[None]

    def outputs(first, last, late=()):
        rows_of = functools.partial(pl.BlockSpec, index_map=lambda i, *_: (first + i, 0))
        heads_of = pl.BlockSpec((heads, BLOCK), lambda i, *_: (0, first + i))
        return pl.pallas_call(
            functools.partial(output_kernel, first, bool(late)),
            grid_spec=prefetch(
                grid=(last - first,),
                in_specs=[
                    rows_of((BLOCK, width)), rows_of((BLOCK, 2 * N)), heads_of, heads_of,
                    pl.BlockSpec((BLOCK // CHUNK, N, width), lambda i, *_: (first + i, 0, 0)),
                    whole((1, width)), whole((2 * heads, width)),
                ] + ([heads_of, whole((N, width)), pl.BlockSpec(memory_space=pl.ANY)] if late else []),
                out_specs=rows_of((BLOCK, width)),
            ),
            out_shape=jax.ShapeDtypeStruct((span, width), BF16),
            input_output_aliases={10: 0} if late else {},
            compiler_params=params(60),
            cost_estimate=pl.CostEstimate(
                flops=2 * (last - first) * BLOCK * width * N * 4,
                bytes_accessed=(last - first) * (4 << 20),
                transcendentals=(last - first) * BLOCK * CHUNK * heads,
            ),
            name="outputs",
        )(meta, act, rest, step_size[0], cum, sin, gain, rep16, *late)

    side = width // 2
    count = lax.axis_size("seq")
    pairs = [(index, index ^ 1) for index in range(count)]
    early = lax.ppermute(pay, "seq", pairs)
    got = lax.all_to_all(
        fin.reshape(owners, CAP, rows, N), "stream", split_axis=0, concat_axis=0, tiled=True
    )
    half = pl.pallas_call(
        pair_kernel,
        in_specs=[smem, whole((PAY, width)), whole((PAY, width))],
        out_specs=whole((PAY, side)),
        out_shape=jax.ShapeDtypeStruct((PAY, side), BF16),
        compiler_params=params(60),
        name="pair",
    )(shard, pay, early)
    chips = count // 2
    behind = [shifted(half, "seq", 2 * far) for far in range(chips - 1, 0, -1)]
    early_blocks = steps - 3
    base = outputs(0, early_blocks)
    *behind, base = lax.optimization_barrier((*behind, base))
    mine = pl.pallas_call(
        prefix_kernel,
        in_specs=[whole((PAY, side))] * len(behind),
        out_specs=whole((N, side)),
        out_shape=jax.ShapeDtypeStruct((N, side), BF16),
        compiler_params=params(60),
        name="prefix",
    )(*behind)
    other = lax.ppermute(mine, "seq", pairs)
    other, got = lax.optimization_barrier((other, got))
    carried, *send = pl.pallas_call(
        carry_kernel,
        in_specs=[smem, smem, smem, whole((N, side)), whole((N, side)), whole((PAY, width)), whole((8, width))],
        out_specs=[whole((N, width))] + [whole((width, N))] * owners,
        out_shape=[jax.ShapeDtypeStruct((N, width), BF16)]
        + [jax.ShapeDtypeStruct((width, N), BF16)] * owners,
        compiler_params=params(60),
        name="carry",
    )(shard, stream, meta, mine, other, early, first)
    more = [send[0]]
    for apart in range(1, owners):
        swap = [(index, index ^ apart) for index in range(owners)]
        more.append(lax.ppermute(send[apart], "stream", swap))

    base = outputs(early_blocks, steps, (carry, carried, base))
    out = pl.pallas_call(
        correct_kernel,
        grid_spec=prefetch(
            grid=(early_blocks,),
            in_specs=[
                pl.BlockSpec((BLOCK, width), lambda i, *_: (i, 0)),
                pl.BlockSpec((BLOCK, N), lambda i, *_: (i, 1)),
                per_head,
                whole((N, width)), whole((2 * heads, width)),
            ],
            out_specs=pl.BlockSpec((BLOCK, width), lambda i, *_: (i, 0)),
        ),
        out_shape=jax.ShapeDtypeStruct((span, width), BF16),
        input_output_aliases={1: 0},
        compiler_params=params(60),
        cost_estimate=pl.CostEstimate(
            flops=2 * span * width * N, bytes_accessed=18 << 20, transcendentals=0
        ),
        name="correct",
    )(meta, base, rest, carry, carried, rep16)

    apart = (jnp.arange(owners) ^ stream)[:, None, None]
    extra = jnp.zeros((owners, width, N), F32)
    for index in range(owners):
        extra = jnp.where(apart == index, more[index][None].astype(F32), extra)
    ranks = jnp.arange(CAP)[None, :, None, None]
    ssm = got[:, :, :width].astype(F32) + jnp.where(ranks == 0, extra[:, None], 0.0)
    ssm = ssm.reshape(1, 1, owners, CAP, heads, P_SIZE, N)
    tiles = channels // N
    conv = got[:, :, width : width + 3 * tiles].reshape(owners, CAP, tiles, 3, N)
    conv = conv.transpose(0, 1, 3, 2, 4).reshape(1, 1, owners, CAP, 3, channels)
    return out[None], ssm, conv


def solution(mesh):
    in_specs = (
        P("stream", "seq", None),
        P(),
        P(),
        P("stream", None, "seq"),
        P("stream", None, "seq"),
        P(),
        P("stream", None),
        P("stream", None),
    )
    out_specs = (
        P("stream", "seq", None),
        P("stream", "seq", None, None, None, None, None),
        P("stream", "seq", None, None, None, None),
    )
    return jax.shard_map(
        on_device, mesh=mesh, in_specs=in_specs, out_specs=out_specs, check_vma=False
    )
```

```python
import functools

import jax
import jax.numpy as jnp
import numpy as np
from jax import lax
from jax.experimental import pallas as pl
from jax.experimental.pallas import tpu as pltpu
from jax.sharding import PartitionSpec as P

P_SIZE = 64
N = 128
EMAX = 4
CAP = 2
CHUNK = 128
BLOCK = 512
FAR = 1 << 30
LOG2E = 1.4426950408889634
PAY = 144
TAIL = 32
MIB = 1024 * 1024

F32 = jnp.float32
BF16 = jnp.bfloat16


def shifted(value, axis, steps):
    count = lax.axis_size(axis)
    leading, last = (max(0, -steps), min(count, count - steps))
    return lax.ppermute(value, axis, [(source, source + steps) for source in range(leading, last)])


def iota(shape, axis):
    return lax.broadcasted_iota(jnp.int32, shape, axis)


def outer_dot(left, right):
    return lax.dot_general(left, right, (((0,), (0,)), ((), ())), preferred_element_type=F32)


def halves(value):
    high = value.astype(BF16)
    low = (value - high.astype(F32)).astype(BF16)
    return jnp.concatenate([high, low], axis=0)


def thirds(value):
    high = value.astype(BF16)
    rest = value - high.astype(F32)
    mid = rest.astype(BF16)
    low = (rest - mid.astype(F32)).astype(BF16)
    return jnp.concatenate([high, mid, low], axis=0)


def spread_row(column, rep):
    return jnp.sum(rep * column, axis=0, keepdims=True)


def last_start(meta, place):
    start = meta[0]
    for slot in range(EMAX):
        end = meta[1 + slot]
        start = jnp.where(end <= place, end, start)
    return start


def next_end(meta, place):
    end = FAR
    for slot in reversed(range(EMAX)):
        end = jnp.where(meta[1 + slot] > place, meta[1 + slot], end)
    return end


def starts_of(meta, rows):
    start = jnp.full(rows.shape, meta[0], jnp.int32)
    for slot in range(EMAX):
        end = meta[1 + slot]
        start = jnp.where(rows >= end, end, start)
    return start


def read_docs(bounds, owners, meta, count, anchor, span):
    for slot in range(EMAX):
        meta[1 + slot] = FAR
        meta[5 + slot] = 0
    for owner in range(count.shape[0]):
        count[owner] = 0

    def one(index, carry):
        found, prior, start = carry
        end = bounds[0, index]
        owner = owners[0, index]
        mine = (end > prior) & (end > anchor) & (end <= anchor + span) & (found < EMAX)

        @pl.when(mine)
        def _():
            meta[1 + found] = end - anchor
            rank = count[owner]
            meta[5 + found] = jnp.where(rank < CAP, owner * CAP + rank, -1)
            count[owner] = rank + 1

        return found + mine.astype(jnp.int32), end, jnp.where(end <= anchor, end, start)

    zero = jnp.int32(0)
    _, _, start = lax.fori_loop(0, bounds.shape[1], one, (zero, zero, zero))
    meta[0] = start - anchor


def conv_kernel(
    shard_ref, bounds, owners, x_ref, rim_ref, w_ref, bias_ref, move_ref, slot_ref,
    act_ref, rest_ref, tail_ref, meta,
    edge16, weights, moves, count,
):
    step = pl.program_id(0)
    span = pl.num_programs(0) * BLOCK
    parts = BLOCK // CHUNK
    first = step * BLOCK

    @pl.when(step == 0)
    def _():
        read_docs(bounds, owners, meta, count, shard_ref[0] * span, span)
        tail_ref[...] = jnp.zeros_like(tail_ref)
        edge16[...] = rim_ref[...]
        weights[0:4] = 0.5 * w_ref[...]
        weights[4:5] = 0.5 * bias_ref[...]
        moves[0] = move_ref[...]

    choices = []
    for part in range(parts):
        begin = first + part * CHUNK
        near = (meta[0] > begin - 3) & (meta[0] < begin + CHUNK)
        for slot in range(EMAX):
            near = near | ((meta[1 + slot] > begin - 3) & (meta[1 + slot] < begin + CHUNK))

        @pl.when(near)
        def _():
            tick = slot_ref[...] // 4 + begin
            kept = (tick - starts_of(meta, tick) >= slot_ref[...] % 4).astype(F32)
            moves[1 + part, :, :128] = (kept * move_ref[:, :128].astype(F32)).astype(BF16)
            moves[1 + part, :, 128:] = (kept[:, :16] * move_ref[:, 128:].astype(F32)).astype(BF16)

        choices.append(jnp.where(near, 1 + part, 0))

    for part in range(parts):
        low = part * CHUNK
        rows = slice(low, low + CHUNK)
        pick = moves[choices[part]]
        for tile in range(x_ref.shape[1] // 256):
            cols = slice(tile * 256, tile * 256 + 256)
            if part:
                wide = x_ref[low - 16 : low + CHUNK, cols]
            else:
                wide = jnp.concatenate([edge16[:, cols], x_ref[rows, cols]], axis=0)
            moved = jnp.dot(pick, wide, preferred_element_type=F32)
            moved = moved.reshape(CHUNK // 8, 3, 8, 256)
            mixed = weights[4:5, cols] + weights[0:1, cols] * x_ref[rows, cols].astype(F32)
            for lag in range(1, 4):
                mixed = mixed + weights[lag : lag + 1, cols] * moved[:, lag - 1].reshape(CHUNK, 256)
            value = (mixed + mixed * jnp.tanh(mixed)).astype(BF16)
            if tile * 256 < act_ref.shape[1]:
                act_ref[rows, cols] = value
            else:
                rest_ref[rows, :] = value

    def finish(slot, _):
        end = meta[1 + slot]
        start = jnp.where(slot > 0, meta[jnp.maximum(slot, 1)], meta[0])
        low = pl.multiple_of((end - 1 - first) // CHUNK * CHUNK, CHUNK)
        begin = first + low
        target = meta[5 + slot]
        row = iota((16, CHUNK), 0)
        col = iota((16, CHUNK), 1) + begin
        pick = (col == end - 3 + row) & (col >= start) & (row < 3)
        row16 = iota((16, 16), 0)
        col16 = iota((16, 16), 1) + begin - 16
        pick16 = (col16 == end - 3 + row16) & (col16 >= start) & (row16 < 3)
        before = pl.multiple_of(jnp.maximum(low - 16, 0), 16)
        rim = jnp.where(low > 0, x_ref[pl.ds(before, 16), :].astype(F32), edge16[...].astype(F32))
        last = jnp.dot(
            pick.astype(F32).astype(BF16), x_ref[pl.ds(low, CHUNK), :], preferred_element_type=F32
        ) + jnp.dot(pick16.astype(F32).astype(BF16), rim.astype(BF16), preferred_element_type=F32)
        tiles = x_ref.shape[1] // 128
        tail = jnp.concatenate(
            [last[:3, tile * 128 : tile * 128 + 128] for tile in range(tiles)]
            + [jnp.zeros((TAIL - 3 * tiles, 128), F32)],
            axis=0,
        )

        @pl.when(target >= 0)
        def _():
            tail_ref[target] = tail.astype(BF16)

        return 0

    lax.fori_loop(*ended(meta, first), finish, 0)
    edge16[...] = x_ref[BLOCK - 16 :, :]


def ended(meta, first):
    done = jnp.int32(0)
    upto = jnp.int32(0)
    for slot in range(EMAX):
        done = done + (meta[1 + slot] <= first).astype(jnp.int32)
        upto = upto + (meta[1 + slot] <= first + BLOCK).astype(jnp.int32)
    return done, upto


def states_kernel(
    meta, act_ref, b_ref, dt_ref, ld_ref, rep_ref, rep16_ref, tri_ref, tail_ref,
    cum_ref, carry_ref, sin_ref, pay_ref, fin_ref, first_ref,
    state, total, totals,
):
    step = pl.program_id(0)
    heads = dt_ref.shape[0]
    width = rep_ref.shape[1]
    span = pl.num_programs(0) * BLOCK
    parts = BLOCK // CHUNK
    first = step * BLOCK

    @pl.when(step == 0)
    def _():
        state[...] = jnp.zeros_like(state)
        total[...] = jnp.zeros_like(total)
        fin_ref[:, :width] = jnp.zeros_like(fin_ref[:, :width])
        fin_ref[:, width:] = tail_ref[...]
        first_ref[...] = jnp.zeros_like(first_ref)

    spans = [slice(part * CHUNK, part * CHUNK + CHUNK) for part in range(parts)]
    pieces = jnp.concatenate([thirds(ld_ref[:, rows] * LOG2E) for rows in spans], axis=0)
    summed = jnp.dot(pieces, tri_ref[...], preferred_element_type=F32)
    open_end = jnp.where(meta[0] < 0, meta[1], -1)
    running = total[...]
    weights = []
    throughs = []
    for part, rows in enumerate(spans):
        begin = first + part * CHUNK
        at = 3 * heads * part
        cum = summed[at : at + heads] + summed[at + heads : at + 2 * heads] + summed[at + 2 * heads : at + 3 * heads]
        cum_ref[:, rows] = cum
        lane = iota((heads, CHUNK), 1) + begin
        carry_ref[:, rows] = jnp.where(lane < open_end, jnp.exp2(running + cum), 0.0)
        totals[part] = running
        start = last_start(meta, begin + CHUNK - 1)
        last = cum[:, CHUNK - 1 :]
        weight = jnp.where(lane >= start, jnp.exp2(last - cum) * dt_ref[:, rows], 0.0)
        weights.append(weight.T.astype(BF16))
        throughs.append(spread_row(jnp.where(start < begin, jnp.exp2(last), 0.0), rep_ref[...]))
        running = running + last
    total[...] = running
    weight = jnp.concatenate(weights, axis=0)
    turned = [b_ref[rows, :].T for rows in spans]
    for tile in range(width // 256):
        cols = slice(tile * 256, tile * 256 + 256)
        scale = jnp.dot(weight, rep16_ref[:heads, cols], preferred_element_type=F32)
        load = scale.astype(BF16) * act_ref[:, cols]
        held = state[:, cols]
        for part, rows in enumerate(spans):
            sin_ref[part, :, cols] = held.astype(BF16)
            grown = jnp.dot(turned[part], load[rows], preferred_element_type=F32)
            held = throughs[part][:, cols] * held + grown
        state[:, cols] = held

    def finish(slot, _):
        end = meta[1 + slot]
        start = jnp.where(slot > 0, meta[jnp.maximum(slot, 1)], meta[0])
        part = (end - 1 - first) // CHUNK
        low = pl.multiple_of(part * CHUNK, CHUNK)
        begin = first + low
        lane = iota((heads, CHUNK), 1) + begin
        cum = cum_ref[:, pl.ds(low, CHUNK)]
        at_end = jnp.sum(jnp.where(lane == end - 1, cum, 0.0), axis=1, keepdims=True)
        inside = (lane < end) & (lane >= start)
        weight = jnp.exp2(jnp.minimum(at_end - cum, 0.0)) * dt_ref[:, pl.ds(low, CHUNK)]
        weight = jnp.where(inside, weight, 0.0).T.astype(BF16)
        scale = jnp.dot(weight, rep16_ref[:heads], preferred_element_type=F32)
        load = scale.astype(BF16) * act_ref[pl.ds(low, CHUNK), :]
        local = outer_dot(b_ref[pl.ds(low, CHUNK), :], load)
        through = spread_row(jnp.where(start < begin, jnp.exp2(at_end), 0.0), rep_ref[...])
        final = local + through * sin_ref[part].astype(F32)
        target = meta[5 + slot]
        opened = jnp.where(start < 0, jnp.exp2(totals[part][:, :1] + at_end), 0.0)

        @pl.when(slot == 0)
        def _():
            first_ref[...] = jnp.broadcast_to(spread_row(opened, rep_ref[...]), first_ref.shape)

        @pl.when(target >= 0)
        def _():
            fin_ref[target, :width] = final.astype(BF16).T

        return 0

    lax.fori_loop(*ended(meta, first), finish, 0)

    @pl.when(step == pl.num_programs(0) - 1)
    def _():
        start = last_start(meta, span - 1)
        gate = spread_row(jnp.where(start < 0, jnp.exp2(total[:, :1]), 0.0), rep_ref[...])
        gate = jnp.broadcast_to(gate, (PAY - N, width))
        high = gate.astype(BF16).astype(F32)
        pay_ref[:N] = state[...].astype(BF16)
        pay_ref[N:] = jnp.where(iota((PAY - N, width), 0) == 0, high, gate - high).astype(BF16)


def output_kernel(origin, late, meta, act_ref, rest_ref, dt_ref, cum_ref, sin_ref, gain_ref, rep16_ref, each_ref, *refs):
    out_ref = refs[-1]
    step = origin + pl.program_id(0)
    heads = dt_ref.shape[0]
    width = out_ref.shape[1]
    parts = BLOCK // CHUNK
    for part in range(parts):
        begin = step * BLOCK + part * CHUNK
        rows = slice(part * CHUNK, part * CHUNK + CHUNK)
        cum = cum_ref[:, rows]
        back = cum - jnp.log2(dt_ref[:, rows])
        ahead = jnp.concatenate(
            [thirds(cum), jnp.ones((3 * heads, CHUNK), BF16), jnp.zeros((CHUNK - 6 * heads, CHUNK), BF16)], axis=0
        ).T
        back = thirds(-back)
        b_act = rest_ref[rows, :N]
        c_act = rest_ref[rows, N:]
        place = iota((CHUNK, CHUNK), 0) + begin
        other = iota((CHUNK, CHUNK), 1) + begin
        scores = lax.dot_general(c_act, b_act, (((1,), (1,)), ((), ())), preferred_element_type=F32)
        scores = jnp.where((other <= place) & (other >= starts_of(meta, place)), scores, 0.0)
        scores = jnp.concatenate([scores, scores], axis=1)
        blank = jnp.zeros((CHUNK - 6 * heads, 256), BF16)
        lane = iota((heads, CHUNK), 1) + begin
        before = jnp.where(last_start(meta, begin) < begin, next_end(meta, begin), -1)
        entry = jnp.where(lane < before, jnp.exp2(cum), 0.0)
        entry = jnp.concatenate([entry, entry - entry.astype(BF16).astype(F32)], axis=0).T.astype(BF16)
        if late:
            extra = refs[0][:, rows]
            extra = jnp.concatenate([extra, extra - extra.astype(BF16).astype(F32)], axis=0).T.astype(BF16)
        left_half = iota((CHUNK, 128), 1) < P_SIZE
        for quad in range(heads // 4):
            cols = slice(quad * 256, quad * 256 + 256)
            outer = jnp.dot(c_act, sin_ref[part, :, cols], preferred_element_type=F32)
            scale = jnp.dot(entry, rep16_ref[:, cols], preferred_element_type=F32)
            sums = []
            for pair in (2 * quad, 2 * quad + 1):
                own = each_ref[:, pair * 256 : pair * 256 + 256]
                against = jnp.concatenate([own, jnp.concatenate([back, back], axis=1) * own, blank], axis=0)
                spread = jnp.dot(ahead, against, preferred_element_type=F32)
                mix = (jnp.exp2(jnp.minimum(spread, 0.0)) * scores).astype(BF16)
                x_pair = act_ref[rows, pair * 128 : pair * 128 + 128]
                zero = jnp.zeros_like(x_pair)
                split = jnp.concatenate(
                    [jnp.where(left_half, x_pair, zero), jnp.where(left_half, zero, x_pair)], axis=0
                )
                sums.append(jnp.dot(mix, split, preferred_element_type=F32))
            inner = jnp.concatenate(sums, axis=1)
            value = inner + scale * outer + gain_ref[:, cols] * act_ref[rows, cols].astype(F32)
            if late:
                outer = jnp.dot(c_act, refs[1][:, cols], preferred_element_type=F32)
                scale = jnp.dot(extra, rep16_ref[:, cols], preferred_element_type=F32)
                value = value + scale * outer
            out_ref[rows, cols] = value.astype(BF16)


def gates_of(pay_ref, cols):
    gates = pay_ref[N:, cols].astype(F32)
    return gates[0:1] + gates[1:2]


def pair_kernel(shard_ref, own_ref, got_ref, half_ref):
    side = half_ref.shape[1]

    def join(early, late, cols):
        after = gates_of(late, cols)
        gate = jnp.broadcast_to(after * gates_of(early, cols), (PAY - N, side))
        high = gate.astype(BF16).astype(F32)
        half_ref[:N] = (late[:N, cols].astype(F32) + after * early[:N, cols].astype(F32)).astype(BF16)
        half_ref[N:] = jnp.where(iota((PAY - N, side), 0) == 0, high, gate - high).astype(BF16)

    @pl.when(shard_ref[0] % 2 == 0)
    def _():
        join(own_ref, got_ref, slice(0, side))

    @pl.when(shard_ref[0] % 2 == 1)
    def _():
        join(got_ref, own_ref, slice(side, 2 * side))


def prefix_kernel(*refs):
    prefix_ref = refs[-1]
    side = prefix_ref.shape[1]
    total = jnp.zeros((N, side), F32)
    for ref in refs[:-1]:
        total = gates_of(ref, slice(0, side)) * total + ref[:N].astype(F32)
    prefix_ref[...] = total.astype(BF16)


def carry_kernel(shard_ref, stream_ref, meta, mine_ref, other_ref, early_ref, first_ref, carried_ref, *sends):
    side = mine_ref.shape[1]
    lower, upper = slice(0, side), slice(side, 2 * side)

    @pl.when(shard_ref[0] % 2 == 0)
    def _():
        carried_ref[:, lower] = mine_ref[...]
        carried_ref[:, upper] = other_ref[...]

    @pl.when(shard_ref[0] % 2 == 1)
    def _():
        for cols, part in ((lower, other_ref), (upper, mine_ref)):
            carried_ref[:, cols] = (
                early_ref[:N, cols].astype(F32) + gates_of(early_ref, cols) * part[...].astype(F32)
            ).astype(BF16)

    value = (first_ref[0:1] * carried_ref[...].astype(F32)).T.astype(BF16)
    apart = (meta[5] // CAP) ^ stream_ref[0]
    for index, ref in enumerate(sends):
        ref[...] = jnp.where(apart == index, value, jnp.zeros_like(value))


def correct_kernel(meta, base_ref, c_ref, carry_ref, carried_ref, rep16_ref, out_ref):
    width = out_ref.shape[1]
    touched = (meta[0] < 0) & (meta[1] > pl.program_id(0) * BLOCK)

    @pl.when(touched)
    def _():
        entry = carry_ref[...]
        entry = jnp.concatenate([entry, entry - entry.astype(BF16).astype(F32)], axis=0).T.astype(BF16)
        for tile in range(width // 256):
            cols = slice(tile * 256, tile * 256 + 256)
            outer = jnp.dot(c_ref[...], carried_ref[:, cols], preferred_element_type=F32)
            scale = jnp.dot(entry, rep16_ref[:, cols], preferred_element_type=F32)
            out_ref[:, cols] = (base_ref[:, cols].astype(F32) + scale * outer).astype(BF16)

    @pl.when(jnp.logical_not(touched))
    def _():
        out_ref[...] = base_ref[...]


def params(mib):
    return pltpu.CompilerParams(vmem_limit_bytes=mib * MIB)


def whole(shape):
    return pl.BlockSpec(shape, lambda *_: (0,) * len(shape))


def on_device(
    conv_input, conv_weight, conv_bias, step_size, log_decay, skip_gain, doc_bounds, doc_owner
):
    span, channels = conv_input.shape[1:]
    heads = step_size.shape[1]
    width = heads * P_SIZE
    steps = span // BLOCK
    chunks = span // CHUNK
    owners = lax.axis_size("stream")
    slots = owners * CAP
    rows = width + TAIL
    shard = lax.axis_index("seq").astype(jnp.int32).reshape(1)
    rows_in = conv_input[0]
    rim = shifted(rows_in[span - 16 :], "seq", 1)
    rep = (np.arange(width)[None, :] // P_SIZE == np.arange(heads)[:, None]).astype(np.float32)
    rep16 = np.concatenate([rep, rep], 0).astype(BF16)
    each = np.arange(heads * CHUNK)[None, :] // CHUNK == np.arange(3 * heads)[:, None] % heads
    each = each.astype(BF16)
    ticks = np.arange(CHUNK)
    tri = (ticks[:, None] <= ticks[None, :]).astype(BF16)
    order = np.arange(3 * CHUNK)
    tick, lag = 8 * (order // 24) + order % 8, order % 24 // 8 + 1
    source = np.arange(CHUNK + 16)
    move = (source[None, :] - 16 == (tick - lag)[:, None]).astype(BF16)
    slot = np.broadcast_to((4 * tick + lag)[:, None], (3 * CHUNK, 128)).astype(np.int32)
    smem = pl.BlockSpec(memory_space=pltpu.SMEM)
    stream = lax.axis_index("stream").astype(jnp.int32).reshape(1)
    per_head = pl.BlockSpec((heads, BLOCK), lambda i, *_: (0, i))
    prefetch = functools.partial(pltpu.PrefetchScalarGridSpec, num_scalar_prefetch=1)
    by_rows = pl.BlockSpec((BLOCK, channels), lambda i, *_: (i, 0))
    by_width = pl.BlockSpec((BLOCK, width), lambda i, *_: (i, 0))
    by_rest = pl.BlockSpec((BLOCK, 2 * N), lambda i, *_: (i, 0))
    act, rest, tails, meta = pl.pallas_call(
        conv_kernel,
        grid=(steps,),
        in_specs=[
            smem, smem, smem, by_rows, whole((16, channels)),
            whole((4, channels)), whole((1, channels)), whole(move.shape), whole(slot.shape),
        ],
        out_specs=[by_width, by_rest, whole((slots, TAIL, N)), smem],
        out_shape=[
            jax.ShapeDtypeStruct((span, width), BF16),
            jax.ShapeDtypeStruct((span, 2 * N), BF16),
            jax.ShapeDtypeStruct((slots, TAIL, N), BF16),
            jax.ShapeDtypeStruct((16,), jnp.int32),
        ],
        scratch_shapes=[
            pltpu.VMEM((16, channels), BF16),
            pltpu.VMEM((8, channels), F32),
            pltpu.VMEM((1 + BLOCK // CHUNK,) + move.shape, BF16),
            pltpu.SMEM((owners,), jnp.int32),
        ],
        compiler_params=params(60),
        cost_estimate=pl.CostEstimate(
            flops=2 * span * channels * 400, bytes_accessed=21 << 20, transcendentals=span * channels
        ),
        name="conv",
    )(shard, doc_bounds, doc_owner, rows_in, rim, conv_weight, conv_bias[None], move, slot)
    cum, carry, sin, pay, fin, first = pl.pallas_call(
        states_kernel,
        grid_spec=prefetch(
            grid=(steps,),
            in_specs=[
                by_width, pl.BlockSpec((BLOCK, N), lambda i, *_: (i, 0)), per_head, per_head,
                whole((heads, width)), whole((2 * heads, width)), whole((CHUNK, CHUNK)),
                whole((slots, TAIL, N)),
            ],
            out_specs=[
                per_head, per_head,
                pl.BlockSpec((BLOCK // CHUNK, N, width), lambda i, *_: (i, 0, 0)),
                whole((PAY, width)), whole((slots, rows, N)), whole((8, width)),
            ],
            scratch_shapes=[
                pltpu.VMEM((N, width), F32),
                pltpu.VMEM((heads, CHUNK), F32),
                pltpu.VMEM((BLOCK // CHUNK, heads, CHUNK), F32),
            ],
        ),
        out_shape=[
            jax.ShapeDtypeStruct((heads, span), F32),
            jax.ShapeDtypeStruct((heads, span), F32),
            jax.ShapeDtypeStruct((chunks, N, width), BF16),
            jax.ShapeDtypeStruct((PAY, width), BF16),
            jax.ShapeDtypeStruct((slots, rows, N), BF16),
            jax.ShapeDtypeStruct((8, width), F32),
        ],
        compiler_params=params(60),
        cost_estimate=pl.CostEstimate(
            flops=2 * span * width * N * 2, bytes_accessed=22 << 20, transcendentals=span * heads
        ),
        name="states",
    )(meta, act, rest, step_size[0], log_decay[0], rep, rep16, tri, tails)

    gain = jnp.repeat(skip_gain, P_SIZE)[None]

    def outputs(first, last, late=()):
        rows_of = functools.partial(pl.BlockSpec, index_map=lambda i, *_: (first + i, 0))
        heads_of = pl.BlockSpec((heads, BLOCK), lambda i, *_: (0, first + i))
        return pl.pallas_call(
            functools.partial(output_kernel, first, bool(late)),
            grid_spec=prefetch(
                grid=(last - first,),
                in_specs=[
                    rows_of((BLOCK, width)), rows_of((BLOCK, 2 * N)), heads_of, heads_of,
                    pl.BlockSpec((BLOCK // CHUNK, N, width), lambda i, *_: (first + i, 0, 0)),
                    whole((1, width)), whole((2 * heads, width)), whole(each.shape),
                ] + ([heads_of, whole((N, width)), pl.BlockSpec(memory_space=pl.ANY)] if late else []),
                out_specs=rows_of((BLOCK, width)),
            ),
            out_shape=jax.ShapeDtypeStruct((span, width), BF16),
            input_output_aliases={11: 0} if late else {},
            compiler_params=params(60),
            cost_estimate=pl.CostEstimate(
                flops=2 * (last - first) * BLOCK * width * N * 4,
                bytes_accessed=(last - first) * (4 << 20),
                transcendentals=(last - first) * BLOCK * CHUNK * heads,
            ),
            name="outputs",
        )(meta, act, rest, step_size[0], cum, sin, gain, rep16, each, *late)

    side = width // 2
    count = lax.axis_size("seq")
    pairs = [(index, index ^ 1) for index in range(count)]
    early = lax.ppermute(pay, "seq", pairs)
    got = lax.all_to_all(
        fin.reshape(owners, CAP, rows, N), "stream", split_axis=0, concat_axis=0, tiled=True
    )
    half = pl.pallas_call(
        pair_kernel,
        in_specs=[smem, whole((PAY, width)), whole((PAY, width))],
        out_specs=whole((PAY, side)),
        out_shape=jax.ShapeDtypeStruct((PAY, side), BF16),
        compiler_params=params(8),
        name="pair",
    )(shard, pay, early)
    chips = count // 2
    behind = [shifted(half, "seq", 2 * far) for far in range(chips - 1, 0, -1)]
    base = outputs(0, steps)
    *behind, base = lax.optimization_barrier((*behind, base))
    mine = pl.pallas_call(
        prefix_kernel,
        in_specs=[whole((PAY, side))] * len(behind),
        out_specs=whole((N, side)),
        out_shape=jax.ShapeDtypeStruct((N, side), BF16),
        compiler_params=params(8),
        name="prefix",
    )(*behind)
    other = lax.ppermute(mine, "seq", pairs)
    other, got = lax.optimization_barrier((other, got))
    carried, *send = pl.pallas_call(
        carry_kernel,
        in_specs=[smem, smem, smem, whole((N, side)), whole((N, side)), whole((PAY, width)), whole((8, width))],
        out_specs=[whole((N, width))] + [whole((width, N))] * owners,
        out_shape=[jax.ShapeDtypeStruct((N, width), BF16)]
        + [jax.ShapeDtypeStruct((width, N), BF16)] * owners,
        compiler_params=params(8),
        name="carry",
    )(shard, stream, meta, mine, other, early, first)
    more = [send[0]]
    for apart in range(1, owners):
        swap = [(index, index ^ apart) for index in range(owners)]
        more.append(lax.ppermute(send[apart], "stream", swap))

    out = pl.pallas_call(
        correct_kernel,
        grid_spec=prefetch(
            grid=(steps,),
            in_specs=[
                pl.BlockSpec((BLOCK, width), lambda i, *_: (i, 0)),
                pl.BlockSpec((BLOCK, N), lambda i, *_: (i, 1)),
                per_head,
                whole((N, width)), whole((2 * heads, width)),
            ],
            out_specs=pl.BlockSpec((BLOCK, width), lambda i, *_: (i, 0)),
        ),
        out_shape=jax.ShapeDtypeStruct((span, width), BF16),
        input_output_aliases={1: 0},
        compiler_params=params(60),
        cost_estimate=pl.CostEstimate(
            flops=2 * span * width * N, bytes_accessed=18 << 20, transcendentals=0
        ),
        name="correct",
    )(meta, base, rest, carry, carried, rep16)

    apart = (jnp.arange(owners) ^ stream)[:, None, None]
    extra = jnp.broadcast_to(more[0][None], (owners, width, N))
    for index in range(1, owners):
        extra = jnp.where(apart == index, more[index][None], extra)
    ranks = jnp.arange(CAP)[None, :, None, None]
    extra = jnp.where(ranks == 0, extra[:, None], jnp.zeros_like(extra[:, None]))
    ssm = got[:, :, :width].astype(F32) + extra.astype(F32)
    ssm = ssm.reshape(1, 1, owners, CAP, heads, P_SIZE, N)
    tiles = channels // N
    conv = got[:, :, width : width + 3 * tiles].reshape(owners, CAP, tiles, 3, N)
    conv = conv.transpose(0, 1, 3, 2, 4).reshape(1, 1, owners, CAP, 3, channels)
    return out[None], ssm, conv


def solution(mesh):
    in_specs = (
        P("stream", "seq", None),
        P(),
        P(),
        P("stream", None, "seq"),
        P("stream", None, "seq"),
        P(),
        P("stream", None),
        P("stream", None),
    )
    out_specs = (
        P("stream", "seq", None),
        P("stream", "seq", None, None, None, None, None),
        P("stream", "seq", None, None, None, None),
    )
    return jax.shard_map(
        on_device, mesh=mesh, in_specs=in_specs, out_specs=out_specs, check_vma=False
    )
```

```python
import functools

import jax
import jax.numpy as jnp
import numpy as np
from jax import lax
from jax.experimental import pallas as pl
from jax.experimental.pallas import tpu as pltpu
from jax.sharding import PartitionSpec as P

P_SIZE = 64
N = 128
EMAX = 4
CAP = 2
CHUNK = 128
BLOCK = 512
FAR = 1 << 30
AHEAD = 3
LOG2E = 1.4426950408889634
PAY = 144
TAIL = 32
MIB = 1024 * 1024

F32 = jnp.float32
BF16 = jnp.bfloat16


def shifted(value, axis, steps):
    count = lax.axis_size(axis)
    leading, last = (max(0, -steps), min(count, count - steps))
    return lax.ppermute(value, axis, [(source, source + steps) for source in range(leading, last)])


def iota(shape, axis):
    return lax.broadcasted_iota(jnp.int32, shape, axis)


def outer_dot(left, right):
    return lax.dot_general(left, right, (((0,), (0,)), ((), ())), preferred_element_type=F32)


def halves(value):
    high = value.astype(BF16)
    low = (value - high.astype(F32)).astype(BF16)
    return jnp.concatenate([high, low], axis=0)


def thirds(value):
    high = value.astype(BF16)
    rest = value - high.astype(F32)
    mid = rest.astype(BF16)
    low = (rest - mid.astype(F32)).astype(BF16)
    return jnp.concatenate([high, mid, low], axis=0)


def spread_row(column, rep):
    return jnp.sum(rep * column, axis=0, keepdims=True)


def last_start(meta, place):
    start = meta[0]
    for slot in range(EMAX):
        end = meta[1 + slot]
        start = jnp.where(end <= place, end, start)
    return start


def next_end(meta, place):
    end = FAR
    for slot in reversed(range(EMAX)):
        end = jnp.where(meta[1 + slot] > place, meta[1 + slot], end)
    return end


def starts_of(meta, rows):
    start = jnp.full(rows.shape, meta[0], jnp.int32)
    for slot in range(EMAX):
        end = meta[1 + slot]
        start = jnp.where(rows >= end, end, start)
    return start


def block_copy(index, hbm, held, sem, inward):
    place = pl.ds(pl.multiple_of(index * held.shape[1], held.shape[1]), held.shape[1])
    there = hbm.at[place]
    if inward:
        return pltpu.make_async_copy(there, held.at[index], sem.at[index])
    return pltpu.make_async_copy(held.at[index], there, sem.at[index])


def arrive(step, origin, hbm, held, sem):
    steps = held.shape[0]
    source = hbm.at[pl.ds(origin * held.shape[1], steps * held.shape[1])]

    @pl.when(step == 0)
    def _():
        for index in range(min(AHEAD, steps)):
            block_copy(index, source, held, sem, True).start()

    @pl.when(step + AHEAD < steps)
    def _():
        block_copy(step + AHEAD, source, held, sem, True).start()

    block_copy(step, source, held, sem, True).wait()
    return held.at[step]


def leave(step, hbm, held, sem):
    block_copy(step, hbm, held, sem, False).start()

    @pl.when(step == held.shape[0] - 1)
    def _():
        for index in range(held.shape[0]):
            block_copy(index, hbm, held, sem, False).wait()


def stream_buffers(steps, shape, dtype):
    return [pltpu.VMEM((steps,) + shape, dtype), pltpu.SemaphoreType.DMA((steps,))]


def read_docs(bounds, owners, meta, count, anchor, span):
    for slot in range(EMAX):
        meta[1 + slot] = FAR
        meta[5 + slot] = 0
    for owner in range(count.shape[0]):
        count[owner] = 0

    def one(index, carry):
        found, prior, start = carry
        end = bounds[0, index]
        owner = owners[0, index]
        mine = (end > prior) & (end > anchor) & (end <= anchor + span) & (found < EMAX)

        @pl.when(mine)
        def _():
            meta[1 + found] = end - anchor
            rank = count[owner]
            meta[5 + found] = jnp.where(rank < CAP, owner * CAP + rank, -1)
            count[owner] = rank + 1

        return found + mine.astype(jnp.int32), end, jnp.where(end <= anchor, end, start)

    zero = jnp.int32(0)
    _, _, start = lax.fori_loop(0, bounds.shape[1], one, (zero, zero, zero))
    meta[0] = start - anchor


def conv_kernel(
    shard_ref, bounds, owners, x_hbm, rim_ref, w_ref, bias_ref, move_ref, slot_ref,
    act_hbm, rest_hbm, tail_ref, meta,
    x_held, x_sem, act_held, act_sem, rest_held, rest_sem,
    edge16, weights, moves, lines, count,
):
    step = pl.program_id(0)
    x_ref = arrive(step, 0, x_hbm, x_held, x_sem)
    act_ref, rest_ref = act_held.at[step], rest_held.at[step]
    span = pl.num_programs(0) * BLOCK
    parts = BLOCK // CHUNK
    first = step * BLOCK

    @pl.when(step == 0)
    def _():
        read_docs(bounds, owners, meta, count, shard_ref[0] * span, span)
        tail_ref[...] = jnp.zeros_like(tail_ref)
        lines[...] = jnp.zeros_like(lines)
        edge16[...] = rim_ref[...]
        weights[0:4] = 0.5 * w_ref[...]
        weights[4:5] = 0.5 * bias_ref[...].reshape(1, weights.shape[1])
        moves[0] = move_ref[...]

    choices = []
    for part in range(parts):
        begin = first + part * CHUNK
        near = (meta[0] > begin - 3) & (meta[0] < begin + CHUNK)
        for slot in range(EMAX):
            near = near | ((meta[1 + slot] > begin - 3) & (meta[1 + slot] < begin + CHUNK))

        @pl.when(near)
        def _():
            tick = slot_ref[...] // 4 + begin
            kept = (tick - starts_of(meta, tick) >= slot_ref[...] % 4).astype(F32)
            moves[1 + part, :, :128] = (kept * move_ref[:, :128].astype(F32)).astype(BF16)
            moves[1 + part, :, 128:] = (kept[:, :16] * move_ref[:, 128:].astype(F32)).astype(BF16)

        choices.append(jnp.where(near, 1 + part, 0))

    for part in range(parts):
        low = part * CHUNK
        rows = slice(low, low + CHUNK)
        pick = moves[choices[part]]
        for tile in range(x_ref.shape[1] // 256):
            cols = slice(tile * 256, tile * 256 + 256)
            if part:
                wide = x_ref[low - 16 : low + CHUNK, cols]
            else:
                wide = jnp.concatenate([edge16[:, cols], x_ref[rows, cols]], axis=0)
            moved = jnp.dot(pick, wide, preferred_element_type=F32)
            moved = moved.reshape(CHUNK // 8, 3, 8, 256)
            mixed = weights[4:5, cols] + weights[0:1, cols] * x_ref[rows, cols].astype(F32)
            for lag in range(1, 4):
                mixed = mixed + weights[lag : lag + 1, cols] * moved[:, lag - 1].reshape(CHUNK, 256)
            value = (mixed + mixed * jnp.tanh(mixed)).astype(BF16)
            if tile * 256 < act_ref.shape[1]:
                act_ref[rows, cols] = value
            else:
                rest_ref[rows, :] = value

    def finish(slot, _):
        end = meta[1 + slot]
        start = jnp.where(slot > 0, meta[jnp.maximum(slot, 1)], meta[0])
        low = pl.multiple_of((end - 1 - first) // CHUNK * CHUNK, CHUNK)
        begin = first + low
        target = meta[5 + slot]
        row = iota((16, CHUNK), 0)
        col = iota((16, CHUNK), 1) + begin
        pick = (col == end - 3 + row) & (col >= start) & (row < 3)
        row16 = iota((16, 16), 0)
        col16 = iota((16, 16), 1) + begin - 16
        pick16 = (col16 == end - 3 + row16) & (col16 >= start) & (row16 < 3)
        before = pl.multiple_of(jnp.maximum(low - 16, 0), 16)
        rim = jnp.where(low > 0, x_ref[pl.ds(before, 16), :].astype(F32), edge16[...].astype(F32))
        last = jnp.dot(
            pick.astype(F32).astype(BF16), x_ref[pl.ds(low, CHUNK), :], preferred_element_type=F32
        ) + jnp.dot(pick16.astype(F32).astype(BF16), rim.astype(BF16), preferred_element_type=F32)
        tiles = x_ref.shape[1] // 128
        for index in range(3):
            for tile in range(tiles):
                at = index * tiles + tile
                lines[at : at + 1] = last[index : index + 1, tile * 128 : tile * 128 + 128]

        @pl.when(target >= 0)
        def _():
            tail_ref[target] = lines[...].astype(BF16)

        return 0

    lax.fori_loop(*ended(meta, first), finish, 0)
    edge16[...] = x_ref[BLOCK - 16 :, :]
    leave(step, act_hbm, act_held, act_sem)
    leave(step, rest_hbm, rest_held, rest_sem)


def ended(meta, first):
    done = jnp.int32(0)
    upto = jnp.int32(0)
    for slot in range(EMAX):
        done = done + (meta[1 + slot] <= first).astype(jnp.int32)
        upto = upto + (meta[1 + slot] <= first + BLOCK).astype(jnp.int32)
    return done, upto


def states_kernel(
    meta, act_hbm, b_ref, dt_ref, ld_ref, rep_ref, rep16_ref, tri_ref, tail_ref,
    cum_ref, carry_ref, sin_hbm, pay_ref, fin_ref, first_ref,
    act_held, act_sem, sin_held, sin_sem, state, total, totals, blank, made, blank_sem, made_sem,
):
    step = pl.program_id(0)
    heads = dt_ref.shape[0]
    width = rep_ref.shape[1]
    span = pl.num_programs(0) * BLOCK
    parts = BLOCK // CHUNK
    first = step * BLOCK
    act_ref = arrive(step, 0, act_hbm, act_held, act_sem)
    sin_ref = sin_held.at[step]

    @pl.when(step == 0)
    def _():
        state[...] = jnp.zeros_like(state)
        total[...] = jnp.zeros_like(total)
        blank[...] = jnp.zeros_like(blank)
        for index in range(fin_ref.shape[0]):
            pltpu.make_async_copy(blank, fin_ref.at[index], blank_sem.at[index]).start()
        first_ref[...] = jnp.zeros_like(first_ref)

    spans = [slice(part * CHUNK, part * CHUNK + CHUNK) for part in range(parts)]
    pieces = jnp.concatenate([thirds(ld_ref[:, rows] * LOG2E) for rows in spans], axis=0)
    summed = jnp.dot(pieces, tri_ref[...], preferred_element_type=F32)
    open_end = jnp.where(meta[0] < 0, meta[1], -1)
    running = total[...]
    weights = []
    throughs = []
    for part, rows in enumerate(spans):
        begin = first + part * CHUNK
        at = 3 * heads * part
        cum = summed[at : at + heads] + summed[at + heads : at + 2 * heads] + summed[at + 2 * heads : at + 3 * heads]
        cum_ref[:, rows] = cum
        lane = iota((heads, CHUNK), 1) + begin
        carry_ref[:, rows] = jnp.where(lane < open_end, jnp.exp2(running + cum), 0.0)
        totals[part] = running
        start = last_start(meta, begin + CHUNK - 1)
        last = cum[:, CHUNK - 1 :]
        weight = jnp.where(lane >= start, jnp.exp2(last - cum) * dt_ref[:, rows], 0.0)
        weights.append(weight.T.astype(BF16))
        throughs.append(spread_row(jnp.where(start < begin, jnp.exp2(last), 0.0), rep_ref[...]))
        running = running + last
    total[...] = running
    weight = jnp.concatenate(weights, axis=0)
    turned = [b_ref[rows, :].T for rows in spans]
    for tile in range(width // 256):
        cols = slice(tile * 256, tile * 256 + 256)
        scale = jnp.dot(weight, rep16_ref[:heads, cols], preferred_element_type=F32)
        load = scale.astype(BF16) * act_ref[:, cols]
        held = state[:, cols]
        for part, rows in enumerate(spans):
            sin_ref[part, :, cols] = held.astype(BF16)
            grown = jnp.dot(turned[part], load[rows], preferred_element_type=F32)
            held = throughs[part][:, cols] * held + grown
        state[:, cols] = held
    leave(step, sin_hbm, sin_held, sin_sem)

    def finish(slot, _):
        end = meta[1 + slot]
        start = jnp.where(slot > 0, meta[jnp.maximum(slot, 1)], meta[0])
        part = (end - 1 - first) // CHUNK
        low = pl.multiple_of(part * CHUNK, CHUNK)
        begin = first + low
        lane = iota((heads, CHUNK), 1) + begin
        cum = cum_ref[:, pl.ds(low, CHUNK)]
        at_end = jnp.sum(jnp.where(lane == end - 1, cum, 0.0), axis=1, keepdims=True)
        inside = (lane < end) & (lane >= start)
        weight = jnp.exp2(jnp.minimum(at_end - cum, 0.0)) * dt_ref[:, pl.ds(low, CHUNK)]
        weight = jnp.where(inside, weight, 0.0).T.astype(BF16)
        scale = jnp.dot(weight, rep16_ref[:heads], preferred_element_type=F32)
        load = scale.astype(BF16) * act_ref[pl.ds(low, CHUNK), :]
        local = outer_dot(b_ref[pl.ds(low, CHUNK), :], load)
        through = spread_row(jnp.where(start < begin, jnp.exp2(at_end), 0.0), rep_ref[...])
        final = local + through * sin_ref[part].astype(F32)
        target = meta[5 + slot]
        opened = jnp.where(start < 0, jnp.exp2(totals[part][:, :1] + at_end), 0.0)

        @pl.when(slot == 0)
        def _():
            first_ref[...] = jnp.broadcast_to(spread_row(opened, rep_ref[...]), first_ref.shape)

        @pl.when(target >= 0)
        def _():
            made[slot, :width] = final.astype(BF16).T
            made[slot, width:] = tail_ref[target]
            pltpu.make_async_copy(made.at[slot], fin_ref.at[target], made_sem.at[slot]).start()

        return 0

    @pl.when(step == 0)
    def _():
        for index in range(fin_ref.shape[0]):
            pltpu.make_async_copy(blank, fin_ref.at[index], blank_sem.at[index]).wait()

    lax.fori_loop(*ended(meta, first), finish, 0)

    @pl.when(step == pl.num_programs(0) - 1)
    def _():
        for slot in range(EMAX):

            @pl.when((meta[1 + slot] <= span) & (meta[5 + slot] >= 0))
            def _():
                pltpu.make_async_copy(made.at[slot], fin_ref.at[meta[5 + slot]], made_sem.at[slot]).wait()

        start = last_start(meta, span - 1)
        gate = spread_row(jnp.where(start < 0, jnp.exp2(total[:, :1]), 0.0), rep_ref[...])
        gate = jnp.broadcast_to(gate, (PAY - N, width))
        high = gate.astype(BF16).astype(F32)
        pay_ref[:N] = state[...].astype(BF16)
        pay_ref[N:] = jnp.where(iota((PAY - N, width), 0) == 0, high, gate - high).astype(BF16)


def output_kernel(
    meta, act_hbm, rest_ref, dt_ref, cum_ref, sin_hbm, gain_in, rep_ref, rep16_ref, each_ref, out_hbm,
    act_held, act_sem, sin_held, sin_sem, out_held, out_sem, gain_ref,
):
    step = pl.program_id(0)
    act_ref = arrive(step, 0, act_hbm, act_held, act_sem)
    sin_ref = arrive(step, 0, sin_hbm, sin_held, sin_sem)
    out_ref = out_held.at[step]
    heads = dt_ref.shape[0]
    width = out_ref.shape[1]
    parts = BLOCK // CHUNK

    @pl.when(pl.program_id(0) == 0)
    def _():
        row = jnp.zeros((1, width), F32)
        for head in range(heads):
            row = row + gain_in[head] * rep_ref[head : head + 1, :]
        gain_ref[...] = row

    for part in range(parts):
        begin = step * BLOCK + part * CHUNK
        rows = slice(part * CHUNK, part * CHUNK + CHUNK)
        cum = cum_ref[:, rows]
        back = cum - jnp.log2(dt_ref[:, rows])
        ahead = jnp.concatenate(
            [thirds(cum), jnp.ones((3 * heads, CHUNK), BF16), jnp.zeros((CHUNK - 6 * heads, CHUNK), BF16)], axis=0
        ).T
        back = thirds(-back)
        b_act = rest_ref[rows, :N]
        c_act = rest_ref[rows, N:]
        place = iota((CHUNK, CHUNK), 0) + begin
        other = iota((CHUNK, CHUNK), 1) + begin
        scores = lax.dot_general(c_act, b_act, (((1,), (1,)), ((), ())), preferred_element_type=F32)
        scores = jnp.where((other <= place) & (other >= starts_of(meta, place)), scores, 0.0)
        scores = jnp.concatenate([scores, scores], axis=1)
        blank = jnp.zeros((CHUNK - 6 * heads, 256), BF16)
        lane = iota((heads, CHUNK), 1) + begin
        before = jnp.where(last_start(meta, begin) < begin, next_end(meta, begin), -1)
        entry = jnp.where(lane < before, jnp.exp2(cum), 0.0)
        entry = jnp.concatenate([entry, entry - entry.astype(BF16).astype(F32)], axis=0).T.astype(BF16)
        left_half = iota((CHUNK, 128), 1) < P_SIZE
        for quad in range(heads // 4):
            cols = slice(quad * 256, quad * 256 + 256)
            outer = jnp.dot(c_act, sin_ref[part, :, cols], preferred_element_type=F32)
            scale = jnp.dot(entry, rep16_ref[:, cols], preferred_element_type=F32)
            sums = []
            for pair in (2 * quad, 2 * quad + 1):
                own = each_ref[:, pair * 256 : pair * 256 + 256]
                against = jnp.concatenate([own, jnp.concatenate([back, back], axis=1) * own, blank], axis=0)
                spread = jnp.dot(ahead, against, preferred_element_type=F32)
                mix = (jnp.exp2(jnp.minimum(spread, 0.0)) * scores).astype(BF16)
                x_pair = act_ref[rows, pair * 128 : pair * 128 + 128]
                zero = jnp.zeros_like(x_pair)
                split = jnp.concatenate(
                    [jnp.where(left_half, x_pair, zero), jnp.where(left_half, zero, x_pair)], axis=0
                )
                sums.append(jnp.dot(mix, split, preferred_element_type=F32))
            inner = jnp.concatenate(sums, axis=1)
            value = inner + scale * outer + gain_ref[:, cols] * act_ref[rows, cols].astype(F32)
            out_ref[rows, cols] = value.astype(BF16)
    leave(step, out_hbm, out_held, out_sem)


def gates_of(pay_ref, cols):
    gates = pay_ref[N:, cols].astype(F32)
    return gates[0:1] + gates[1:2]


def pair_kernel(shard_ref, own_ref, got_ref, half_ref):
    side = half_ref.shape[1]

    def join(early, late, cols):
        after = gates_of(late, cols)
        gate = jnp.broadcast_to(after * gates_of(early, cols), (PAY - N, side))
        high = gate.astype(BF16).astype(F32)
        half_ref[:N] = (late[:N, cols].astype(F32) + after * early[:N, cols].astype(F32)).astype(BF16)
        half_ref[N:] = jnp.where(iota((PAY - N, side), 0) == 0, high, gate - high).astype(BF16)

    @pl.when(shard_ref[0] % 2 == 0)
    def _():
        join(own_ref, got_ref, slice(0, side))

    @pl.when(shard_ref[0] % 2 == 1)
    def _():
        join(got_ref, own_ref, slice(side, 2 * side))


def prefix_kernel(*refs):
    prefix_ref = refs[-1]
    side = prefix_ref.shape[1]
    total = jnp.zeros((N, side), F32)
    for ref in refs[:-1]:
        total = gates_of(ref, slice(0, side)) * total + ref[:N].astype(F32)
    prefix_ref[...] = total.astype(BF16)


def carry_kernel(shard_ref, stream_ref, meta, mine_ref, other_ref, early_ref, first_ref, carried_ref, *sends):
    side = mine_ref.shape[1]
    lower, upper = slice(0, side), slice(side, 2 * side)

    @pl.when(shard_ref[0] % 2 == 0)
    def _():
        carried_ref[:, lower] = mine_ref[...]
        carried_ref[:, upper] = other_ref[...]

    @pl.when(shard_ref[0] % 2 == 1)
    def _():
        for cols, part in ((lower, other_ref), (upper, mine_ref)):
            carried_ref[:, cols] = (
                early_ref[:N, cols].astype(F32) + gates_of(early_ref, cols) * part[...].astype(F32)
            ).astype(BF16)

    value = (first_ref[0:1] * carried_ref[...].astype(F32)).T.astype(BF16)
    apart = (meta[5] // CAP) ^ stream_ref[0]
    for index, ref in enumerate(sends):
        ref[...] = jnp.where(apart == index, value, jnp.zeros_like(value))


def correct_kernel(
    meta, base_hbm, c_ref, carry_ref, carried_ref, rep16_ref, out_hbm, held, in_sem, out_sem
):
    step = pl.program_id(0)
    steps = held.shape[0]
    width = held.shape[2]

    def touched(index):
        return (meta[0] < 0) & (meta[1] > index * BLOCK)

    def begin(index):
        @pl.when(touched(index))
        def _():
            block_copy(index, base_hbm, held, in_sem, True).start()

    @pl.when(step == 0)
    def _():
        for index in range(AHEAD):
            begin(index)

    @pl.when(step + AHEAD < steps)
    def _():
        begin(step + AHEAD)

    @pl.when(touched(step))
    def _():
        block_copy(step, base_hbm, held, in_sem, True).wait()
        entry = carry_ref[...]
        entry = jnp.concatenate([entry, entry - entry.astype(BF16).astype(F32)], axis=0).T.astype(BF16)
        for tile in range(width // 256):
            cols = slice(tile * 256, tile * 256 + 256)
            outer = jnp.dot(c_ref[...], carried_ref[:, cols], preferred_element_type=F32)
            scale = jnp.dot(entry, rep16_ref[:, cols], preferred_element_type=F32)
            held[step, :, cols] = (held[step, :, cols].astype(F32) + scale * outer).astype(BF16)
        block_copy(step, out_hbm, held, out_sem, False).start()

    @pl.when(step == steps - 1)
    def _():
        for index in range(held.shape[0]):

            @pl.when(touched(index))
            def _():
                block_copy(index, out_hbm, held, out_sem, False).wait()


def params(mib):
    return pltpu.CompilerParams(vmem_limit_bytes=mib * MIB)


def whole(shape):
    return pl.BlockSpec(shape, lambda *_: (0,) * len(shape))


def on_device(
    conv_input, conv_weight, conv_bias, step_size, log_decay, skip_gain, doc_bounds, doc_owner
):
    span, channels = conv_input.shape[1:]
    heads = step_size.shape[1]
    width = heads * P_SIZE
    steps = span // BLOCK
    chunks = span // CHUNK
    owners = lax.axis_size("stream")
    slots = owners * CAP
    rows = width + TAIL
    shard = lax.axis_index("seq").astype(jnp.int32).reshape(1)
    rows_in = conv_input[0]
    rim = shifted(rows_in[span - 16 :], "seq", 1)
    rep = (np.arange(width)[None, :] // P_SIZE == np.arange(heads)[:, None]).astype(np.float32)
    rep16 = np.concatenate([rep, rep], 0).astype(BF16)
    each = np.arange(heads * CHUNK)[None, :] // CHUNK == np.arange(3 * heads)[:, None] % heads
    each = each.astype(BF16)
    ticks = np.arange(CHUNK)
    tri = (ticks[:, None] <= ticks[None, :]).astype(BF16)
    order = np.arange(3 * CHUNK)
    tick, lag = 8 * (order // 24) + order % 8, order % 24 // 8 + 1
    source = np.arange(CHUNK + 16)
    move = (source[None, :] - 16 == (tick - lag)[:, None]).astype(BF16)
    slot = np.broadcast_to((4 * tick + lag)[:, None], (3 * CHUNK, 128)).astype(np.int32)
    smem = pl.BlockSpec(memory_space=pltpu.SMEM)
    stream = lax.axis_index("stream").astype(jnp.int32).reshape(1)
    per_head = pl.BlockSpec((heads, BLOCK), lambda i, *_: (0, i))
    prefetch = functools.partial(pltpu.PrefetchScalarGridSpec, num_scalar_prefetch=1)
    in_hbm = pl.BlockSpec(memory_space=pl.ANY)
    act, rest, tails, meta = pl.pallas_call(
        conv_kernel,
        grid=(steps,),
        in_specs=[
            smem, smem, smem, in_hbm, whole((16, channels)),
            whole((4, channels)), whole((channels,)), whole(move.shape), whole(slot.shape),
        ],
        out_specs=[in_hbm, in_hbm, whole((slots, TAIL, N)), smem],
        out_shape=[
            jax.ShapeDtypeStruct((span, width), BF16),
            jax.ShapeDtypeStruct((span, 2 * N), BF16),
            jax.ShapeDtypeStruct((slots, TAIL, N), BF16),
            jax.ShapeDtypeStruct((16,), jnp.int32),
        ],
        scratch_shapes=[
            *stream_buffers(steps, (BLOCK, channels), BF16),
            *stream_buffers(steps, (BLOCK, width), BF16),
            *stream_buffers(steps, (BLOCK, 2 * N), BF16),
            pltpu.VMEM((16, channels), BF16),
            pltpu.VMEM((8, channels), F32),
            pltpu.VMEM((1 + BLOCK // CHUNK,) + move.shape, BF16),
            pltpu.VMEM((TAIL, N), F32),
            pltpu.SMEM((owners,), jnp.int32),
        ],
        compiler_params=params(60),
        cost_estimate=pl.CostEstimate(
            flops=2 * span * channels * 400, bytes_accessed=21 << 20, transcendentals=span * channels
        ),
        name="conv",
    )(shard, doc_bounds, doc_owner, rows_in, rim, conv_weight, conv_bias, move, slot)
    cum, carry, sin, pay, fin, first = pl.pallas_call(
        states_kernel,
        grid_spec=prefetch(
            grid=(steps,),
            in_specs=[
                in_hbm, pl.BlockSpec((BLOCK, N), lambda i, *_: (i, 0)), per_head, per_head,
                whole((heads, width)), whole((2 * heads, width)), whole((CHUNK, CHUNK)),
                whole((slots, TAIL, N)),
            ],
            out_specs=[
                per_head, per_head,
                in_hbm,
                whole((PAY, width)), pl.BlockSpec(memory_space=pl.ANY), whole((8, width)),
            ],
            scratch_shapes=[
                *stream_buffers(steps, (BLOCK, width), BF16),
                *stream_buffers(steps, (BLOCK // CHUNK, N, width), BF16),
                pltpu.VMEM((N, width), F32),
                pltpu.VMEM((heads, CHUNK), F32),
                pltpu.VMEM((BLOCK // CHUNK, heads, CHUNK), F32),
                pltpu.VMEM((rows, N), BF16),
                pltpu.VMEM((EMAX, rows, N), BF16),
                pltpu.SemaphoreType.DMA((slots,)),
                pltpu.SemaphoreType.DMA((EMAX,)),
            ],
        ),
        out_shape=[
            jax.ShapeDtypeStruct((heads, span), F32),
            jax.ShapeDtypeStruct((heads, span), F32),
            jax.ShapeDtypeStruct((chunks, N, width), BF16),
            jax.ShapeDtypeStruct((PAY, width), BF16),
            jax.ShapeDtypeStruct((slots, rows, N), BF16),
            jax.ShapeDtypeStruct((8, width), F32),
        ],
        compiler_params=params(60),
        cost_estimate=pl.CostEstimate(
            flops=2 * span * width * N * 2, bytes_accessed=22 << 20, transcendentals=span * heads
        ),
        name="states",
    )(meta, act, rest, step_size[0], log_decay[0], rep, rep16, tri, tails)


    base_call = pl.pallas_call(
        output_kernel,
        grid_spec=prefetch(
            grid=(steps,),
            in_specs=[
                in_hbm, pl.BlockSpec((BLOCK, 2 * N), lambda i, *_: (i, 0)), per_head, per_head, in_hbm,
                smem, whole((heads, width)), whole((2 * heads, width)), whole(each.shape),
            ],
            out_specs=in_hbm,
            scratch_shapes=[
                *stream_buffers(steps, (BLOCK, width), BF16),
                *stream_buffers(steps, (BLOCK // CHUNK, N, width), BF16),
                *stream_buffers(steps, (BLOCK, width), BF16),
                pltpu.VMEM((1, width), F32),
            ],
        ),
        out_shape=jax.ShapeDtypeStruct((span, width), BF16),
        compiler_params=params(60),
        cost_estimate=pl.CostEstimate(
            flops=2 * span * width * N * 4, bytes_accessed=30 << 20, transcendentals=span * CHUNK * heads
        ),
        name="outputs",
    )

    side = width // 2
    count = lax.axis_size("seq")
    pairs = [(index, index ^ 1) for index in range(count)]
    early = lax.ppermute(pay, "seq", pairs)
    got = lax.all_to_all(
        fin.reshape(owners, CAP, rows, N), "stream", split_axis=0, concat_axis=0, tiled=True
    )
    half = pl.pallas_call(
        pair_kernel,
        in_specs=[smem, whole((PAY, width)), whole((PAY, width))],
        out_specs=whole((PAY, side)),
        out_shape=jax.ShapeDtypeStruct((PAY, side), BF16),
        compiler_params=params(8),
        name="pair",
    )(shard, pay, early)
    chips = count // 2
    behind = [shifted(half, "seq", 2 * far) for far in range(chips - 1, 0, -1)]
    base = base_call(meta, act, rest, step_size[0], cum, sin, skip_gain, rep, rep16, each)
    *behind, base = lax.optimization_barrier((*behind, base))
    mine = pl.pallas_call(
        prefix_kernel,
        in_specs=[whole((PAY, side))] * len(behind),
        out_specs=whole((N, side)),
        out_shape=jax.ShapeDtypeStruct((N, side), BF16),
        compiler_params=params(8),
        name="prefix",
    )(*behind)
    other = lax.ppermute(mine, "seq", pairs)
    other, got = lax.optimization_barrier((other, got))
    carried, *send = pl.pallas_call(
        carry_kernel,
        in_specs=[smem, smem, smem, whole((N, side)), whole((N, side)), whole((PAY, width)), whole((8, width))],
        out_specs=[whole((N, width))] + [whole((width, N))] * owners,
        out_shape=[jax.ShapeDtypeStruct((N, width), BF16)]
        + [jax.ShapeDtypeStruct((width, N), BF16)] * owners,
        compiler_params=params(8),
        name="carry",
    )(shard, stream, meta, mine, other, early, first)
    more = [send[0]]
    for apart in range(1, owners):
        swap = [(index, index ^ apart) for index in range(owners)]
        more.append(lax.ppermute(send[apart], "stream", swap))

    out = pl.pallas_call(
        correct_kernel,
        grid_spec=prefetch(
            grid=(steps,),
            in_specs=[
                in_hbm,
                pl.BlockSpec((BLOCK, N), lambda i, *_: (i, 1)),
                per_head,
                whole((N, width)), whole((2 * heads, width)),
            ],
            out_specs=in_hbm,
            scratch_shapes=[*stream_buffers(steps, (BLOCK, width), BF16), pltpu.SemaphoreType.DMA((steps,))],
        ),
        out_shape=jax.ShapeDtypeStruct((span, width), BF16),
        input_output_aliases={1: 0},
        compiler_params=params(60),
        cost_estimate=pl.CostEstimate(
            flops=2 * span * width * N, bytes_accessed=18 << 20, transcendentals=0
        ),
        name="correct",
    )(meta, base, rest, carry, carried, rep16)

    apart = (jnp.arange(owners) ^ stream)[:, None, None]
    extra = jnp.broadcast_to(more[0][None], (owners, width, N))
    for index in range(1, owners):
        extra = jnp.where(apart == index, more[index][None], extra)
    ranks = jnp.arange(CAP)[None, :, None, None]
    extra = jnp.where(ranks == 0, extra[:, None], jnp.zeros_like(extra[:, None]))
    ssm = got[:, :, :width].astype(F32) + extra.astype(F32)
    ssm = ssm.reshape(1, 1, owners, CAP, heads, P_SIZE, N)
    tiles = channels // N
    conv = got[:, :, width : width + 3 * tiles].reshape(1, 1, owners, CAP, 3, channels)
    return out[None], ssm, conv


def solution(mesh):
    in_specs = (
        P("stream", "seq", None),
        P(),
        P(),
        P("stream", None, "seq"),
        P("stream", None, "seq"),
        P(),
        P("stream", None),
        P("stream", None),
    )
    out_specs = (
        P("stream", "seq", None),
        P("stream", "seq", None, None, None, None, None),
        P("stream", "seq", None, None, None, None),
    )
    return jax.shard_map(
        on_device, mesh=mesh, in_specs=in_specs, out_specs=out_specs, check_vma=False
    )
```

```python
import functools

import jax
import jax.numpy as jnp
import numpy as np
from jax import lax
from jax.experimental import pallas as pl
from jax.experimental.pallas import tpu as pltpu
from jax.sharding import PartitionSpec as P

P_SIZE = 64
N = 128
EMAX = 4
CAP = 2
CHUNK = 128
BLOCK = 512
FAR = 1 << 30
LOG2E = 1.4426950408889634
PAY = 144
TAIL = 32
MIB = 1024 * 1024

F32 = jnp.float32
BF16 = jnp.bfloat16


def shifted(value, axis, steps):
    count = lax.axis_size(axis)
    leading, last = (max(0, -steps), min(count, count - steps))
    return lax.ppermute(value, axis, [(source, source + steps) for source in range(leading, last)])


def iota(shape, axis):
    return lax.broadcasted_iota(jnp.int32, shape, axis)


def outer_dot(left, right):
    return lax.dot_general(left, right, (((0,), (0,)), ((), ())), preferred_element_type=F32)


def halves(value):
    high = value.astype(BF16)
    low = (value - high.astype(F32)).astype(BF16)
    return jnp.concatenate([high, low], axis=0)


def thirds(value):
    high = value.astype(BF16)
    rest = value - high.astype(F32)
    mid = rest.astype(BF16)
    low = (rest - mid.astype(F32)).astype(BF16)
    return jnp.concatenate([high, mid, low], axis=0)


def spread_row(column, rep):
    return jnp.sum(rep * column, axis=0, keepdims=True)


def last_start(meta, place):
    start = meta[0]
    for slot in range(EMAX):
        end = meta[1 + slot]
        start = jnp.where(end <= place, end, start)
    return start


def next_end(meta, place):
    end = FAR
    for slot in reversed(range(EMAX)):
        end = jnp.where(meta[1 + slot] > place, meta[1 + slot], end)
    return end


def starts_of(meta, rows):
    start = jnp.full(rows.shape, meta[0], jnp.int32)
    for slot in range(EMAX):
        end = meta[1 + slot]
        start = jnp.where(rows >= end, end, start)
    return start


def read_docs(bounds, owners, meta, count, anchor, span):
    for slot in range(EMAX):
        meta[1 + slot] = FAR
        meta[5 + slot] = 0
    for owner in range(count.shape[0]):
        count[owner] = 0

    def one(index, carry):
        found, prior, start = carry
        end = bounds[0, index]
        owner = owners[0, index]
        mine = (end > prior) & (end > anchor) & (end <= anchor + span) & (found < EMAX)

        @pl.when(mine)
        def _():
            meta[1 + found] = end - anchor
            rank = count[owner]
            meta[5 + found] = jnp.where(rank < CAP, owner * CAP + rank, -1)
            count[owner] = rank + 1

        return found + mine.astype(jnp.int32), end, jnp.where(end <= anchor, end, start)

    zero = jnp.int32(0)
    _, _, start = lax.fori_loop(0, bounds.shape[1], one, (zero, zero, zero))
    meta[0] = start - anchor


def conv_kernel(
    shard_ref, bounds, owners, x_ref, rim_ref, w_ref, bias_ref, move_ref, slot_ref,
    act_ref, b_ref, c_ref, meta,
    edge16, weights, moves, count,
):
    step = pl.program_id(0)
    span = pl.num_programs(0) * BLOCK
    parts = BLOCK // CHUNK
    first = step * BLOCK

    @pl.when(step == 0)
    def _():
        read_docs(bounds, owners, meta, count, shard_ref[0] * span, span)
        edge16[...] = rim_ref[...]
        weights[0:4] = 0.5 * w_ref[...]
        weights[4:5] = 0.5 * bias_ref[...].reshape(1, weights.shape[1])
        moves[0] = move_ref[...]

    choices = []
    for part in range(parts):
        begin = first + part * CHUNK
        near = (meta[0] > begin - 3) & (meta[0] < begin + CHUNK)
        for slot in range(EMAX):
            near = near | ((meta[1 + slot] > begin - 3) & (meta[1 + slot] < begin + CHUNK))

        @pl.when(near)
        def _():
            tick = slot_ref[...] // 4 + begin
            kept = (tick - starts_of(meta, tick) >= slot_ref[...] % 4).astype(F32)
            moves[1 + part, :, :128] = (kept * move_ref[:, :128].astype(F32)).astype(BF16)
            moves[1 + part, :, 128:] = (kept[:, :16] * move_ref[:, 128:].astype(F32)).astype(BF16)

        choices.append(jnp.where(near, 1 + part, 0))

    for part in range(parts):
        low = part * CHUNK
        rows = slice(low, low + CHUNK)
        pick = moves[choices[part]]
        for tile in range(x_ref.shape[1] // 256):
            cols = slice(tile * 256, tile * 256 + 256)
            if part:
                wide = x_ref[low - 16 : low + CHUNK, cols]
            else:
                wide = jnp.concatenate([edge16[:, cols], x_ref[rows, cols]], axis=0)
            moved = jnp.dot(pick, wide, preferred_element_type=F32)
            moved = moved.reshape(CHUNK // 8, 3, 8, 256)
            mixed = weights[4:5, cols] + weights[0:1, cols] * x_ref[rows, cols].astype(F32)
            for lag in range(1, 4):
                mixed = mixed + weights[lag : lag + 1, cols] * moved[:, lag - 1].reshape(CHUNK, 256)
            value = (mixed + mixed * jnp.tanh(mixed)).astype(BF16)
            if tile * 256 < act_ref.shape[1]:
                act_ref[rows, cols] = value
            else:
                b_ref[rows, :] = value[:, :N]
                c_ref[rows, :] = value[:, N:]

    edge16[...] = x_ref[BLOCK - 16 :, :]


def states_kernel(
    meta, act_ref, b_ref, dt_ref, ld_ref, rep_ref, rep16_ref, tri_ref,
    cum_ref, carry_ref, sin_ref, pay_ref,
    state, total,
):
    step = pl.program_id(0)
    heads = dt_ref.shape[0]
    width = rep_ref.shape[1]
    span = pl.num_programs(0) * BLOCK
    parts = BLOCK // CHUNK
    first = step * BLOCK

    @pl.when(step == 0)
    def _():
        state[...] = jnp.zeros_like(state)
        total[...] = jnp.zeros_like(total)

    spans = [slice(part * CHUNK, part * CHUNK + CHUNK) for part in range(parts)]
    pieces = jnp.concatenate([thirds(ld_ref[:, rows] * LOG2E) for rows in spans], axis=0)
    summed = jnp.dot(pieces, tri_ref[...], preferred_element_type=F32)
    open_end = jnp.where(meta[0] < 0, meta[1], -1)
    running = total[...]
    weights = []
    throughs = []
    for part, rows in enumerate(spans):
        begin = first + part * CHUNK
        at = 3 * heads * part
        cum = summed[at : at + heads] + summed[at + heads : at + 2 * heads] + summed[at + 2 * heads : at + 3 * heads]
        cum_ref[:, rows] = cum
        lane = iota((heads, CHUNK), 1) + begin
        carry_ref[:, rows] = jnp.where(lane < open_end, jnp.exp2(running + cum), 0.0)
        start = last_start(meta, begin + CHUNK - 1)
        last = cum[:, CHUNK - 1 :]
        weight = jnp.where(lane >= start, jnp.exp2(last - cum) * dt_ref[:, rows], 0.0)
        weights.append(weight.T.astype(BF16))
        throughs.append(spread_row(jnp.where(start < begin, jnp.exp2(last), 0.0), rep_ref[...]))
        running = running + last
    total[...] = running
    weight = jnp.concatenate(weights, axis=0)
    turned = [b_ref[rows, :].T for rows in spans]
    for tile in range(width // 256):
        cols = slice(tile * 256, tile * 256 + 256)
        scale = jnp.dot(weight, rep16_ref[:heads, cols], preferred_element_type=F32)
        load = scale.astype(BF16) * act_ref[:, cols]
        held = state[:, cols]
        for part, rows in enumerate(spans):
            sin_ref[part, :, cols] = held.astype(BF16)
            grown = jnp.dot(turned[part], load[rows], preferred_element_type=F32)
            held = throughs[part][:, cols] * held + grown
        state[:, cols] = held

    @pl.when(step == pl.num_programs(0) - 1)
    def _():
        start = last_start(meta, span - 1)
        gate = spread_row(jnp.where(start < 0, jnp.exp2(total[:, :1]), 0.0), rep_ref[...])
        gate = jnp.broadcast_to(gate, (PAY - N, width))
        high = gate.astype(BF16).astype(F32)
        pay_ref[:N] = state[...].astype(BF16)
        pay_ref[N:] = jnp.where(iota((PAY - N, width), 0) == 0, high, gate - high).astype(BF16)


def finals_kernel(
    meta, act_hbm, b_hbm, sin_hbm, x_hbm, rim_ref, dt_ref, cum_ref, carry_ref, rep_ref, rep16_ref,
    fin_hbm, first_ref,
    act_held, b_held, sin_held, x_held, edge_held, blank, made, lines, in_sem, blank_sem, made_sem,
):
    heads, span = dt_ref.shape
    width = rep_ref.shape[1]

    def place(slot):
        return pl.multiple_of((meta[1 + slot] - 1) // CHUNK * CHUNK, CHUNK)

    def copies(slot):
        low = place(slot)
        rows = pl.ds(low, CHUNK)
        before = pl.ds(pl.multiple_of(jnp.maximum(low - 16, 0), 16), 16)
        pairs = (
            (act_hbm.at[rows], act_held), (b_hbm.at[rows], b_held), (sin_hbm.at[low // CHUNK], sin_held),
            (x_hbm.at[rows], x_held), (x_hbm.at[before], edge_held),
        )
        return [
            pltpu.make_async_copy(source, target.at[slot], in_sem.at[slot, index])
            for index, (source, target) in enumerate(pairs)
        ]

    def fetch(slot, _):
        for copy in copies(slot):
            copy.start()
        return 0

    found = jnp.int32(0)
    for slot in range(EMAX):
        found = found + (meta[1 + slot] <= span).astype(jnp.int32)
    lax.fori_loop(0, found, fetch, 0)
    blank[...] = jnp.zeros_like(blank)
    blanks = [
        pltpu.make_async_copy(blank, fin_hbm.at[index], blank_sem.at[index])
        for index in range(fin_hbm.shape[0])
    ]
    for copy in blanks:
        copy.start()
    first_ref[...] = jnp.zeros_like(first_ref)
    lines[...] = jnp.zeros_like(lines)
    for copy in blanks:
        copy.wait()

    def finish(slot, _):
        for copy in copies(slot):
            copy.wait()
        end = meta[1 + slot]
        start = jnp.where(slot > 0, meta[jnp.maximum(slot, 1)], meta[0])
        low = place(slot)
        there = pl.ds(low, CHUNK)
        lane = iota((heads, CHUNK), 1) + low
        cum = cum_ref[:, there]
        at_end = jnp.sum(jnp.where(lane == end - 1, cum, 0.0), axis=1, keepdims=True)
        inside = (lane < end) & (lane >= start)
        weight = jnp.exp2(jnp.minimum(at_end - cum, 0.0)) * dt_ref[:, there]
        weight = jnp.where(inside, weight, 0.0).T.astype(BF16)
        scale = jnp.dot(weight, rep16_ref[:heads], preferred_element_type=F32)
        load = scale.astype(BF16) * act_held[slot]
        local = outer_dot(b_held[slot], load)
        through = spread_row(jnp.where(start < low, jnp.exp2(at_end), 0.0), rep_ref[...])
        final = local + through * sin_held[slot].astype(F32)
        target = meta[5 + slot]

        @pl.when((slot == 0) & (start < 0))
        def _():
            opened = jnp.sum(jnp.where(lane == end - 1, carry_ref[:, there], 0.0), axis=1, keepdims=True)
            first_ref[...] = jnp.broadcast_to(spread_row(opened, rep_ref[...]), first_ref.shape)

        row = iota((16, CHUNK), 0)
        col = iota((16, CHUNK), 1) + low
        pick = (col == end - 3 + row) & (col >= start) & (row < 3)
        row16 = iota((16, 16), 0)
        col16 = iota((16, 16), 1) + low - 16
        pick16 = (col16 == end - 3 + row16) & (col16 >= start) & (row16 < 3)
        rim = jnp.where(low > 0, edge_held[slot].astype(F32), rim_ref[...].astype(F32))
        last = jnp.dot(
            pick.astype(F32).astype(BF16), x_held[slot], preferred_element_type=F32
        ) + jnp.dot(pick16.astype(F32).astype(BF16), rim.astype(BF16), preferred_element_type=F32)
        tiles = x_held.shape[2] // 128
        for index in range(3):
            for tile in range(tiles):
                at = index * tiles + tile
                lines[at : at + 1] = last[index : index + 1, tile * 128 : tile * 128 + 128]

        @pl.when(target >= 0)
        def _():
            made[slot, :width] = final.astype(BF16).T
            made[slot, width:] = lines[...].astype(BF16)
            pltpu.make_async_copy(made.at[slot], fin_hbm.at[target], made_sem.at[slot]).start()

        return 0

    lax.fori_loop(0, found, finish, 0)

    def close(slot, _):
        @pl.when(meta[5 + slot] >= 0)
        def _():
            pltpu.make_async_copy(made.at[slot], fin_hbm.at[meta[5 + slot]], made_sem.at[slot]).wait()

        return 0

    lax.fori_loop(0, found, close, 0)


def output_kernel(origin, late, meta, act_ref, b_ref, c_ref, dt_ref, cum_ref, sin_ref, gain_in, rep_ref, rep16_ref, each_ref, *refs):
    out_ref, gain_ref = refs[-2:]
    step = origin + pl.program_id(0)
    heads = dt_ref.shape[0]
    width = out_ref.shape[1]
    parts = BLOCK // CHUNK

    @pl.when(pl.program_id(0) == 0)
    def _():
        row = jnp.zeros((1, width), F32)
        for head in range(heads):
            row = row + gain_in[head] * rep_ref[head : head + 1, :]
        gain_ref[...] = row

    for part in range(parts):
        begin = step * BLOCK + part * CHUNK
        rows = slice(part * CHUNK, part * CHUNK + CHUNK)
        cum = cum_ref[:, rows]
        back = cum - jnp.log2(dt_ref[:, rows])
        ahead = jnp.concatenate(
            [thirds(cum), jnp.ones((3 * heads, CHUNK), BF16), jnp.zeros((CHUNK - 6 * heads, CHUNK), BF16)], axis=0
        ).T
        back = thirds(-back)
        b_act = b_ref[rows, :]
        c_act = c_ref[rows, :]
        place = iota((CHUNK, CHUNK), 0) + begin
        other = iota((CHUNK, CHUNK), 1) + begin
        scores = lax.dot_general(c_act, b_act, (((1,), (1,)), ((), ())), preferred_element_type=F32)
        scores = jnp.where((other <= place) & (other >= starts_of(meta, place)), scores, 0.0)
        scores = jnp.concatenate([scores, scores], axis=1)
        blank = jnp.zeros((CHUNK - 6 * heads, 256), BF16)
        lane = iota((heads, CHUNK), 1) + begin
        before = jnp.where(last_start(meta, begin) < begin, next_end(meta, begin), -1)
        entry = jnp.where(lane < before, jnp.exp2(cum), 0.0)
        entry = jnp.concatenate([entry, entry - entry.astype(BF16).astype(F32)], axis=0).T.astype(BF16)
        if late:
            extra = refs[0][:, rows]
            extra = jnp.concatenate([extra, extra - extra.astype(BF16).astype(F32)], axis=0).T.astype(BF16)
        left_half = iota((CHUNK, 128), 1) < P_SIZE
        for quad in range(heads // 4):
            cols = slice(quad * 256, quad * 256 + 256)
            outer = jnp.dot(c_act, sin_ref[part, :, cols], preferred_element_type=F32)
            scale = jnp.dot(entry, rep16_ref[:, cols], preferred_element_type=F32)
            sums = []
            for pair in (2 * quad, 2 * quad + 1):
                own = each_ref[:, pair * 256 : pair * 256 + 256]
                against = jnp.concatenate([own, jnp.concatenate([back, back], axis=1) * own, blank], axis=0)
                spread = jnp.dot(ahead, against, preferred_element_type=F32)
                mix = (jnp.exp2(jnp.minimum(spread, 0.0)) * scores).astype(BF16)
                x_pair = act_ref[rows, pair * 128 : pair * 128 + 128]
                zero = jnp.zeros_like(x_pair)
                split = jnp.concatenate(
                    [jnp.where(left_half, x_pair, zero), jnp.where(left_half, zero, x_pair)], axis=0
                )
                sums.append(jnp.dot(mix, split, preferred_element_type=F32))
            inner = jnp.concatenate(sums, axis=1)
            value = inner + scale * outer + gain_ref[:, cols] * act_ref[rows, cols].astype(F32)
            if late:
                outer = jnp.dot(c_act, refs[1][:, cols], preferred_element_type=F32)
                scale = jnp.dot(extra, rep16_ref[:, cols], preferred_element_type=F32)
                value = value + scale * outer
            out_ref[rows, cols] = value.astype(BF16)


def gates_of(pay_ref, cols):
    gates = pay_ref[N:, cols].astype(F32)
    return gates[0:1] + gates[1:2]


def pair_kernel(shard_ref, own_ref, got_ref, half_ref):
    side = half_ref.shape[1]

    def join(early, late, cols):
        after = gates_of(late, cols)
        gate = jnp.broadcast_to(after * gates_of(early, cols), (PAY - N, side))
        high = gate.astype(BF16).astype(F32)
        half_ref[:N] = (late[:N, cols].astype(F32) + after * early[:N, cols].astype(F32)).astype(BF16)
        half_ref[N:] = jnp.where(iota((PAY - N, side), 0) == 0, high, gate - high).astype(BF16)

    @pl.when(shard_ref[0] % 2 == 0)
    def _():
        join(own_ref, got_ref, slice(0, side))

    @pl.when(shard_ref[0] % 2 == 1)
    def _():
        join(got_ref, own_ref, slice(side, 2 * side))


def prefix_kernel(*refs):
    prefix_ref = refs[-1]
    side = prefix_ref.shape[1]
    total = jnp.zeros((N, side), F32)
    for ref in refs[:-1]:
        total = gates_of(ref, slice(0, side)) * total + ref[:N].astype(F32)
    prefix_ref[...] = total.astype(BF16)


def carry_kernel(shard_ref, stream_ref, meta, mine_ref, other_ref, early_ref, first_ref, carried_ref, *sends):
    side = mine_ref.shape[1]
    lower, upper = slice(0, side), slice(side, 2 * side)

    @pl.when(shard_ref[0] % 2 == 0)
    def _():
        carried_ref[:, lower] = mine_ref[...]
        carried_ref[:, upper] = other_ref[...]

    @pl.when(shard_ref[0] % 2 == 1)
    def _():
        for cols, part in ((lower, other_ref), (upper, mine_ref)):
            carried_ref[:, cols] = (
                early_ref[:N, cols].astype(F32) + gates_of(early_ref, cols) * part[...].astype(F32)
            ).astype(BF16)

    value = (first_ref[0:1] * carried_ref[...].astype(F32)).T.astype(BF16)
    apart = (meta[5] // CAP) ^ stream_ref[0]
    for index, ref in enumerate(sends):
        ref[...] = jnp.where(apart == index, value, jnp.zeros_like(value))


def correct_kernel(meta, base_hbm, c_ref, carry_ref, carried_ref, rep16_ref, out_hbm, held, in_sem, out_sem):
    steps, _, width = held.shape
    reach = jnp.where(meta[0] < 0, jnp.minimum(meta[1], steps * BLOCK), 0)
    touched = (reach + BLOCK - 1) // BLOCK

    def copy(index, source, target, sem):
        place = pl.ds(pl.multiple_of(index * BLOCK, BLOCK), BLOCK)
        if source is held:
            return pltpu.make_async_copy(held.at[index], target.at[place], sem.at[index])
        return pltpu.make_async_copy(source.at[place], held.at[index], sem.at[index])

    def fetch(index, _):
        copy(index, base_hbm, held, in_sem).start()
        return 0

    def add(index, _):
        copy(index, base_hbm, held, in_sem).wait()
        rows = pl.ds(pl.multiple_of(index * BLOCK, BLOCK), BLOCK)
        entry = carry_ref[:, rows]
        entry = jnp.concatenate([entry, entry - entry.astype(BF16).astype(F32)], axis=0).T.astype(BF16)
        c_act = c_ref[rows, :]
        for tile in range(width // 256):
            cols = slice(tile * 256, tile * 256 + 256)
            outer = jnp.dot(c_act, carried_ref[:, cols], preferred_element_type=F32)
            scale = jnp.dot(entry, rep16_ref[:, cols], preferred_element_type=F32)
            held[index, :, cols] = (held[index, :, cols].astype(F32) + scale * outer).astype(BF16)
        copy(index, held, out_hbm, out_sem).start()
        return 0

    def close(index, _):
        copy(index, held, out_hbm, out_sem).wait()
        return 0

    lax.fori_loop(0, touched, fetch, 0)
    lax.fori_loop(0, touched, add, 0)
    lax.fori_loop(0, touched, close, 0)


def params(mib):
    return pltpu.CompilerParams(vmem_limit_bytes=mib * MIB)


def whole(shape):
    return pl.BlockSpec(shape, lambda *_: (0,) * len(shape))


def on_device(
    conv_input, conv_weight, conv_bias, step_size, log_decay, skip_gain, doc_bounds, doc_owner
):
    span, channels = conv_input.shape[1:]
    heads = step_size.shape[1]
    width = heads * P_SIZE
    steps = span // BLOCK
    chunks = span // CHUNK
    owners = lax.axis_size("stream")
    slots = owners * CAP
    rows = width + TAIL
    shard = lax.axis_index("seq").astype(jnp.int32).reshape(1)
    rows_in = conv_input[0]
    rim = shifted(rows_in[span - 16 :], "seq", 1)
    rep = (np.arange(width)[None, :] // P_SIZE == np.arange(heads)[:, None]).astype(np.float32)
    rep16 = np.concatenate([rep, rep], 0).astype(BF16)
    each = np.arange(heads * CHUNK)[None, :] // CHUNK == np.arange(3 * heads)[:, None] % heads
    each = each.astype(BF16)
    ticks = np.arange(CHUNK)
    tri = (ticks[:, None] <= ticks[None, :]).astype(BF16)
    order = np.arange(3 * CHUNK)
    tick, lag = 8 * (order // 24) + order % 8, order % 24 // 8 + 1
    source = np.arange(CHUNK + 16)
    move = (source[None, :] - 16 == (tick - lag)[:, None]).astype(BF16)
    slot = np.broadcast_to((4 * tick + lag)[:, None], (3 * CHUNK, 128)).astype(np.int32)
    smem = pl.BlockSpec(memory_space=pltpu.SMEM)
    stream = lax.axis_index("stream").astype(jnp.int32).reshape(1)
    per_head = pl.BlockSpec((heads, BLOCK), lambda i, *_: (0, i))
    prefetch = functools.partial(pltpu.PrefetchScalarGridSpec, num_scalar_prefetch=1)
    by_rows = pl.BlockSpec((BLOCK, channels), lambda i, *_: (i, 0))
    by_width = pl.BlockSpec((BLOCK, width), lambda i, *_: (i, 0))
    by_rest = pl.BlockSpec((BLOCK, N), lambda i, *_: (i, 0))
    act, b_act, c_act, meta = pl.pallas_call(
        conv_kernel,
        grid=(steps,),
        in_specs=[
            smem, smem, smem, by_rows, whole((16, channels)),
            whole((4, channels)), whole((channels,)), whole(move.shape), whole(slot.shape),
        ],
        out_specs=[by_width, by_rest, by_rest, smem],
        out_shape=[
            jax.ShapeDtypeStruct((span, width), BF16),
            jax.ShapeDtypeStruct((span, N), BF16),
            jax.ShapeDtypeStruct((span, N), BF16),
            jax.ShapeDtypeStruct((16,), jnp.int32),
        ],
        scratch_shapes=[
            pltpu.VMEM((16, channels), BF16),
            pltpu.VMEM((8, channels), F32),
            pltpu.VMEM((1 + BLOCK // CHUNK,) + move.shape, BF16),
            pltpu.SMEM((owners,), jnp.int32),
        ],
        compiler_params=params(60),
        cost_estimate=pl.CostEstimate(
            flops=2 * span * channels * 400, bytes_accessed=21 << 20, transcendentals=span * channels
        ),
        name="conv",
    )(shard, doc_bounds, doc_owner, rows_in, rim, conv_weight, conv_bias, move, slot)
    in_hbm = pl.BlockSpec(memory_space=pl.ANY)
    cum, carry, sin, pay = pl.pallas_call(
        states_kernel,
        grid_spec=prefetch(
            grid=(steps,),
            in_specs=[
                by_width, by_rest, per_head, per_head,
                whole((heads, width)), whole((2 * heads, width)), whole((CHUNK, CHUNK)),
            ],
            out_specs=[
                per_head, per_head,
                pl.BlockSpec((BLOCK // CHUNK, N, width), lambda i, *_: (i, 0, 0)),
                whole((PAY, width)),
            ],
            scratch_shapes=[
                pltpu.VMEM((N, width), F32),
                pltpu.VMEM((heads, CHUNK), F32),
            ],
        ),
        out_shape=[
            jax.ShapeDtypeStruct((heads, span), F32),
            jax.ShapeDtypeStruct((heads, span), F32),
            jax.ShapeDtypeStruct((chunks, N, width), BF16),
            jax.ShapeDtypeStruct((PAY, width), BF16),
        ],
        compiler_params=params(60),
        cost_estimate=pl.CostEstimate(
            flops=2 * span * width * N * 2, bytes_accessed=22 << 20, transcendentals=span * heads
        ),
        name="states",
    )(meta, act, b_act, step_size[0], log_decay[0], rep, rep16, tri)


    def outputs(first, last, late=()):
        rows_of = functools.partial(pl.BlockSpec, index_map=lambda i, *_: (first + i, 0))
        heads_of = pl.BlockSpec((heads, BLOCK), lambda i, *_: (0, first + i))
        return pl.pallas_call(
            functools.partial(output_kernel, first, bool(late)),
            grid_spec=prefetch(
                grid=(last - first,),
                in_specs=[
                    rows_of((BLOCK, width)), rows_of((BLOCK, N)), rows_of((BLOCK, N)), heads_of, heads_of,
                    pl.BlockSpec((BLOCK // CHUNK, N, width), lambda i, *_: (first + i, 0, 0)),
                    smem, whole((heads, width)), whole((2 * heads, width)), whole(each.shape),
                ] + ([heads_of, whole((N, width)), pl.BlockSpec(memory_space=pl.ANY)] if late else []),
                out_specs=rows_of((BLOCK, width)),
                scratch_shapes=[pltpu.VMEM((1, width), F32)],
            ),
            out_shape=jax.ShapeDtypeStruct((span, width), BF16),
            input_output_aliases={13: 0} if late else {},
            compiler_params=params(60),
            cost_estimate=pl.CostEstimate(
                flops=2 * (last - first) * BLOCK * width * N * 4,
                bytes_accessed=(last - first) * (4 << 20),
                transcendentals=(last - first) * BLOCK * CHUNK * heads,
            ),
            name="outputs",
        )(meta, act, b_act, c_act, step_size[0], cum, sin, skip_gain, rep, rep16, each, *late)

    side = width // 2
    count = lax.axis_size("seq")
    pairs = [(index, index ^ 1) for index in range(count)]
    early = lax.ppermute(pay, "seq", pairs)
    half = pl.pallas_call(
        pair_kernel,
        in_specs=[smem, whole((PAY, width)), whole((PAY, width))],
        out_specs=whole((PAY, side)),
        out_shape=jax.ShapeDtypeStruct((PAY, side), BF16),
        compiler_params=params(8),
        name="pair",
    )(shard, pay, early)
    chips = count // 2
    behind = [shifted(half, "seq", 2 * far) for far in range(chips - 1, 0, -1)]
    scanned, half = lax.optimization_barrier((sin, half))
    fin, first = pl.pallas_call(
        finals_kernel,
        in_specs=[
            smem, in_hbm, in_hbm, in_hbm, in_hbm, whole((16, channels)),
            whole((heads, span)), whole((heads, span)), whole((heads, span)),
            whole((heads, width)), whole((2 * heads, width)),
        ],
        out_specs=[in_hbm, whole((8, width))],
        out_shape=[
            jax.ShapeDtypeStruct((slots, rows, N), BF16),
            jax.ShapeDtypeStruct((8, width), F32),
        ],
        scratch_shapes=[
            pltpu.VMEM((EMAX, CHUNK, width), BF16),
            pltpu.VMEM((EMAX, CHUNK, N), BF16),
            pltpu.VMEM((EMAX, N, width), BF16),
            pltpu.VMEM((EMAX, CHUNK, channels), BF16),
            pltpu.VMEM((EMAX, 16, channels), BF16),
            pltpu.VMEM((rows, N), BF16),
            pltpu.VMEM((EMAX, rows, N), BF16),
            pltpu.VMEM((TAIL, N), F32),
            pltpu.SemaphoreType.DMA((EMAX, 5)),
            pltpu.SemaphoreType.DMA((slots,)),
            pltpu.SemaphoreType.DMA((EMAX,)),
        ],
        compiler_params=params(58),
        cost_estimate=pl.CostEstimate(flops=1 << 28, bytes_accessed=6 << 20, transcendentals=0),
        name="finals",
    )(meta, act, b_act, scanned, rows_in, rim, step_size[0], cum, carry, rep, rep16)
    sin, fin = lax.optimization_barrier((sin, fin))
    got = lax.all_to_all(
        fin.reshape(owners, CAP, rows, N), "stream", split_axis=0, concat_axis=0, tiled=True
    )
    base = outputs(0, steps)
    *behind, base = lax.optimization_barrier((*behind, base))
    mine = pl.pallas_call(
        prefix_kernel,
        in_specs=[whole((PAY, side))] * len(behind),
        out_specs=whole((N, side)),
        out_shape=jax.ShapeDtypeStruct((N, side), BF16),
        compiler_params=params(8),
        name="prefix",
    )(*behind)
    other = lax.ppermute(mine, "seq", pairs)
    other, got = lax.optimization_barrier((other, got))
    carried, *send = pl.pallas_call(
        carry_kernel,
        in_specs=[smem, smem, smem, whole((N, side)), whole((N, side)), whole((PAY, width)), whole((8, width))],
        out_specs=[whole((N, width))] + [whole((width, N))] * owners,
        out_shape=[jax.ShapeDtypeStruct((N, width), BF16)]
        + [jax.ShapeDtypeStruct((width, N), BF16)] * owners,
        compiler_params=params(8),
        name="carry",
    )(shard, stream, meta, mine, other, early, first)
    more = [send[0]]
    for apart in range(1, owners):
        swap = [(index, index ^ apart) for index in range(owners)]
        more.append(lax.ppermute(send[apart], "stream", swap))

    out = pl.pallas_call(
        correct_kernel,
        in_specs=[smem, in_hbm, whole((span, N)), whole((heads, span)), whole((N, width)), whole((2 * heads, width))],
        out_specs=in_hbm,
        out_shape=jax.ShapeDtypeStruct((span, width), BF16),
        scratch_shapes=[
            pltpu.VMEM((steps, BLOCK, width), BF16),
            pltpu.SemaphoreType.DMA((steps,)),
            pltpu.SemaphoreType.DMA((steps,)),
        ],
        input_output_aliases={1: 0},
        compiler_params=params(58),
        cost_estimate=pl.CostEstimate(
            flops=2 * span * width * N, bytes_accessed=18 << 20, transcendentals=0
        ),
        name="correct",
    )(meta, base, c_act, carry, carried, rep16)

    apart = (jnp.arange(owners) ^ stream)[:, None, None]
    extra = jnp.broadcast_to(more[0][None], (owners, width, N))
    for index in range(1, owners):
        extra = jnp.where(apart == index, more[index][None], extra)
    ranks = jnp.arange(CAP)[None, :, None, None]
    extra = jnp.where(ranks == 0, extra[:, None], jnp.zeros_like(extra[:, None]))
    ssm = got[:, :, :width].astype(F32) + extra.astype(F32)
    ssm = ssm.reshape(1, 1, owners, CAP, heads, P_SIZE, N)
    tiles = channels // N
    conv = got[:, :, width : width + 3 * tiles].reshape(1, 1, owners, CAP, 3, channels)
    return out[None], ssm, conv


def solution(mesh):
    in_specs = (
        P("stream", "seq", None),
        P(),
        P(),
        P("stream", None, "seq"),
        P("stream", None, "seq"),
        P(),
        P("stream", None),
        P("stream", None),
    )
    out_specs = (
        P("stream", "seq", None),
        P("stream", "seq", None, None, None, None, None),
        P("stream", "seq", None, None, None, None),
    )
    return jax.shard_map(
        on_device, mesh=mesh, in_specs=in_specs, out_specs=out_specs, check_vma=False
    )
```

```python
import functools

import jax
import jax.numpy as jnp
import numpy as np
from jax import lax
from jax.experimental import pallas as pl
from jax.experimental.pallas import tpu as pltpu
from jax.sharding import PartitionSpec as P

P_SIZE = 64
N = 128
EMAX = 4
CAP = 2
CHUNK = 128
BLOCK = 512
FAR = 1 << 30
LOG2E = 1.4426950408889634
PAY = 144
TAIL = 32
MIB = 1024 * 1024

F32 = jnp.float32
BF16 = jnp.bfloat16


def shifted(value, axis, steps):
    count = lax.axis_size(axis)
    leading, last = (max(0, -steps), min(count, count - steps))
    return lax.ppermute(value, axis, [(source, source + steps) for source in range(leading, last)])


def iota(shape, axis):
    return lax.broadcasted_iota(jnp.int32, shape, axis)


def outer_dot(left, right):
    return lax.dot_general(left, right, (((0,), (0,)), ((), ())), preferred_element_type=F32)


def halves(value):
    high = value.astype(BF16)
    low = (value - high.astype(F32)).astype(BF16)
    return jnp.concatenate([high, low], axis=0)


def thirds(value):
    high = value.astype(BF16)
    rest = value - high.astype(F32)
    mid = rest.astype(BF16)
    low = (rest - mid.astype(F32)).astype(BF16)
    return jnp.concatenate([high, mid, low], axis=0)


def spread_row(column, rep):
    return jnp.sum(rep * column, axis=0, keepdims=True)


def last_start(meta, place):
    start = meta[0]
    for slot in range(EMAX):
        end = meta[1 + slot]
        start = jnp.where(end <= place, end, start)
    return start


def next_end(meta, place):
    end = FAR
    for slot in reversed(range(EMAX)):
        end = jnp.where(meta[1 + slot] > place, meta[1 + slot], end)
    return end


def starts_of(meta, rows):
    start = jnp.full(rows.shape, meta[0], jnp.int32)
    for slot in range(EMAX):
        end = meta[1 + slot]
        start = jnp.where(rows >= end, end, start)
    return start


def read_docs(bounds, owners, meta, count, anchor, span):
    for slot in range(EMAX):
        meta[1 + slot] = FAR
        meta[5 + slot] = 0
    for owner in range(count.shape[0]):
        count[owner] = 0

    def one(index, carry):
        found, prior, start = carry
        end = bounds[0, index]
        owner = owners[0, index]
        mine = (end > prior) & (end > anchor) & (end <= anchor + span) & (found < EMAX)

        @pl.when(mine)
        def _():
            meta[1 + found] = end - anchor
            rank = count[owner]
            meta[5 + found] = jnp.where(rank < CAP, owner * CAP + rank, -1)
            count[owner] = rank + 1

        return found + mine.astype(jnp.int32), end, jnp.where(end <= anchor, end, start)

    zero = jnp.int32(0)
    _, _, start = lax.fori_loop(0, bounds.shape[1], one, (zero, zero, zero))
    meta[0] = start - anchor


def states_kernel(
    shard_ref, bounds, owners, x_ref, rim_ref, w_ref, bias_ref, move_ref, slot_ref,
    dt_ref, ld_ref, rep_ref, rep16_ref, tri_ref,
    act_ref, b_ref, c_ref, cum_ref, carry_ref, sin_ref, pay_ref, meta,
    edge16, weights, moves, state, total, count,
):
    step = pl.program_id(0)
    heads = dt_ref.shape[0]
    width = rep_ref.shape[1]
    span = pl.num_programs(0) * BLOCK
    parts = BLOCK // CHUNK
    first = step * BLOCK

    @pl.when(step == 0)
    def _():
        read_docs(bounds, owners, meta, count, shard_ref[0] * span, span)
        edge16[...] = rim_ref[...]
        weights[0:4] = 0.5 * w_ref[...]
        weights[4:5] = 0.5 * bias_ref[...].reshape(1, weights.shape[1])
        moves[0] = move_ref[...]
        state[...] = jnp.zeros_like(state)
        total[...] = jnp.zeros_like(total)

    choices = []
    for part in range(parts):
        begin = first + part * CHUNK
        near = (meta[0] > begin - 3) & (meta[0] < begin + CHUNK)
        for slot in range(EMAX):
            near = near | ((meta[1 + slot] > begin - 3) & (meta[1 + slot] < begin + CHUNK))

        @pl.when(near)
        def _():
            tick = slot_ref[...] // 4 + begin
            kept = (tick - starts_of(meta, tick) >= slot_ref[...] % 4).astype(F32)
            moves[1 + part, :, :128] = (kept * move_ref[:, :128].astype(F32)).astype(BF16)
            moves[1 + part, :, 128:] = (kept[:, :16] * move_ref[:, 128:].astype(F32)).astype(BF16)

        choices.append(jnp.where(near, 1 + part, 0))

    for part in range(parts):
        low = part * CHUNK
        rows = slice(low, low + CHUNK)
        pick = moves[choices[part]]
        for tile in range(x_ref.shape[1] // 256):
            cols = slice(tile * 256, tile * 256 + 256)
            if part:
                wide = x_ref[low - 16 : low + CHUNK, cols]
            else:
                wide = jnp.concatenate([edge16[:, cols], x_ref[rows, cols]], axis=0)
            moved = jnp.dot(pick, wide, preferred_element_type=F32)
            moved = moved.reshape(CHUNK // 8, 3, 8, 256)
            mixed = weights[4:5, cols] + weights[0:1, cols] * x_ref[rows, cols].astype(F32)
            for lag in range(1, 4):
                mixed = mixed + weights[lag : lag + 1, cols] * moved[:, lag - 1].reshape(CHUNK, 256)
            value = (mixed + mixed * jnp.tanh(mixed)).astype(BF16)
            if tile * 256 < act_ref.shape[1]:
                act_ref[rows, cols] = value
            else:
                b_ref[rows, :] = value[:, :N]
                c_ref[rows, :] = value[:, N:]

    edge16[...] = x_ref[BLOCK - 16 :, :]

    spans = [slice(part * CHUNK, part * CHUNK + CHUNK) for part in range(parts)]
    pieces = jnp.concatenate([thirds(ld_ref[:, rows] * LOG2E) for rows in spans], axis=0)
    summed = jnp.dot(pieces, tri_ref[...], preferred_element_type=F32)
    open_end = jnp.where(meta[0] < 0, meta[1], -1)
    running = total[...]
    scales = []
    throughs = []
    for part, rows in enumerate(spans):
        begin = first + part * CHUNK
        at = 3 * heads * part
        cum = summed[at : at + heads] + summed[at + heads : at + 2 * heads] + summed[at + 2 * heads : at + 3 * heads]
        cum_ref[:, rows] = cum
        lane = iota((heads, CHUNK), 1) + begin
        carry_ref[:, rows] = jnp.where(lane < open_end, jnp.exp2(running + cum), 0.0)
        start = last_start(meta, begin + CHUNK - 1)
        last = cum[:, CHUNK - 1 :]
        weight = jnp.where(lane >= start, jnp.exp2(last - cum) * dt_ref[:, rows], 0.0)
        scales.append(weight.T.astype(BF16))
        throughs.append(spread_row(jnp.where(start < begin, jnp.exp2(last), 0.0), rep_ref[...]))
        running = running + last
    total[...] = running
    weight = jnp.concatenate(scales, axis=0)
    turned = [b_ref[rows, :].T for rows in spans]
    for tile in range(width // 256):
        cols = slice(tile * 256, tile * 256 + 256)
        scale = jnp.dot(weight, rep16_ref[:heads, cols], preferred_element_type=F32)
        load = scale.astype(BF16) * act_ref[:, cols]
        held = state[:, cols]
        for part, rows in enumerate(spans):
            sin_ref[part, :, cols] = held.astype(BF16)
            grown = jnp.dot(turned[part], load[rows], preferred_element_type=F32)
            held = throughs[part][:, cols] * held + grown
        state[:, cols] = held

    @pl.when(step == pl.num_programs(0) - 1)
    def _():
        start = last_start(meta, span - 1)
        gate = spread_row(jnp.where(start < 0, jnp.exp2(total[:, :1]), 0.0), rep_ref[...])
        gate = jnp.broadcast_to(gate, (PAY - N, width))
        high = gate.astype(BF16).astype(F32)
        pay_ref[:N] = state[...].astype(BF16)
        pay_ref[N:] = jnp.where(iota((PAY - N, width), 0) == 0, high, gate - high).astype(BF16)


def finals_kernel(
    meta, act_hbm, b_hbm, sin_hbm, x_hbm, rim_ref, dt_ref, cum_ref, carry_ref, rep_ref, rep16_ref,
    fin_hbm, first_ref,
    act_held, b_held, sin_held, x_held, edge_held, blank, made, lines, in_sem, blank_sem, made_sem,
):
    heads, span = dt_ref.shape
    width = rep_ref.shape[1]

    def place(slot):
        return pl.multiple_of((jnp.minimum(meta[1 + slot], span) - 1) // CHUNK * CHUNK, CHUNK)

    def copies(slot):
        low = place(slot)
        rows = pl.ds(low, CHUNK)
        before = pl.ds(pl.multiple_of(jnp.maximum(low - 16, 0), 16), 16)
        pairs = (
            (act_hbm.at[rows], act_held), (b_hbm.at[rows], b_held), (sin_hbm.at[low // CHUNK], sin_held),
            (x_hbm.at[rows], x_held), (x_hbm.at[before], edge_held),
        )
        return [
            pltpu.make_async_copy(source, target.at[slot], in_sem.at[slot, index])
            for index, (source, target) in enumerate(pairs)
        ]

    fetched = [copies(slot) for slot in range(EMAX)]
    for copy in sum(fetched, []):
        copy.start()
    blank[...] = jnp.zeros_like(blank)
    blanks = [
        pltpu.make_async_copy(blank, fin_hbm.at[index], blank_sem.at[index])
        for index in range(fin_hbm.shape[0])
    ]
    for copy in blanks:
        copy.start()
    lines[...] = jnp.zeros_like(lines)
    for copy in sum(fetched, []):
        copy.wait()
    for slot in range(EMAX):
        end = meta[1 + slot]
        start = meta[slot]
        low = place(slot)
        there = pl.ds(low, CHUNK)
        lane = iota((heads, CHUNK), 1) + low
        cum = cum_ref[:, there]
        at_end = jnp.sum(jnp.where(lane == end - 1, cum, 0.0), axis=1, keepdims=True)
        inside = (lane < end) & (lane >= start)
        weight = jnp.exp2(jnp.minimum(at_end - cum, 0.0)) * dt_ref[:, there]
        weight = jnp.where(inside, weight, 0.0).T.astype(BF16)
        scale = jnp.dot(weight, rep16_ref[:heads], preferred_element_type=F32)
        load = scale.astype(BF16) * act_held[slot]
        local = outer_dot(b_held[slot], load)
        through = spread_row(jnp.where(start < low, jnp.exp2(at_end), 0.0), rep_ref[...])
        final = local + through * sin_held[slot].astype(F32)
        if slot == 0:
            opened = jnp.sum(jnp.where(lane == end - 1, carry_ref[:, there], 0.0), axis=1, keepdims=True)
            first_ref[...] = jnp.broadcast_to(spread_row(opened, rep_ref[...]), first_ref.shape)
        row = iota((16, CHUNK), 0)
        col = iota((16, CHUNK), 1) + low
        pick = (col == end - 3 + row) & (col >= start) & (row < 3)
        row16 = iota((16, 16), 0)
        col16 = iota((16, 16), 1) + low - 16
        pick16 = (col16 == end - 3 + row16) & (col16 >= start) & (row16 < 3)
        rim = jnp.where(low > 0, edge_held[slot].astype(F32), rim_ref[...].astype(F32))
        last = jnp.dot(
            pick.astype(F32).astype(BF16), x_held[slot], preferred_element_type=F32
        ) + jnp.dot(pick16.astype(F32).astype(BF16), rim.astype(BF16), preferred_element_type=F32)
        tiles = x_held.shape[2] // 128
        for index in range(3):
            for tile in range(tiles):
                at = index * tiles + tile
                lines[slot, at : at + 1] = last[index : index + 1, tile * 128 : tile * 128 + 128]

        made[slot, :width] = final.astype(BF16).T
        made[slot, width:] = lines[slot].astype(BF16)
    for copy in blanks:
        copy.wait()
    used = [(meta[1 + slot] <= span) & (meta[5 + slot] >= 0) for slot in range(EMAX)]

    def send(slot):
        return pltpu.make_async_copy(made.at[slot], fin_hbm.at[meta[5 + slot]], made_sem.at[slot])

    for slot in range(EMAX):

        @pl.when(used[slot])
        def _():
            send(slot).start()

    for slot in range(EMAX):

        @pl.when(used[slot])
        def _():
            send(slot).wait()


def output_kernel(origin, late, meta, act_ref, b_ref, c_ref, dt_ref, cum_ref, sin_ref, gain_in, rep_ref, rep16_ref, *refs):
    out_ref, gain_ref = refs[-2:]
    step = origin + pl.program_id(0)
    heads = dt_ref.shape[0]
    width = out_ref.shape[1]
    parts = BLOCK // CHUNK

    @pl.when(pl.program_id(0) == 0)
    def _():
        row = jnp.zeros((1, width), F32)
        for head in range(heads):
            row = row + gain_in[head] * rep_ref[head : head + 1, :]
        gain_ref[...] = row

    for part in range(parts):
        begin = step * BLOCK + part * CHUNK
        rows = slice(part * CHUNK, part * CHUNK + CHUNK)
        cum = cum_ref[:, rows]
        back = cum - jnp.log2(dt_ref[:, rows])
        ahead = cum.T
        b_act = b_ref[rows, :]
        c_act = c_ref[rows, :]
        place = iota((CHUNK, CHUNK), 0) + begin
        other = iota((CHUNK, CHUNK), 1) + begin
        scores = lax.dot_general(c_act, b_act, (((1,), (1,)), ((), ())), preferred_element_type=F32)
        scores = jnp.where((other <= place) & (other >= starts_of(meta, place)), scores, 0.0)
        lane = iota((heads, CHUNK), 1) + begin
        before = jnp.where(last_start(meta, begin) < begin, next_end(meta, begin), -1)
        entry = jnp.where(lane < before, jnp.exp2(cum), 0.0)
        entry = jnp.concatenate([entry, entry - entry.astype(BF16).astype(F32)], axis=0).T.astype(BF16)
        if late:
            extra = refs[0][:, rows]
            extra = jnp.concatenate([extra, extra - extra.astype(BF16).astype(F32)], axis=0).T.astype(BF16)
        left_half = iota((CHUNK, 128), 1) < P_SIZE
        for quad in range(heads // 4):
            cols = slice(quad * 256, quad * 256 + 256)
            outer = jnp.dot(c_act, sin_ref[part, :, cols], preferred_element_type=F32)
            scale = jnp.dot(entry, rep16_ref[:, cols], preferred_element_type=F32)
            sums = []
            for pair in (2 * quad, 2 * quad + 1):
                mixes = []
                for head in (2 * pair, 2 * pair + 1):
                    spread = jnp.minimum(ahead[:, head : head + 1] - back[head : head + 1, :], 0.0)
                    mixes.append((jnp.exp2(spread) * scores).astype(BF16))
                mix = jnp.concatenate(mixes, axis=1)
                x_pair = act_ref[rows, pair * 128 : pair * 128 + 128]
                zero = jnp.zeros_like(x_pair)
                split = jnp.concatenate(
                    [jnp.where(left_half, x_pair, zero), jnp.where(left_half, zero, x_pair)], axis=0
                )
                sums.append(jnp.dot(mix, split, preferred_element_type=F32))
            inner = jnp.concatenate(sums, axis=1)
            value = inner + scale * outer + gain_ref[:, cols] * act_ref[rows, cols].astype(F32)
            if late:
                outer = jnp.dot(c_act, refs[1][:, cols], preferred_element_type=F32)
                scale = jnp.dot(extra, rep16_ref[:, cols], preferred_element_type=F32)
                value = value + scale * outer
            out_ref[rows, cols] = value.astype(BF16)


def gates_of(pay_ref, cols):
    gates = pay_ref[N:, cols].astype(F32)
    return gates[0:1] + gates[1:2]


def pair_kernel(shard_ref, own_ref, got_ref, half_ref):
    side = half_ref.shape[1]

    def join(early, late, cols):
        after = gates_of(late, cols)
        gate = jnp.broadcast_to(after * gates_of(early, cols), (PAY - N, side))
        high = gate.astype(BF16).astype(F32)
        half_ref[:N] = (late[:N, cols].astype(F32) + after * early[:N, cols].astype(F32)).astype(BF16)
        half_ref[N:] = jnp.where(iota((PAY - N, side), 0) == 0, high, gate - high).astype(BF16)

    @pl.when(shard_ref[0] % 2 == 0)
    def _():
        join(own_ref, got_ref, slice(0, side))

    @pl.when(shard_ref[0] % 2 == 1)
    def _():
        join(got_ref, own_ref, slice(side, 2 * side))


def prefix_kernel(*refs):
    prefix_ref = refs[-1]
    side = prefix_ref.shape[1]
    total = jnp.zeros((N, side), F32)
    for ref in refs[:-1]:
        total = gates_of(ref, slice(0, side)) * total + ref[:N].astype(F32)
    prefix_ref[...] = total.astype(BF16)


def carry_kernel(shard_ref, stream_ref, meta, mine_ref, other_ref, early_ref, first_ref, carried_ref, *sends):
    side = mine_ref.shape[1]
    lower, upper = slice(0, side), slice(side, 2 * side)

    @pl.when(shard_ref[0] % 2 == 0)
    def _():
        carried_ref[:, lower] = mine_ref[...]
        carried_ref[:, upper] = other_ref[...]

    @pl.when(shard_ref[0] % 2 == 1)
    def _():
        for cols, part in ((lower, other_ref), (upper, mine_ref)):
            carried_ref[:, cols] = (
                early_ref[:N, cols].astype(F32) + gates_of(early_ref, cols) * part[...].astype(F32)
            ).astype(BF16)

    value = (first_ref[0:1] * carried_ref[...].astype(F32)).T.astype(BF16)
    apart = (meta[5] // CAP) ^ stream_ref[0]
    for index, ref in enumerate(sends):
        ref[...] = jnp.where(apart == index, value, jnp.zeros_like(value))


def correct_kernel(meta, base_hbm, c_ref, carry_ref, carried_ref, rep16_ref, out_hbm, held, in_sem, out_sem):
    steps, _, width = held.shape
    reach = jnp.where(meta[0] < 0, jnp.minimum(meta[1], steps * BLOCK), 0)
    touched = (reach + BLOCK - 1) // BLOCK

    def copy(index, source, target, sem):
        place = pl.ds(pl.multiple_of(index * BLOCK, BLOCK), BLOCK)
        if source is held:
            return pltpu.make_async_copy(held.at[index], target.at[place], sem.at[index])
        return pltpu.make_async_copy(source.at[place], held.at[index], sem.at[index])

    def fetch(index, _):
        copy(index, base_hbm, held, in_sem).start()
        return 0

    def add(index, _):
        copy(index, base_hbm, held, in_sem).wait()
        rows = pl.ds(pl.multiple_of(index * BLOCK, BLOCK), BLOCK)
        entry = carry_ref[:, rows]
        entry = jnp.concatenate([entry, entry - entry.astype(BF16).astype(F32)], axis=0).T.astype(BF16)
        c_act = c_ref[rows, :]
        for tile in range(width // 256):
            cols = slice(tile * 256, tile * 256 + 256)
            outer = jnp.dot(c_act, carried_ref[:, cols], preferred_element_type=F32)
            scale = jnp.dot(entry, rep16_ref[:, cols], preferred_element_type=F32)
            held[index, :, cols] = (held[index, :, cols].astype(F32) + scale * outer).astype(BF16)
        copy(index, held, out_hbm, out_sem).start()
        return 0

    def close(index, _):
        copy(index, held, out_hbm, out_sem).wait()
        return 0

    lax.fori_loop(0, touched, fetch, 0)
    lax.fori_loop(0, touched, add, 0)
    lax.fori_loop(0, touched, close, 0)


def params(mib):
    return pltpu.CompilerParams(vmem_limit_bytes=mib * MIB)


def whole(shape):
    return pl.BlockSpec(shape, lambda *_: (0,) * len(shape))


def on_device(
    conv_input, conv_weight, conv_bias, step_size, log_decay, skip_gain, doc_bounds, doc_owner
):
    span, channels = conv_input.shape[1:]
    heads = step_size.shape[1]
    width = heads * P_SIZE
    steps = span // BLOCK
    chunks = span // CHUNK
    owners = lax.axis_size("stream")
    slots = owners * CAP
    rows = width + TAIL
    shard = lax.axis_index("seq").astype(jnp.int32).reshape(1)
    rows_in = conv_input[0]
    rim = shifted(rows_in[span - 16 :], "seq", 1)
    rep = (np.arange(width)[None, :] // P_SIZE == np.arange(heads)[:, None]).astype(np.float32)
    rep16 = np.concatenate([rep, rep], 0).astype(BF16)
    ticks = np.arange(CHUNK)
    tri = (ticks[:, None] <= ticks[None, :]).astype(BF16)
    order = np.arange(3 * CHUNK)
    tick, lag = 8 * (order // 24) + order % 8, order % 24 // 8 + 1
    source = np.arange(CHUNK + 16)
    move = (source[None, :] - 16 == (tick - lag)[:, None]).astype(BF16)
    slot = np.broadcast_to((4 * tick + lag)[:, None], (3 * CHUNK, 128)).astype(np.int32)
    smem = pl.BlockSpec(memory_space=pltpu.SMEM)
    stream = lax.axis_index("stream").astype(jnp.int32).reshape(1)
    per_head = pl.BlockSpec((heads, BLOCK), lambda i, *_: (0, i))
    prefetch = functools.partial(pltpu.PrefetchScalarGridSpec, num_scalar_prefetch=1)
    by_rows = pl.BlockSpec((BLOCK, channels), lambda i, *_: (i, 0))
    by_width = pl.BlockSpec((BLOCK, width), lambda i, *_: (i, 0))
    by_rest = pl.BlockSpec((BLOCK, N), lambda i, *_: (i, 0))
    in_hbm = pl.BlockSpec(memory_space=pl.ANY)
    act, b_act, c_act, cum, carry, sin, pay, meta = pl.pallas_call(
        states_kernel,
        grid=(steps,),
        in_specs=[
            smem, smem, smem, by_rows, whole((16, channels)),
            whole((4, channels)), whole((channels,)), whole(move.shape), whole(slot.shape),
            per_head, per_head, whole((heads, width)), whole((2 * heads, width)), whole((CHUNK, CHUNK)),
        ],
        out_specs=[
            by_width, by_rest, by_rest, per_head, per_head,
            pl.BlockSpec((BLOCK // CHUNK, N, width), lambda i, *_: (i, 0, 0)),
            whole((PAY, width)), smem,
        ],
        out_shape=[
            jax.ShapeDtypeStruct((span, width), BF16),
            jax.ShapeDtypeStruct((span, N), BF16),
            jax.ShapeDtypeStruct((span, N), BF16),
            jax.ShapeDtypeStruct((heads, span), F32),
            jax.ShapeDtypeStruct((heads, span), F32),
            jax.ShapeDtypeStruct((chunks, N, width), BF16),
            jax.ShapeDtypeStruct((PAY, width), BF16),
            jax.ShapeDtypeStruct((16,), jnp.int32),
        ],
        scratch_shapes=[
            pltpu.VMEM((16, channels), BF16),
            pltpu.VMEM((8, channels), F32),
            pltpu.VMEM((1 + BLOCK // CHUNK,) + move.shape, BF16),
            pltpu.VMEM((N, width), F32),
            pltpu.VMEM((heads, CHUNK), F32),
            pltpu.SMEM((owners,), jnp.int32),
        ],
        compiler_params=params(60),
        cost_estimate=pl.CostEstimate(
            flops=2 * span * channels * 600, bytes_accessed=32 << 20, transcendentals=span * channels
        ),
        name="states",
    )(
        shard, doc_bounds, doc_owner, rows_in, rim, conv_weight, conv_bias, move, slot,
        step_size[0], log_decay[0], rep, rep16, tri,
    )

    def outputs(first, last, late=()):
        rows_of = functools.partial(pl.BlockSpec, index_map=lambda i, *_: (first + i, 0))
        heads_of = pl.BlockSpec((heads, BLOCK), lambda i, *_: (0, first + i))
        return pl.pallas_call(
            functools.partial(output_kernel, first, bool(late)),
            grid_spec=prefetch(
                grid=(last - first,),
                in_specs=[
                    rows_of((BLOCK, width)), rows_of((BLOCK, N)), rows_of((BLOCK, N)), heads_of, heads_of,
                    pl.BlockSpec((BLOCK // CHUNK, N, width), lambda i, *_: (first + i, 0, 0)),
                    smem, whole((heads, width)), whole((2 * heads, width)),
                ] + ([heads_of, whole((N, width)), pl.BlockSpec(memory_space=pl.ANY)] if late else []),
                out_specs=rows_of((BLOCK, width)),
                scratch_shapes=[pltpu.VMEM((1, width), F32)],
            ),
            out_shape=jax.ShapeDtypeStruct((span, width), BF16),
            input_output_aliases={13: 0} if late else {},
            compiler_params=params(60),
            cost_estimate=pl.CostEstimate(
                flops=2 * (last - first) * BLOCK * width * N * 4,
                bytes_accessed=(last - first) * (4 << 20),
                transcendentals=(last - first) * BLOCK * CHUNK * heads,
            ),
            name="outputs",
        )(meta, act, b_act, c_act, step_size[0], cum, sin, skip_gain, rep, rep16, *late)

    side = width // 2
    count = lax.axis_size("seq")
    pairs = [(index, index ^ 1) for index in range(count)]
    early = lax.ppermute(pay, "seq", pairs)
    half = pl.pallas_call(
        pair_kernel,
        in_specs=[smem, whole((PAY, width)), whole((PAY, width))],
        out_specs=whole((PAY, side)),
        out_shape=jax.ShapeDtypeStruct((PAY, side), BF16),
        compiler_params=params(8),
        name="pair",
    )(shard, pay, early)
    chips = count // 2
    behind = [shifted(half, "seq", 2 * far) for far in range(chips - 1, 0, -1)]
    scanned, half = lax.optimization_barrier((sin, half))
    fin, first = pl.pallas_call(
        finals_kernel,
        in_specs=[
            smem, in_hbm, in_hbm, in_hbm, in_hbm, whole((16, channels)),
            whole((heads, span)), whole((heads, span)), whole((heads, span)),
            whole((heads, width)), whole((2 * heads, width)),
        ],
        out_specs=[in_hbm, whole((8, width))],
        out_shape=[
            jax.ShapeDtypeStruct((slots, rows, N), BF16),
            jax.ShapeDtypeStruct((8, width), F32),
        ],
        scratch_shapes=[
            pltpu.VMEM((EMAX, CHUNK, width), BF16),
            pltpu.VMEM((EMAX, CHUNK, N), BF16),
            pltpu.VMEM((EMAX, N, width), BF16),
            pltpu.VMEM((EMAX, CHUNK, channels), BF16),
            pltpu.VMEM((EMAX, 16, channels), BF16),
            pltpu.VMEM((rows, N), BF16),
            pltpu.VMEM((EMAX, rows, N), BF16),
            pltpu.VMEM((EMAX, TAIL, N), F32),
            pltpu.SemaphoreType.DMA((EMAX, 5)),
            pltpu.SemaphoreType.DMA((slots,)),
            pltpu.SemaphoreType.DMA((EMAX,)),
        ],
        compiler_params=params(58),
        cost_estimate=pl.CostEstimate(flops=1 << 28, bytes_accessed=6 << 20, transcendentals=0),
        name="finals",
    )(meta, act, b_act, scanned, rows_in, rim, step_size[0], cum, carry, rep, rep16)
    sin, fin = lax.optimization_barrier((sin, fin))
    got = lax.all_to_all(
        fin.reshape(owners, CAP, rows, N), "stream", split_axis=0, concat_axis=0, tiled=True
    )
    base = outputs(0, steps)
    *behind, base = lax.optimization_barrier((*behind, base))
    mine = pl.pallas_call(
        prefix_kernel,
        in_specs=[whole((PAY, side))] * len(behind),
        out_specs=whole((N, side)),
        out_shape=jax.ShapeDtypeStruct((N, side), BF16),
        compiler_params=params(8),
        name="prefix",
    )(*behind)
    other = lax.ppermute(mine, "seq", pairs)
    other, got = lax.optimization_barrier((other, got))
    carried, *send = pl.pallas_call(
        carry_kernel,
        in_specs=[smem, smem, smem, whole((N, side)), whole((N, side)), whole((PAY, width)), whole((8, width))],
        out_specs=[whole((N, width))] + [whole((width, N))] * owners,
        out_shape=[jax.ShapeDtypeStruct((N, width), BF16)]
        + [jax.ShapeDtypeStruct((width, N), BF16)] * owners,
        compiler_params=params(8),
        name="carry",
    )(shard, stream, meta, mine, other, early, first)
    more = [send[0]]
    for apart in range(1, owners):
        swap = [(index, index ^ apart) for index in range(owners)]
        more.append(lax.ppermute(send[apart], "stream", swap))

    out = pl.pallas_call(
        correct_kernel,
        in_specs=[smem, in_hbm, whole((span, N)), whole((heads, span)), whole((N, width)), whole((2 * heads, width))],
        out_specs=in_hbm,
        out_shape=jax.ShapeDtypeStruct((span, width), BF16),
        scratch_shapes=[
            pltpu.VMEM((steps, BLOCK, width), BF16),
            pltpu.SemaphoreType.DMA((steps,)),
            pltpu.SemaphoreType.DMA((steps,)),
        ],
        input_output_aliases={1: 0},
        compiler_params=params(58),
        cost_estimate=pl.CostEstimate(
            flops=2 * span * width * N, bytes_accessed=18 << 20, transcendentals=0
        ),
        name="correct",
    )(meta, base, c_act, carry, carried, rep16)

    apart = (jnp.arange(owners) ^ stream)[:, None, None]
    extra = jnp.broadcast_to(more[0][None], (owners, width, N))
    for index in range(1, owners):
        extra = jnp.where(apart == index, more[index][None], extra)
    ranks = jnp.arange(CAP)[None, :, None, None]
    extra = jnp.where(ranks == 0, extra[:, None], jnp.zeros_like(extra[:, None]))
    ssm = got[:, :, :width].astype(F32) + extra.astype(F32)
    ssm = ssm.reshape(1, 1, owners, CAP, heads, P_SIZE, N)
    tiles = channels // N
    conv = got[:, :, width : width + 3 * tiles].reshape(1, 1, owners, CAP, 3, channels)
    return out[None], ssm, conv


def solution(mesh):
    in_specs = (
        P("stream", "seq", None),
        P(),
        P(),
        P("stream", None, "seq"),
        P("stream", None, "seq"),
        P(),
        P("stream", None),
        P("stream", None),
    )
    out_specs = (
        P("stream", "seq", None),
        P("stream", "seq", None, None, None, None, None),
        P("stream", "seq", None, None, None, None),
    )
    return jax.shard_map(
        on_device, mesh=mesh, in_specs=in_specs, out_specs=out_specs, check_vma=False
    )
```

```python
import functools

import jax
import jax.numpy as jnp
import numpy as np
from jax import lax
from jax.experimental import pallas as pl
from jax.experimental.pallas import tpu as pltpu
from jax.sharding import PartitionSpec as P

P_SIZE = 64
N = 128
EMAX = 4
CAP = 2
CHUNK = 128
BLOCK = 512
FAR = 1 << 30
LOG2E = 1.4426950408889634
PAY = 144
TAIL = 32
MIB = 1024 * 1024

F32 = jnp.float32
BF16 = jnp.bfloat16


def shifted(value, axis, steps):
    count = lax.axis_size(axis)
    leading, last = (max(0, -steps), min(count, count - steps))
    return lax.ppermute(value, axis, [(source, source + steps) for source in range(leading, last)])


def iota(shape, axis):
    return lax.broadcasted_iota(jnp.int32, shape, axis)


def outer_dot(left, right):
    return lax.dot_general(left, right, (((0,), (0,)), ((), ())), preferred_element_type=F32)


def halves(value):
    high = value.astype(BF16)
    low = (value - high.astype(F32)).astype(BF16)
    return jnp.concatenate([high, low], axis=0)


def thirds(value):
    high = value.astype(BF16)
    rest = value - high.astype(F32)
    mid = rest.astype(BF16)
    low = (rest - mid.astype(F32)).astype(BF16)
    return jnp.concatenate([high, mid, low], axis=0)


def spread_row(column, rep):
    return jnp.sum(rep * column, axis=0, keepdims=True)


def last_start(meta, place):
    start = meta[0]
    for slot in range(EMAX):
        end = meta[1 + slot]
        start = jnp.where(end <= place, end, start)
    return start


def next_end(meta, place):
    end = FAR
    for slot in reversed(range(EMAX)):
        end = jnp.where(meta[1 + slot] > place, meta[1 + slot], end)
    return end


def starts_of(meta, rows):
    start = jnp.full(rows.shape, meta[0], jnp.int32)
    for slot in range(EMAX):
        end = meta[1 + slot]
        start = jnp.where(rows >= end, end, start)
    return start


def read_docs(bounds, owners, meta, count, anchor, span):
    for slot in range(EMAX):
        meta[1 + slot] = FAR
        meta[5 + slot] = 0
    for owner in range(count.shape[0]):
        count[owner] = 0

    def one(index, carry):
        found, prior, start = carry
        end = bounds[0, index]
        owner = owners[0, index]
        mine = (end > prior) & (end > anchor) & (end <= anchor + span) & (found < EMAX)

        @pl.when(mine)
        def _():
            meta[1 + found] = end - anchor
            rank = count[owner]
            meta[5 + found] = jnp.where(rank < CAP, owner * CAP + rank, -1)
            count[owner] = rank + 1

        return found + mine.astype(jnp.int32), end, jnp.where(end <= anchor, end, start)

    zero = jnp.int32(0)
    _, _, start = lax.fori_loop(0, bounds.shape[1], one, (zero, zero, zero))
    meta[0] = start - anchor


def states_kernel(
    shard_ref, bounds, owners, x_ref, rim_ref, w_ref, bias_ref, move_ref, slot_ref,
    dt_ref, ld_ref, rep_ref, rep16_ref, tri_ref,
    act_ref, b_ref, c_ref, cum_ref, carry_ref, sin_ref, pay_ref, meta,
    edge16, weights, moves, state, total, count,
):
    step = pl.program_id(0)
    heads = dt_ref.shape[0]
    width = rep_ref.shape[1]
    span = pl.num_programs(0) * BLOCK
    parts = BLOCK // CHUNK
    first = step * BLOCK

    @pl.when(step == 0)
    def _():
        read_docs(bounds, owners, meta, count, shard_ref[0] * span, span)
        edge16[...] = rim_ref[...]
        weights[0:4] = 0.5 * w_ref[...]
        weights[4:5] = 0.5 * bias_ref[...].reshape(1, weights.shape[1])
        moves[0] = move_ref[...]
        state[...] = jnp.zeros_like(state)
        total[...] = jnp.zeros_like(total)

    choices = []
    for part in range(parts):
        begin = first + part * CHUNK
        near = (meta[0] > begin - 3) & (meta[0] < begin + CHUNK)
        for slot in range(EMAX):
            near = near | ((meta[1 + slot] > begin - 3) & (meta[1 + slot] < begin + CHUNK))

        @pl.when(near)
        def _():
            tick = slot_ref[...] // 4 + begin
            kept = (tick - starts_of(meta, tick) >= slot_ref[...] % 4).astype(F32)
            moves[1 + part, :, :128] = (kept * move_ref[:, :128].astype(F32)).astype(BF16)
            moves[1 + part, :, 128:] = (kept[:, :16] * move_ref[:, 128:].astype(F32)).astype(BF16)

        choices.append(jnp.where(near, 1 + part, 0))

    for part in range(parts):
        low = part * CHUNK
        rows = slice(low, low + CHUNK)
        pick = moves[choices[part]]
        for tile in range(x_ref.shape[1] // 256):
            cols = slice(tile * 256, tile * 256 + 256)
            if part:
                wide = x_ref[low - 16 : low + CHUNK, cols]
            else:
                wide = jnp.concatenate([edge16[:, cols], x_ref[rows, cols]], axis=0)
            moved = jnp.dot(pick, wide, preferred_element_type=F32)
            moved = moved.reshape(CHUNK // 8, 3, 8, 256)
            mixed = weights[4:5, cols] + weights[0:1, cols] * x_ref[rows, cols].astype(F32)
            for lag in range(1, 4):
                mixed = mixed + weights[lag : lag + 1, cols] * moved[:, lag - 1].reshape(CHUNK, 256)
            value = (mixed + mixed * jnp.tanh(mixed)).astype(BF16)
            if tile * 256 < act_ref.shape[1]:
                act_ref[rows, cols] = value
            else:
                b_ref[rows, :] = value[:, :N]
                c_ref[rows, :] = value[:, N:]

    edge16[...] = x_ref[BLOCK - 16 :, :]

    spans = [slice(part * CHUNK, part * CHUNK + CHUNK) for part in range(parts)]
    pieces = jnp.concatenate([thirds(ld_ref[:, rows] * LOG2E) for rows in spans], axis=0)
    summed = jnp.dot(pieces, tri_ref[...], preferred_element_type=F32)
    open_end = jnp.where(meta[0] < 0, meta[1], -1)
    running = total[...]
    scales = []
    throughs = []
    for part, rows in enumerate(spans):
        begin = first + part * CHUNK
        at = 3 * heads * part
        cum = summed[at : at + heads] + summed[at + heads : at + 2 * heads] + summed[at + 2 * heads : at + 3 * heads]
        cum_ref[:, rows] = cum
        lane = iota((heads, CHUNK), 1) + begin
        carry_ref[:, rows] = jnp.where(lane < open_end, jnp.exp2(running + cum), 0.0)
        start = last_start(meta, begin + CHUNK - 1)
        last = cum[:, CHUNK - 1 :]
        weight = jnp.where(lane >= start, jnp.exp2(last - cum) * dt_ref[:, rows], 0.0)
        scales.append(weight.T.astype(BF16))
        throughs.append(spread_row(jnp.where(start < begin, jnp.exp2(last), 0.0), rep_ref[...]))
        running = running + last
    total[...] = running
    weight = jnp.concatenate(scales, axis=0)
    turned = [b_ref[rows, :].T for rows in spans]
    for tile in range(width // 256):
        cols = slice(tile * 256, tile * 256 + 256)
        scale = jnp.dot(weight, rep16_ref[:heads, cols], preferred_element_type=F32)
        load = scale.astype(BF16) * act_ref[:, cols]
        held = state[:, cols]
        for part, rows in enumerate(spans):
            sin_ref[part, :, cols] = held.astype(BF16)
            grown = jnp.dot(turned[part], load[rows], preferred_element_type=F32)
            held = throughs[part][:, cols] * held + grown
        state[:, cols] = held

    @pl.when(step == pl.num_programs(0) - 1)
    def _():
        start = last_start(meta, span - 1)
        gate = spread_row(jnp.where(start < 0, jnp.exp2(total[:, :1]), 0.0), rep_ref[...])
        gate = jnp.broadcast_to(gate, (PAY - N, width))
        high = gate.astype(BF16).astype(F32)
        pay_ref[:N] = state[...].astype(BF16)
        pay_ref[N:] = jnp.where(iota((PAY - N, width), 0) == 0, high, gate - high).astype(BF16)


def finals_kernel(
    meta, act_hbm, b_hbm, sin_hbm, x_hbm, rim_ref, dt_ref, cum_ref, carry_ref, rep_ref, rep16_ref,
    fin_hbm, first_ref,
    act_held, b_held, sin_held, x_held, edge_held, blank, made, lines, in_sem, blank_sem, made_sem,
):
    heads, span = dt_ref.shape
    width = rep_ref.shape[1]

    def place(slot):
        return pl.multiple_of((jnp.minimum(meta[1 + slot], span) - 1) // CHUNK * CHUNK, CHUNK)

    def copies(slot):
        low = place(slot)
        rows = pl.ds(low, CHUNK)
        before = pl.ds(pl.multiple_of(jnp.maximum(low - 16, 0), 16), 16)
        pairs = (
            (act_hbm.at[rows], act_held), (b_hbm.at[rows], b_held), (sin_hbm.at[low // CHUNK], sin_held),
            (x_hbm.at[rows], x_held), (x_hbm.at[before], edge_held),
        )
        return [
            pltpu.make_async_copy(source, target.at[slot], in_sem.at[slot, index])
            for index, (source, target) in enumerate(pairs)
        ]

    fetched = [copies(slot) for slot in range(EMAX)]
    for copy in sum(fetched, []):
        copy.start()
    blank[...] = jnp.zeros_like(blank)
    blanks = [
        pltpu.make_async_copy(blank, fin_hbm.at[index], blank_sem.at[index])
        for index in range(fin_hbm.shape[0])
    ]
    for copy in blanks:
        copy.start()
    lines[...] = jnp.zeros_like(lines)
    for copy in sum(fetched, []):
        copy.wait()
    for slot in range(EMAX):
        end = meta[1 + slot]
        start = meta[slot]
        low = place(slot)
        there = pl.ds(low, CHUNK)
        lane = iota((heads, CHUNK), 1) + low
        cum = cum_ref[:, there]
        at_end = jnp.sum(jnp.where(lane == end - 1, cum, 0.0), axis=1, keepdims=True)
        inside = (lane < end) & (lane >= start)
        weight = jnp.exp2(jnp.minimum(at_end - cum, 0.0)) * dt_ref[:, there]
        weight = jnp.where(inside, weight, 0.0).T.astype(BF16)
        scale = jnp.dot(weight, rep16_ref[:heads], preferred_element_type=F32)
        load = scale.astype(BF16) * act_held[slot]
        local = outer_dot(b_held[slot], load)
        through = spread_row(jnp.where(start < low, jnp.exp2(at_end), 0.0), rep_ref[...])
        final = local + through * sin_held[slot].astype(F32)
        if slot == 0:
            opened = jnp.sum(jnp.where(lane == end - 1, carry_ref[:, there], 0.0), axis=1, keepdims=True)
            first_ref[...] = jnp.broadcast_to(spread_row(opened, rep_ref[...]), first_ref.shape)
        row = iota((16, CHUNK), 0)
        col = iota((16, CHUNK), 1) + low
        pick = (col == end - 3 + row) & (col >= start) & (row < 3)
        row16 = iota((16, 16), 0)
        col16 = iota((16, 16), 1) + low - 16
        pick16 = (col16 == end - 3 + row16) & (col16 >= start) & (row16 < 3)
        rim = jnp.where(low > 0, edge_held[slot].astype(F32), rim_ref[...].astype(F32))
        last = jnp.dot(
            pick.astype(F32).astype(BF16), x_held[slot], preferred_element_type=F32
        ) + jnp.dot(pick16.astype(F32).astype(BF16), rim.astype(BF16), preferred_element_type=F32)
        tiles = x_held.shape[2] // 128
        for index in range(3):
            for tile in range(tiles):
                at = index * tiles + tile
                lines[slot, at : at + 1] = last[index : index + 1, tile * 128 : tile * 128 + 128]

        made[slot, :width] = final.astype(BF16).T
        made[slot, width:] = lines[slot].astype(BF16)
    for copy in blanks:
        copy.wait()
    used = [(meta[1 + slot] <= span) & (meta[5 + slot] >= 0) for slot in range(EMAX)]

    def send(slot):
        return pltpu.make_async_copy(made.at[slot], fin_hbm.at[meta[5 + slot]], made_sem.at[slot])

    for slot in range(EMAX):

        @pl.when(used[slot])
        def _():
            send(slot).start()

    for slot in range(EMAX):

        @pl.when(used[slot])
        def _():
            send(slot).wait()


def output_kernel(origin, meta, act_ref, b_ref, c_ref, dt_ref, cum_ref, sin_ref, gain_in, rep_ref, rep16_ref, *refs):
    out_ref, gain_ref = refs[-2:]
    step = origin + pl.program_id(0)
    heads = dt_ref.shape[0]
    width = out_ref.shape[1]
    parts = BLOCK // CHUNK

    @pl.when(pl.program_id(0) == 0)
    def _():
        row = jnp.zeros((1, width), F32)
        for head in range(heads):
            row = row + gain_in[head] * rep_ref[head : head + 1, :]
        gain_ref[...] = row

    for part in range(parts):
        begin = step * BLOCK + part * CHUNK
        rows = slice(part * CHUNK, part * CHUNK + CHUNK)
        cum = cum_ref[:, rows]
        back = cum - jnp.log2(dt_ref[:, rows])
        ahead = cum.T
        b_act = b_ref[rows, :]
        c_act = c_ref[rows, :]
        place = iota((CHUNK, CHUNK), 0) + begin
        other = iota((CHUNK, CHUNK), 1) + begin
        scores = lax.dot_general(c_act, b_act, (((1,), (1,)), ((), ())), preferred_element_type=F32)
        scores = jnp.where((other <= place) & (other >= starts_of(meta, place)), scores, 0.0)
        lane = iota((heads, CHUNK), 1) + begin
        before = jnp.where(last_start(meta, begin) < begin, next_end(meta, begin), -1)
        entry = jnp.where(lane < before, jnp.exp2(cum), 0.0)
        entry = jnp.concatenate([entry, entry - entry.astype(BF16).astype(F32)], axis=0).T.astype(BF16)
        left_half = iota((CHUNK, 128), 1) < P_SIZE
        for quad in range(heads // 4):
            cols = slice(quad * 256, quad * 256 + 256)
            outer = jnp.dot(c_act, sin_ref[part, :, cols], preferred_element_type=F32)
            scale = jnp.dot(entry, rep16_ref[:, cols], preferred_element_type=F32)
            sums = []
            for pair in (2 * quad, 2 * quad + 1):
                mixes = []
                for head in (2 * pair, 2 * pair + 1):
                    spread = jnp.minimum(ahead[:, head : head + 1] - back[head : head + 1, :], 0.0)
                    mixes.append((jnp.exp2(spread) * scores).astype(BF16))
                mix = jnp.concatenate(mixes, axis=1)
                x_pair = act_ref[rows, pair * 128 : pair * 128 + 128]
                zero = jnp.zeros_like(x_pair)
                split = jnp.concatenate(
                    [jnp.where(left_half, x_pair, zero), jnp.where(left_half, zero, x_pair)], axis=0
                )
                sums.append(jnp.dot(mix, split, preferred_element_type=F32))
            inner = jnp.concatenate(sums, axis=1)
            value = inner + scale * outer + gain_ref[:, cols] * act_ref[rows, cols].astype(F32)
            out_ref[rows, cols] = value.astype(BF16)


def gates_of(pay_ref, cols):
    gates = pay_ref[N:, cols].astype(F32)
    return gates[0:1] + gates[1:2]


def pair_kernel(shard_ref, own_ref, got_ref, half_ref):
    side = half_ref.shape[1]

    def join(early, late, cols):
        after = gates_of(late, cols)
        gate = jnp.broadcast_to(after * gates_of(early, cols), (PAY - N, side))
        high = gate.astype(BF16).astype(F32)
        half_ref[:N] = (late[:N, cols].astype(F32) + after * early[:N, cols].astype(F32)).astype(BF16)
        half_ref[N:] = jnp.where(iota((PAY - N, side), 0) == 0, high, gate - high).astype(BF16)

    @pl.when(shard_ref[0] % 2 == 0)
    def _():
        join(own_ref, got_ref, slice(0, side))

    @pl.when(shard_ref[0] % 2 == 1)
    def _():
        join(got_ref, own_ref, slice(side, 2 * side))


def prefix_kernel(*refs):
    prefix_ref = refs[-1]
    side = prefix_ref.shape[1]
    total = jnp.zeros((N, side), F32)
    for ref in refs[:-1]:
        total = gates_of(ref, slice(0, side)) * total + ref[:N].astype(F32)
    prefix_ref[...] = total.astype(BF16)


def carry_kernel(shard_ref, stream_ref, meta, mine_ref, other_ref, early_ref, first_ref, carried_ref, *sends):
    side = mine_ref.shape[1]
    lower, upper = slice(0, side), slice(side, 2 * side)

    @pl.when(shard_ref[0] % 2 == 0)
    def _():
        carried_ref[:, lower] = mine_ref[...]
        carried_ref[:, upper] = other_ref[...]

    @pl.when(shard_ref[0] % 2 == 1)
    def _():
        for cols, part in ((lower, other_ref), (upper, mine_ref)):
            carried_ref[:, cols] = (
                early_ref[:N, cols].astype(F32) + gates_of(early_ref, cols) * part[...].astype(F32)
            ).astype(BF16)

    value = (first_ref[0:1] * carried_ref[...].astype(F32)).T.astype(BF16)
    apart = (meta[5] // CAP) ^ stream_ref[0]
    for index, ref in enumerate(sends):
        ref[...] = jnp.where(apart == index, value, jnp.zeros_like(value))


def correct_kernel(meta, base_hbm, c_ref, carry_ref, carried_ref, rep16_ref, out_hbm, held, in_sem, out_sem):
    steps, _, width = held.shape
    reach = jnp.where(meta[0] < 0, jnp.minimum(meta[1], steps * BLOCK), 0)
    touched = (reach + BLOCK - 1) // BLOCK

    def copy(index, source, target, sem):
        place = pl.ds(pl.multiple_of(index * BLOCK, BLOCK), BLOCK)
        if source is held:
            return pltpu.make_async_copy(held.at[index], target.at[place], sem.at[index])
        return pltpu.make_async_copy(source.at[place], held.at[index], sem.at[index])

    def fetch(index, _):
        copy(index, base_hbm, held, in_sem).start()
        return 0

    def add(index, _):
        copy(index, base_hbm, held, in_sem).wait()
        rows = pl.ds(pl.multiple_of(index * BLOCK, BLOCK), BLOCK)
        entry = carry_ref[:, rows]
        entry = jnp.concatenate([entry, entry - entry.astype(BF16).astype(F32)], axis=0).T.astype(BF16)
        c_act = c_ref[rows, :]
        for tile in range(width // 256):
            cols = slice(tile * 256, tile * 256 + 256)
            outer = jnp.dot(c_act, carried_ref[:, cols], preferred_element_type=F32)
            scale = jnp.dot(entry, rep16_ref[:, cols], preferred_element_type=F32)
            held[index, :, cols] = (held[index, :, cols].astype(F32) + scale * outer).astype(BF16)
        copy(index, held, out_hbm, out_sem).start()
        return 0

    def close(index, _):
        copy(index, held, out_hbm, out_sem).wait()
        return 0

    lax.fori_loop(0, touched, fetch, 0)
    lax.fori_loop(0, touched, add, 0)
    lax.fori_loop(0, touched, close, 0)


def params(mib):
    return pltpu.CompilerParams(vmem_limit_bytes=mib * MIB)


def whole(shape):
    return pl.BlockSpec(shape, lambda *_: (0,) * len(shape))


def on_device(
    conv_input, conv_weight, conv_bias, step_size, log_decay, skip_gain, doc_bounds, doc_owner
):
    span, channels = conv_input.shape[1:]
    heads = step_size.shape[1]
    width = heads * P_SIZE
    steps = span // BLOCK
    chunks = span // CHUNK
    owners = lax.axis_size("stream")
    slots = owners * CAP
    rows = width + TAIL
    shard = lax.axis_index("seq").astype(jnp.int32).reshape(1)
    rows_in = conv_input[0]
    rim = shifted(rows_in[span - 16 :], "seq", 1)
    rep = (np.arange(width)[None, :] // P_SIZE == np.arange(heads)[:, None]).astype(np.float32)
    rep16 = np.concatenate([rep, rep], 0).astype(BF16)
    ticks = np.arange(CHUNK)
    tri = (ticks[:, None] <= ticks[None, :]).astype(BF16)
    order = np.arange(3 * CHUNK)
    tick, lag = 8 * (order // 24) + order % 8, order % 24 // 8 + 1
    source = np.arange(CHUNK + 16)
    move = (source[None, :] - 16 == (tick - lag)[:, None]).astype(BF16)
    slot = np.broadcast_to((4 * tick + lag)[:, None], (3 * CHUNK, 128)).astype(np.int32)
    smem = pl.BlockSpec(memory_space=pltpu.SMEM)
    stream = lax.axis_index("stream").astype(jnp.int32).reshape(1)
    per_head = pl.BlockSpec((heads, BLOCK), lambda i, *_: (0, i))
    prefetch = functools.partial(pltpu.PrefetchScalarGridSpec, num_scalar_prefetch=1)
    by_rows = pl.BlockSpec((BLOCK, channels), lambda i, *_: (i, 0))
    by_width = pl.BlockSpec((BLOCK, width), lambda i, *_: (i, 0))
    by_rest = pl.BlockSpec((BLOCK, N), lambda i, *_: (i, 0))
    in_hbm = pl.BlockSpec(memory_space=pl.ANY)
    act, b_act, c_act, cum, carry, sin, pay, meta = pl.pallas_call(
        states_kernel,
        grid=(steps,),
        in_specs=[
            smem, smem, smem, by_rows, whole((16, channels)),
            whole((4, channels)), whole((channels,)), whole(move.shape), whole(slot.shape),
            per_head, per_head, whole((heads, width)), whole((2 * heads, width)), whole((CHUNK, CHUNK)),
        ],
        out_specs=[
            by_width, by_rest, by_rest, per_head, per_head,
            pl.BlockSpec((BLOCK // CHUNK, N, width), lambda i, *_: (i, 0, 0)),
            whole((PAY, width)), smem,
        ],
        out_shape=[
            jax.ShapeDtypeStruct((span, width), BF16),
            jax.ShapeDtypeStruct((span, N), BF16),
            jax.ShapeDtypeStruct((span, N), BF16),
            jax.ShapeDtypeStruct((heads, span), F32),
            jax.ShapeDtypeStruct((heads, span), F32),
            jax.ShapeDtypeStruct((chunks, N, width), BF16),
            jax.ShapeDtypeStruct((PAY, width), BF16),
            jax.ShapeDtypeStruct((16,), jnp.int32),
        ],
        scratch_shapes=[
            pltpu.VMEM((16, channels), BF16),
            pltpu.VMEM((8, channels), F32),
            pltpu.VMEM((1 + BLOCK // CHUNK,) + move.shape, BF16),
            pltpu.VMEM((N, width), F32),
            pltpu.VMEM((heads, CHUNK), F32),
            pltpu.SMEM((owners,), jnp.int32),
        ],
        compiler_params=params(60),
        cost_estimate=pl.CostEstimate(
            flops=2 * span * channels * 600, bytes_accessed=32 << 20, transcendentals=span * channels
        ),
        name="states",
    )(
        shard, doc_bounds, doc_owner, rows_in, rim, conv_weight, conv_bias, move, slot,
        step_size[0], log_decay[0], rep, rep16, tri,
    )

    def outputs(first, last, *held):
        rows_of = functools.partial(pl.BlockSpec, index_map=lambda i, *_: (first + i, 0))
        heads_of = pl.BlockSpec((heads, BLOCK), lambda i, *_: (0, first + i))
        return pl.pallas_call(
            functools.partial(output_kernel, first),
            grid_spec=prefetch(
                grid=(last - first,),
                in_specs=[
                    rows_of((BLOCK, width)), rows_of((BLOCK, N)), rows_of((BLOCK, N)), heads_of, heads_of,
                    pl.BlockSpec((BLOCK // CHUNK, N, width), lambda i, *_: (first + i, 0, 0)),
                    smem, whole((heads, width)), whole((2 * heads, width)),
                ] + [in_hbm] * len(held),
                out_specs=rows_of((BLOCK, width)),
                scratch_shapes=[pltpu.VMEM((1, width), F32)],
            ),
            out_shape=jax.ShapeDtypeStruct((span, width), BF16),
            input_output_aliases={10: 0} if held else {},
            compiler_params=params(60),
            cost_estimate=pl.CostEstimate(
                flops=2 * (last - first) * BLOCK * width * N * 4,
                bytes_accessed=(last - first) * (4 << 20),
                transcendentals=(last - first) * BLOCK * CHUNK * heads,
            ),
            name="outputs",
        )(meta, act, b_act, c_act, step_size[0], cum, sin, skip_gain, rep, rep16, *held)

    side = width // 2
    count = lax.axis_size("seq")
    pairs = [(index, index ^ 1) for index in range(count)]
    early = lax.ppermute(pay, "seq", pairs)
    half = pl.pallas_call(
        pair_kernel,
        in_specs=[smem, whole((PAY, width)), whole((PAY, width))],
        out_specs=whole((PAY, side)),
        out_shape=jax.ShapeDtypeStruct((PAY, side), BF16),
        compiler_params=params(8),
        name="pair",
    )(shard, pay, early)
    scanned, half = lax.optimization_barrier((sin, half))
    fin, first = pl.pallas_call(
        finals_kernel,
        in_specs=[
            smem, in_hbm, in_hbm, in_hbm, in_hbm, whole((16, channels)),
            whole((heads, span)), whole((heads, span)), whole((heads, span)),
            whole((heads, width)), whole((2 * heads, width)),
        ],
        out_specs=[in_hbm, whole((8, width))],
        out_shape=[
            jax.ShapeDtypeStruct((slots, rows, N), BF16),
            jax.ShapeDtypeStruct((8, width), F32),
        ],
        scratch_shapes=[
            pltpu.VMEM((EMAX, CHUNK, width), BF16),
            pltpu.VMEM((EMAX, CHUNK, N), BF16),
            pltpu.VMEM((EMAX, N, width), BF16),
            pltpu.VMEM((EMAX, CHUNK, channels), BF16),
            pltpu.VMEM((EMAX, 16, channels), BF16),
            pltpu.VMEM((rows, N), BF16),
            pltpu.VMEM((EMAX, rows, N), BF16),
            pltpu.VMEM((EMAX, TAIL, N), F32),
            pltpu.SemaphoreType.DMA((EMAX, 5)),
            pltpu.SemaphoreType.DMA((slots,)),
            pltpu.SemaphoreType.DMA((EMAX,)),
        ],
        compiler_params=params(58),
        cost_estimate=pl.CostEstimate(flops=1 << 28, bytes_accessed=6 << 20, transcendentals=0),
        name="finals",
    )(meta, act, b_act, scanned, rows_in, rim, step_size[0], cum, carry, rep, rep16)
    sin, fin = lax.optimization_barrier((sin, fin))
    got = lax.all_to_all(
        fin.reshape(owners, CAP, rows, N), "stream", split_axis=0, concat_axis=0, tiled=True
    )
    base = outputs(0, 2)
    half, base = lax.optimization_barrier((half, base))
    chips = count // 2
    behind = [shifted(half, "seq", 2 * far) for far in range(chips - 1, 0, -1)]
    base = outputs(2, steps - 2, base)
    *behind, base = lax.optimization_barrier((*behind, base))
    mine = pl.pallas_call(
        prefix_kernel,
        in_specs=[whole((PAY, side))] * len(behind),
        out_specs=whole((N, side)),
        out_shape=jax.ShapeDtypeStruct((N, side), BF16),
        compiler_params=params(8),
        name="prefix",
    )(*behind)
    other = lax.ppermute(mine, "seq", pairs)
    other, got = lax.optimization_barrier((other, got))
    carried, *send = pl.pallas_call(
        carry_kernel,
        in_specs=[smem, smem, smem, whole((N, side)), whole((N, side)), whole((PAY, width)), whole((8, width))],
        out_specs=[whole((N, width))] + [whole((width, N))] * owners,
        out_shape=[jax.ShapeDtypeStruct((N, width), BF16)]
        + [jax.ShapeDtypeStruct((width, N), BF16)] * owners,
        compiler_params=params(8),
        name="carry",
    )(shard, stream, meta, mine, other, early, first)
    more = [send[0]]
    for apart in range(1, owners):
        swap = [(index, index ^ apart) for index in range(owners)]
        more.append(lax.ppermute(send[apart], "stream", swap))

    carried, base = lax.optimization_barrier((carried, base))
    base = outputs(steps - 2, steps, base)
    out = pl.pallas_call(
        correct_kernel,
        in_specs=[smem, in_hbm, whole((span, N)), whole((heads, span)), whole((N, width)), whole((2 * heads, width))],
        out_specs=in_hbm,
        out_shape=jax.ShapeDtypeStruct((span, width), BF16),
        scratch_shapes=[
            pltpu.VMEM((steps, BLOCK, width), BF16),
            pltpu.SemaphoreType.DMA((steps,)),
            pltpu.SemaphoreType.DMA((steps,)),
        ],
        input_output_aliases={1: 0},
        compiler_params=params(58),
        cost_estimate=pl.CostEstimate(
            flops=2 * span * width * N, bytes_accessed=18 << 20, transcendentals=0
        ),
        name="correct",
    )(meta, base, c_act, carry, carried, rep16)

    apart = (jnp.arange(owners) ^ stream)[:, None, None]
    extra = jnp.broadcast_to(more[0][None], (owners, width, N))
    for index in range(1, owners):
        extra = jnp.where(apart == index, more[index][None], extra)
    ranks = jnp.arange(CAP)[None, :, None, None]
    extra = jnp.where(ranks == 0, extra[:, None], jnp.zeros_like(extra[:, None]))
    ssm = got[:, :, :width].astype(F32) + extra.astype(F32)
    ssm = ssm.reshape(1, 1, owners, CAP, heads, P_SIZE, N)
    tiles = channels // N
    conv = got[:, :, width : width + 3 * tiles].reshape(1, 1, owners, CAP, 3, channels)
    return out[None], ssm, conv


def solution(mesh):
    in_specs = (
        P("stream", "seq", None),
        P(),
        P(),
        P("stream", None, "seq"),
        P("stream", None, "seq"),
        P(),
        P("stream", None),
        P("stream", None),
    )
    out_specs = (
        P("stream", "seq", None),
        P("stream", "seq", None, None, None, None, None),
        P("stream", "seq", None, None, None, None),
    )
    return jax.shard_map(
        on_device, mesh=mesh, in_specs=in_specs, out_specs=out_specs, check_vma=False
    )
```

```python
import functools

import jax
import jax.numpy as jnp
import numpy as np
from jax import lax
from jax.experimental import pallas as pl
from jax.experimental.pallas import tpu as pltpu
from jax.sharding import PartitionSpec as P

P_SIZE = 64
N = 128
EMAX = 4
CAP = 2
CHUNK = 128
BLOCK = 512
FAR = 1 << 30
LOG2E = 1.4426950408889634
PAY = 144
TAIL = 32
MIB = 1024 * 1024

F32 = jnp.float32
BF16 = jnp.bfloat16


def shifted(value, axis, steps):
    count = lax.axis_size(axis)
    leading, last = (max(0, -steps), min(count, count - steps))
    return lax.ppermute(value, axis, [(source, source + steps) for source in range(leading, last)])


def iota(shape, axis):
    return lax.broadcasted_iota(jnp.int32, shape, axis)


def outer_dot(left, right):
    return lax.dot_general(left, right, (((0,), (0,)), ((), ())), preferred_element_type=F32)


def halves(value):
    high = value.astype(BF16)
    low = (value - high.astype(F32)).astype(BF16)
    return jnp.concatenate([high, low], axis=0)


def thirds(value):
    high = value.astype(BF16)
    rest = value - high.astype(F32)
    mid = rest.astype(BF16)
    low = (rest - mid.astype(F32)).astype(BF16)
    return jnp.concatenate([high, mid, low], axis=0)


def spread_row(column, rep):
    return jnp.sum(rep * column, axis=0, keepdims=True)


def last_start(meta, place):
    start = meta[0]
    for slot in range(EMAX):
        end = meta[1 + slot]
        start = jnp.where(end <= place, end, start)
    return start


def next_end(meta, place):
    end = FAR
    for slot in reversed(range(EMAX)):
        end = jnp.where(meta[1 + slot] > place, meta[1 + slot], end)
    return end


def starts_of(meta, rows):
    start = jnp.full(rows.shape, meta[0], jnp.int32)
    for slot in range(EMAX):
        end = meta[1 + slot]
        start = jnp.where(rows >= end, end, start)
    return start


def read_docs(bounds, owners, meta, count, anchor, span):
    for slot in range(EMAX):
        meta[1 + slot] = FAR
        meta[5 + slot] = 0
    for owner in range(count.shape[0]):
        count[owner] = 0

    def one(index, carry):
        found, prior, start = carry
        end = bounds[0, index]
        owner = owners[0, index]
        mine = (end > prior) & (end > anchor) & (end <= anchor + span) & (found < EMAX)

        @pl.when(mine)
        def _():
            meta[1 + found] = end - anchor
            rank = count[owner]
            meta[5 + found] = jnp.where(rank < CAP, owner * CAP + rank, -1)
            count[owner] = rank + 1

        return found + mine.astype(jnp.int32), end, jnp.where(end <= anchor, end, start)

    zero = jnp.int32(0)
    _, _, start = lax.fori_loop(0, bounds.shape[1], one, (zero, zero, zero))
    meta[0] = start - anchor


def states_kernel(
    shard_ref, bounds, owners, x_ref, rim_ref, w_ref, bias_ref, move_ref, slot_ref,
    dt_ref, ld_ref, rep_ref, rep16_ref, tri_ref,
    act_ref, b_ref, c_ref, cum_ref, carry_ref, sin_ref, pay_ref, meta,
    edge16, weights, moves, state, total, count,
):
    step = pl.program_id(0)
    heads = dt_ref.shape[0]
    width = rep_ref.shape[1]
    span = pl.num_programs(0) * BLOCK
    parts = BLOCK // CHUNK
    first = step * BLOCK

    @pl.when(step == 0)
    def _():
        read_docs(bounds, owners, meta, count, shard_ref[0] * span, span)
        edge16[...] = rim_ref[...]
        weights[0:4] = 0.5 * w_ref[...]
        weights[4:5] = 0.5 * bias_ref[...].reshape(1, weights.shape[1])
        moves[0] = move_ref[...]
        state[...] = jnp.zeros_like(state)
        total[...] = jnp.zeros_like(total)

    choices = []
    for part in range(parts):
        begin = first + part * CHUNK
        near = (meta[0] > begin - 3) & (meta[0] < begin + CHUNK)
        for slot in range(EMAX):
            near = near | ((meta[1 + slot] > begin - 3) & (meta[1 + slot] < begin + CHUNK))

        @pl.when(near)
        def _():
            tick = slot_ref[...] // 4 + begin
            kept = (tick - starts_of(meta, tick) >= slot_ref[...] % 4).astype(F32)
            moves[1 + part, :, :128] = (kept * move_ref[:, :128].astype(F32)).astype(BF16)
            moves[1 + part, :, 128:] = (kept[:, :16] * move_ref[:, 128:].astype(F32)).astype(BF16)

        choices.append(jnp.where(near, 1 + part, 0))

    for part in range(parts):
        low = part * CHUNK
        rows = slice(low, low + CHUNK)
        pick = moves[choices[part]]
        for tile in range(x_ref.shape[1] // 256):
            cols = slice(tile * 256, tile * 256 + 256)
            if part:
                wide = x_ref[low - 16 : low + CHUNK, cols]
            else:
                wide = jnp.concatenate([edge16[:, cols], x_ref[rows, cols]], axis=0)
            moved = jnp.dot(pick, wide, preferred_element_type=F32)
            moved = moved.reshape(CHUNK // 8, 3, 8, 256)
            mixed = weights[4:5, cols] + weights[0:1, cols] * x_ref[rows, cols].astype(F32)
            for lag in range(1, 4):
                mixed = mixed + weights[lag : lag + 1, cols] * moved[:, lag - 1].reshape(CHUNK, 256)
            value = (mixed + mixed * jnp.tanh(mixed)).astype(BF16)
            if tile * 256 < act_ref.shape[1]:
                act_ref[rows, cols] = value
            else:
                b_ref[rows, :] = value[:, :N]
                c_ref[rows, :] = value[:, N:]

    edge16[...] = x_ref[BLOCK - 16 :, :]

    spans = [slice(part * CHUNK, part * CHUNK + CHUNK) for part in range(parts)]
    pieces = jnp.concatenate([thirds(ld_ref[:, rows] * LOG2E) for rows in spans], axis=0)
    summed = jnp.dot(pieces, tri_ref[...], preferred_element_type=F32)
    open_end = jnp.where(meta[0] < 0, meta[1], -1)
    running = total[...]
    scales = []
    throughs = []
    for part, rows in enumerate(spans):
        begin = first + part * CHUNK
        at = 3 * heads * part
        cum = summed[at : at + heads] + summed[at + heads : at + 2 * heads] + summed[at + 2 * heads : at + 3 * heads]
        cum_ref[:, rows] = cum
        lane = iota((heads, CHUNK), 1) + begin
        carry_ref[:, rows] = jnp.where(lane < open_end, jnp.exp2(running + cum), 0.0)
        start = last_start(meta, begin + CHUNK - 1)
        last = cum[:, CHUNK - 1 :]
        weight = jnp.where(lane >= start, jnp.exp2(last - cum) * dt_ref[:, rows], 0.0)
        scales.append(weight.T.astype(BF16))
        throughs.append(spread_row(jnp.where(start < begin, jnp.exp2(last), 0.0), rep_ref[...]))
        running = running + last
    total[...] = running
    weight = jnp.concatenate(scales, axis=0)
    turned = [b_ref[rows, :].T for rows in spans]
    for tile in range(width // 256):
        cols = slice(tile * 256, tile * 256 + 256)
        scale = jnp.dot(weight, rep16_ref[:heads, cols], preferred_element_type=F32)
        load = scale.astype(BF16) * act_ref[:, cols]
        held = state[:, cols]
        for part, rows in enumerate(spans):
            sin_ref[part, :, cols] = held.astype(BF16)
            grown = jnp.dot(turned[part], load[rows], preferred_element_type=F32)
            held = throughs[part][:, cols] * held + grown
        state[:, cols] = held

    @pl.when(step == pl.num_programs(0) - 1)
    def _():
        start = last_start(meta, span - 1)
        gate = spread_row(jnp.where(start < 0, jnp.exp2(total[:, :1]), 0.0), rep_ref[...])
        gate = jnp.broadcast_to(gate, (PAY - N, width))
        high = gate.astype(BF16).astype(F32)
        pay_ref[:N] = state[...].astype(BF16)
        pay_ref[N:] = jnp.where(iota((PAY - N, width), 0) == 0, high, gate - high).astype(BF16)


def finals_kernel(
    meta, act_hbm, b_hbm, sin_hbm, x_hbm, rim_ref, dt_ref, cum_ref, carry_ref, rep_ref, rep16_ref,
    fin_hbm, first_ref,
    act_held, b_held, sin_held, x_held, edge_held, blank, made, lines, in_sem, blank_sem, made_sem,
):
    heads, span = dt_ref.shape
    width = rep_ref.shape[1]

    def place(slot):
        return pl.multiple_of((meta[1 + slot] - 1) // CHUNK * CHUNK, CHUNK)

    def copies(slot):
        low = place(slot)
        rows = pl.ds(low, CHUNK)
        before = pl.ds(pl.multiple_of(jnp.maximum(low - 16, 0), 16), 16)
        pairs = (
            (act_hbm.at[rows], act_held), (b_hbm.at[rows], b_held), (sin_hbm.at[low // CHUNK], sin_held),
            (x_hbm.at[rows], x_held), (x_hbm.at[before], edge_held),
        )
        return [
            pltpu.make_async_copy(source, target.at[slot], in_sem.at[slot, index])
            for index, (source, target) in enumerate(pairs)
        ]

    def fetch(slot, _):
        for copy in copies(slot):
            copy.start()
        return 0

    found = jnp.int32(0)
    for slot in range(EMAX):
        found = found + (meta[1 + slot] <= span).astype(jnp.int32)
    lax.fori_loop(0, found, fetch, 0)
    blank[...] = jnp.zeros_like(blank)
    blanks = [
        pltpu.make_async_copy(blank, fin_hbm.at[index], blank_sem.at[index])
        for index in range(fin_hbm.shape[0])
    ]
    for copy in blanks:
        copy.start()
    first_ref[...] = jnp.zeros_like(first_ref)
    lines[...] = jnp.zeros_like(lines)
    for copy in blanks:
        copy.wait()

    def finish(slot, _):
        for copy in copies(slot):
            copy.wait()
        end = meta[1 + slot]
        start = jnp.where(slot > 0, meta[jnp.maximum(slot, 1)], meta[0])
        low = place(slot)
        there = pl.ds(low, CHUNK)
        lane = iota((heads, CHUNK), 1) + low
        cum = cum_ref[:, there]
        at_end = jnp.sum(jnp.where(lane == end - 1, cum, 0.0), axis=1, keepdims=True)
        inside = (lane < end) & (lane >= start)
        weight = jnp.exp2(jnp.minimum(at_end - cum, 0.0)) * dt_ref[:, there]
        weight = jnp.where(inside, weight, 0.0).T.astype(BF16)
        scale = jnp.dot(weight, rep16_ref[:heads], preferred_element_type=F32)
        load = scale.astype(BF16) * act_held[slot]
        local = outer_dot(b_held[slot], load)
        through = spread_row(jnp.where(start < low, jnp.exp2(at_end), 0.0), rep_ref[...])
        final = local + through * sin_held[slot].astype(F32)
        target = meta[5 + slot]

        @pl.when((slot == 0) & (start < 0))
        def _():
            opened = jnp.sum(jnp.where(lane == end - 1, carry_ref[:, there], 0.0), axis=1, keepdims=True)
            first_ref[...] = jnp.broadcast_to(spread_row(opened, rep_ref[...]), first_ref.shape)

        row = iota((16, CHUNK), 0)
        col = iota((16, CHUNK), 1) + low
        pick = (col == end - 3 + row) & (col >= start) & (row < 3)
        row16 = iota((16, 16), 0)
        col16 = iota((16, 16), 1) + low - 16
        pick16 = (col16 == end - 3 + row16) & (col16 >= start) & (row16 < 3)
        rim = jnp.where(low > 0, edge_held[slot].astype(F32), rim_ref[...].astype(F32))
        last = jnp.dot(
            pick.astype(F32).astype(BF16), x_held[slot], preferred_element_type=F32
        ) + jnp.dot(pick16.astype(F32).astype(BF16), rim.astype(BF16), preferred_element_type=F32)
        tiles = x_held.shape[2] // 128
        for index in range(3):
            for tile in range(tiles):
                at = index * tiles + tile
                lines[at : at + 1] = last[index : index + 1, tile * 128 : tile * 128 + 128]

        @pl.when(target >= 0)
        def _():
            made[slot, :width] = final.astype(BF16).T
            made[slot, width:] = lines[...].astype(BF16)
            pltpu.make_async_copy(made.at[slot], fin_hbm.at[target], made_sem.at[slot]).start()

        return 0

    lax.fori_loop(0, found, finish, 0)

    def close(slot, _):
        @pl.when(meta[5 + slot] >= 0)
        def _():
            pltpu.make_async_copy(made.at[slot], fin_hbm.at[meta[5 + slot]], made_sem.at[slot]).wait()

        return 0

    lax.fori_loop(0, found, close, 0)


def output_kernel(origin, meta, act_ref, b_ref, c_ref, dt_ref, cum_ref, sin_ref, gain_in, rep_ref, rep16_ref, *refs):
    out_ref, gain_ref = refs[-2:]
    step = origin + pl.program_id(0)
    heads = dt_ref.shape[0]
    width = out_ref.shape[1]
    parts = BLOCK // CHUNK

    @pl.when(pl.program_id(0) == 0)
    def _():
        row = jnp.zeros((1, width), F32)
        for head in range(heads):
            row = row + gain_in[head] * rep_ref[head : head + 1, :]
        gain_ref[...] = row

    for part in range(parts):
        begin = step * BLOCK + part * CHUNK
        rows = slice(part * CHUNK, part * CHUNK + CHUNK)
        cum = cum_ref[:, rows]
        back = cum - jnp.log2(dt_ref[:, rows])
        ahead = cum.T
        b_act = b_ref[rows, :]
        c_act = c_ref[rows, :]
        place = iota((CHUNK, CHUNK), 0) + begin
        other = iota((CHUNK, CHUNK), 1) + begin
        scores = lax.dot_general(c_act, b_act, (((1,), (1,)), ((), ())), preferred_element_type=F32)
        scores = jnp.where((other <= place) & (other >= starts_of(meta, place)), scores, 0.0)
        lane = iota((heads, CHUNK), 1) + begin
        before = jnp.where(last_start(meta, begin) < begin, next_end(meta, begin), -1)
        entry = jnp.where(lane < before, jnp.exp2(cum), 0.0)
        entry = jnp.concatenate([entry, entry - entry.astype(BF16).astype(F32)], axis=0).T.astype(BF16)
        left_half = iota((CHUNK, 128), 1) < P_SIZE
        for quad in range(heads // 4):
            cols = slice(quad * 256, quad * 256 + 256)
            outer = jnp.dot(c_act, sin_ref[part, :, cols], preferred_element_type=F32)
            scale = jnp.dot(entry, rep16_ref[:, cols], preferred_element_type=F32)
            sums = []
            for pair in (2 * quad, 2 * quad + 1):
                mixes = []
                for head in (2 * pair, 2 * pair + 1):
                    spread = jnp.minimum(ahead[:, head : head + 1] - back[head : head + 1, :], 0.0)
                    mixes.append((jnp.exp2(spread) * scores).astype(BF16))
                mix = jnp.concatenate(mixes, axis=1)
                x_pair = act_ref[rows, pair * 128 : pair * 128 + 128]
                zero = jnp.zeros_like(x_pair)
                split = jnp.concatenate(
                    [jnp.where(left_half, x_pair, zero), jnp.where(left_half, zero, x_pair)], axis=0
                )
                sums.append(jnp.dot(mix, split, preferred_element_type=F32))
            inner = jnp.concatenate(sums, axis=1)
            value = inner + scale * outer + gain_ref[:, cols] * act_ref[rows, cols].astype(F32)
            out_ref[rows, cols] = value.astype(BF16)


def gates_of(pay_ref, cols):
    gates = pay_ref[N:, cols].astype(F32)
    return gates[0:1] + gates[1:2]


def pair_kernel(shard_ref, own_ref, got_ref, half_ref):
    side = half_ref.shape[1]

    def join(early, late, cols):
        after = gates_of(late, cols)
        gate = jnp.broadcast_to(after * gates_of(early, cols), (PAY - N, side))
        high = gate.astype(BF16).astype(F32)
        half_ref[:N] = (late[:N, cols].astype(F32) + after * early[:N, cols].astype(F32)).astype(BF16)
        half_ref[N:] = jnp.where(iota((PAY - N, side), 0) == 0, high, gate - high).astype(BF16)

    @pl.when(shard_ref[0] % 2 == 0)
    def _():
        join(own_ref, got_ref, slice(0, side))

    @pl.when(shard_ref[0] % 2 == 1)
    def _():
        join(got_ref, own_ref, slice(side, 2 * side))


def prefix_kernel(*refs):
    prefix_ref = refs[-1]
    side = prefix_ref.shape[1]
    total = jnp.zeros((N, side), F32)
    for ref in refs[:-1]:
        total = gates_of(ref, slice(0, side)) * total + ref[:N].astype(F32)
    prefix_ref[...] = total.astype(BF16)


def carry_kernel(shard_ref, stream_ref, meta, mine_ref, other_ref, early_ref, first_ref, carried_ref, *sends):
    side = mine_ref.shape[1]
    lower, upper = slice(0, side), slice(side, 2 * side)

    @pl.when(shard_ref[0] % 2 == 0)
    def _():
        carried_ref[:, lower] = mine_ref[...]
        carried_ref[:, upper] = other_ref[...]

    @pl.when(shard_ref[0] % 2 == 1)
    def _():
        for cols, part in ((lower, other_ref), (upper, mine_ref)):
            carried_ref[:, cols] = (
                early_ref[:N, cols].astype(F32) + gates_of(early_ref, cols) * part[...].astype(F32)
            ).astype(BF16)

    value = (first_ref[0:1] * carried_ref[...].astype(F32)).T.astype(BF16)
    apart = (meta[5] // CAP) ^ stream_ref[0]
    for index, ref in enumerate(sends):
        ref[...] = jnp.where(apart == index, value, jnp.zeros_like(value))


def correct_kernel(meta, base_hbm, c_ref, carry_ref, carried_ref, rep16_ref, out_hbm, held, in_sem, out_sem):
    steps, _, width = held.shape
    reach = jnp.where(meta[0] < 0, jnp.minimum(meta[1], steps * BLOCK), 0)
    touched = (reach + BLOCK - 1) // BLOCK

    def copy(index, source, target, sem):
        place = pl.ds(pl.multiple_of(index * BLOCK, BLOCK), BLOCK)
        if source is held:
            return pltpu.make_async_copy(held.at[index], target.at[place], sem.at[index])
        return pltpu.make_async_copy(source.at[place], held.at[index], sem.at[index])

    def fetch(index, _):
        copy(index, base_hbm, held, in_sem).start()
        return 0

    def add(index, _):
        copy(index, base_hbm, held, in_sem).wait()
        rows = pl.ds(pl.multiple_of(index * BLOCK, BLOCK), BLOCK)
        entry = carry_ref[:, rows]
        entry = jnp.concatenate([entry, entry - entry.astype(BF16).astype(F32)], axis=0).T.astype(BF16)
        c_act = c_ref[rows, :]
        for tile in range(width // 256):
            cols = slice(tile * 256, tile * 256 + 256)
            outer = jnp.dot(c_act, carried_ref[:, cols], preferred_element_type=F32)
            scale = jnp.dot(entry, rep16_ref[:, cols], preferred_element_type=F32)
            held[index, :, cols] = (held[index, :, cols].astype(F32) + scale * outer).astype(BF16)
        copy(index, held, out_hbm, out_sem).start()
        return 0

    def close(index, _):
        copy(index, held, out_hbm, out_sem).wait()
        return 0

    lax.fori_loop(0, touched, fetch, 0)
    lax.fori_loop(0, touched, add, 0)
    lax.fori_loop(0, touched, close, 0)


def params(mib):
    return pltpu.CompilerParams(vmem_limit_bytes=mib * MIB)


def whole(shape):
    return pl.BlockSpec(shape, lambda *_: (0,) * len(shape))


def on_device(
    conv_input, conv_weight, conv_bias, step_size, log_decay, skip_gain, doc_bounds, doc_owner
):
    span, channels = conv_input.shape[1:]
    heads = step_size.shape[1]
    width = heads * P_SIZE
    steps = span // BLOCK
    chunks = span // CHUNK
    owners = lax.axis_size("stream")
    slots = owners * CAP
    rows = width + TAIL
    shard = lax.axis_index("seq").astype(jnp.int32).reshape(1)
    rows_in = conv_input[0]
    rim = shifted(rows_in[span - 16 :], "seq", 1)
    rep = (np.arange(width)[None, :] // P_SIZE == np.arange(heads)[:, None]).astype(np.float32)
    rep16 = np.concatenate([rep, rep], 0).astype(BF16)
    ticks = np.arange(CHUNK)
    tri = (ticks[:, None] <= ticks[None, :]).astype(BF16)
    order = np.arange(3 * CHUNK)
    tick, lag = 8 * (order // 24) + order % 8, order % 24 // 8 + 1
    source = np.arange(CHUNK + 16)
    move = (source[None, :] - 16 == (tick - lag)[:, None]).astype(BF16)
    slot = np.broadcast_to((4 * tick + lag)[:, None], (3 * CHUNK, 128)).astype(np.int32)
    smem = pl.BlockSpec(memory_space=pltpu.SMEM)
    stream = lax.axis_index("stream").astype(jnp.int32).reshape(1)
    per_head = pl.BlockSpec((heads, BLOCK), lambda i, *_: (0, i))
    prefetch = functools.partial(pltpu.PrefetchScalarGridSpec, num_scalar_prefetch=1)
    by_rows = pl.BlockSpec((BLOCK, channels), lambda i, *_: (i, 0))
    by_width = pl.BlockSpec((BLOCK, width), lambda i, *_: (i, 0))
    by_rest = pl.BlockSpec((BLOCK, N), lambda i, *_: (i, 0))
    in_hbm = pl.BlockSpec(memory_space=pl.ANY)
    act, b_act, c_act, cum, carry, sin, pay, meta = pl.pallas_call(
        states_kernel,
        grid=(steps,),
        in_specs=[
            smem, smem, smem, by_rows, whole((16, channels)),
            whole((4, channels)), whole((channels,)), whole(move.shape), whole(slot.shape),
            per_head, per_head, whole((heads, width)), whole((2 * heads, width)), whole((CHUNK, CHUNK)),
        ],
        out_specs=[
            by_width, by_rest, by_rest, per_head, per_head,
            pl.BlockSpec((BLOCK // CHUNK, N, width), lambda i, *_: (i, 0, 0)),
            whole((PAY, width)), smem,
        ],
        out_shape=[
            jax.ShapeDtypeStruct((span, width), BF16),
            jax.ShapeDtypeStruct((span, N), BF16),
            jax.ShapeDtypeStruct((span, N), BF16),
            jax.ShapeDtypeStruct((heads, span), F32),
            jax.ShapeDtypeStruct((heads, span), F32),
            jax.ShapeDtypeStruct((chunks, N, width), BF16),
            jax.ShapeDtypeStruct((PAY, width), BF16),
            jax.ShapeDtypeStruct((16,), jnp.int32),
        ],
        scratch_shapes=[
            pltpu.VMEM((16, channels), BF16),
            pltpu.VMEM((8, channels), F32),
            pltpu.VMEM((1 + BLOCK // CHUNK,) + move.shape, BF16),
            pltpu.VMEM((N, width), F32),
            pltpu.VMEM((heads, CHUNK), F32),
            pltpu.SMEM((owners,), jnp.int32),
        ],
        compiler_params=params(60),
        cost_estimate=pl.CostEstimate(
            flops=2 * span * channels * 600, bytes_accessed=32 << 20, transcendentals=span * channels
        ),
        name="states",
    )(
        shard, doc_bounds, doc_owner, rows_in, rim, conv_weight, conv_bias, move, slot,
        step_size[0], log_decay[0], rep, rep16, tri,
    )

    def outputs(first, last, *held):
        rows_of = functools.partial(pl.BlockSpec, index_map=lambda i, *_: (first + i, 0))
        heads_of = pl.BlockSpec((heads, BLOCK), lambda i, *_: (0, first + i))
        return pl.pallas_call(
            functools.partial(output_kernel, first),
            grid_spec=prefetch(
                grid=(last - first,),
                in_specs=[
                    rows_of((BLOCK, width)), rows_of((BLOCK, N)), rows_of((BLOCK, N)), heads_of, heads_of,
                    pl.BlockSpec((BLOCK // CHUNK, N, width), lambda i, *_: (first + i, 0, 0)),
                    smem, whole((heads, width)), whole((2 * heads, width)),
                ] + [in_hbm] * len(held),
                out_specs=rows_of((BLOCK, width)),
                scratch_shapes=[pltpu.VMEM((1, width), F32)],
            ),
            out_shape=jax.ShapeDtypeStruct((span, width), BF16),
            input_output_aliases={10: 0} if held else {},
            compiler_params=params(60),
            cost_estimate=pl.CostEstimate(
                flops=2 * (last - first) * BLOCK * width * N * 4,
                bytes_accessed=(last - first) * (4 << 20),
                transcendentals=(last - first) * BLOCK * CHUNK * heads,
            ),
            name="outputs",
        )(meta, act, b_act, c_act, step_size[0], cum, sin, skip_gain, rep, rep16, *held)

    side = width // 2
    count = lax.axis_size("seq")
    pairs = [(index, index ^ 1) for index in range(count)]
    early = lax.ppermute(pay, "seq", pairs)
    half = pl.pallas_call(
        pair_kernel,
        in_specs=[smem, whole((PAY, width)), whole((PAY, width))],
        out_specs=whole((PAY, side)),
        out_shape=jax.ShapeDtypeStruct((PAY, side), BF16),
        compiler_params=params(8),
        name="pair",
    )(shard, pay, early)
    chips = count // 2
    behind = [shifted(half, "seq", 2 * far) for far in range(chips - 1, 0, -1)]
    scanned, half = lax.optimization_barrier((sin, half))
    fin, first = pl.pallas_call(
        finals_kernel,
        in_specs=[
            smem, in_hbm, in_hbm, in_hbm, in_hbm, whole((16, channels)),
            whole((heads, span)), whole((heads, span)), whole((heads, span)),
            whole((heads, width)), whole((2 * heads, width)),
        ],
        out_specs=[in_hbm, whole((8, width))],
        out_shape=[
            jax.ShapeDtypeStruct((slots, rows, N), BF16),
            jax.ShapeDtypeStruct((8, width), F32),
        ],
        scratch_shapes=[
            pltpu.VMEM((EMAX, CHUNK, width), BF16),
            pltpu.VMEM((EMAX, CHUNK, N), BF16),
            pltpu.VMEM((EMAX, N, width), BF16),
            pltpu.VMEM((EMAX, CHUNK, channels), BF16),
            pltpu.VMEM((EMAX, 16, channels), BF16),
            pltpu.VMEM((rows, N), BF16),
            pltpu.VMEM((EMAX, rows, N), BF16),
            pltpu.VMEM((TAIL, N), F32),
            pltpu.SemaphoreType.DMA((EMAX, 5)),
            pltpu.SemaphoreType.DMA((slots,)),
            pltpu.SemaphoreType.DMA((EMAX,)),
        ],
        compiler_params=params(58),
        cost_estimate=pl.CostEstimate(flops=1 << 28, bytes_accessed=6 << 20, transcendentals=0),
        name="finals",
    )(meta, act, b_act, scanned, rows_in, rim, step_size[0], cum, carry, rep, rep16)
    sin, fin = lax.optimization_barrier((sin, fin))
    got = lax.all_to_all(
        fin.reshape(owners, CAP, rows, N), "stream", split_axis=0, concat_axis=0, tiled=True
    )
    base = outputs(0, steps - 2)
    *behind, base = lax.optimization_barrier((*behind, base))
    mine = pl.pallas_call(
        prefix_kernel,
        in_specs=[whole((PAY, side))] * len(behind),
        out_specs=whole((N, side)),
        out_shape=jax.ShapeDtypeStruct((N, side), BF16),
        compiler_params=params(8),
        name="prefix",
    )(*behind)
    other = lax.ppermute(mine, "seq", pairs)
    other, got = lax.optimization_barrier((other, got))
    carried, *send = pl.pallas_call(
        carry_kernel,
        in_specs=[smem, smem, smem, whole((N, side)), whole((N, side)), whole((PAY, width)), whole((8, width))],
        out_specs=[whole((N, width))] + [whole((width, N))] * owners,
        out_shape=[jax.ShapeDtypeStruct((N, width), BF16)]
        + [jax.ShapeDtypeStruct((width, N), BF16)] * owners,
        compiler_params=params(8),
        name="carry",
    )(shard, stream, meta, mine, other, early, first)
    more = [send[0]]
    for apart in range(1, owners):
        swap = [(index, index ^ apart) for index in range(owners)]
        more.append(lax.ppermute(send[apart], "stream", swap))

    carried, base = lax.optimization_barrier((carried, base))
    base = outputs(steps - 2, steps, base)
    out = pl.pallas_call(
        correct_kernel,
        in_specs=[smem, in_hbm, whole((span, N)), whole((heads, span)), whole((N, width)), whole((2 * heads, width))],
        out_specs=in_hbm,
        out_shape=jax.ShapeDtypeStruct((span, width), BF16),
        scratch_shapes=[
            pltpu.VMEM((steps, BLOCK, width), BF16),
            pltpu.SemaphoreType.DMA((steps,)),
            pltpu.SemaphoreType.DMA((steps,)),
        ],
        input_output_aliases={1: 0},
        compiler_params=params(58),
        cost_estimate=pl.CostEstimate(
            flops=2 * span * width * N, bytes_accessed=18 << 20, transcendentals=0
        ),
        name="correct",
    )(meta, base, c_act, carry, carried, rep16)

    apart = (jnp.arange(owners) ^ stream)[:, None, None]
    extra = jnp.broadcast_to(more[0][None], (owners, width, N))
    for index in range(1, owners):
        extra = jnp.where(apart == index, more[index][None], extra)
    ranks = jnp.arange(CAP)[None, :, None, None]
    extra = jnp.where(ranks == 0, extra[:, None], jnp.zeros_like(extra[:, None]))
    ssm = got[:, :, :width].astype(F32) + extra.astype(F32)
    ssm = ssm.reshape(1, 1, owners, CAP, heads, P_SIZE, N)
    tiles = channels // N
    conv = got[:, :, width : width + 3 * tiles].reshape(1, 1, owners, CAP, 3, channels)
    return out[None], ssm, conv


def solution(mesh):
    in_specs = (
        P("stream", "seq", None),
        P(),
        P(),
        P("stream", None, "seq"),
        P("stream", None, "seq"),
        P(),
        P("stream", None),
        P("stream", None),
    )
    out_specs = (
        P("stream", "seq", None),
        P("stream", "seq", None, None, None, None, None),
        P("stream", "seq", None, None, None, None),
    )
    return jax.shard_map(
        on_device, mesh=mesh, in_specs=in_specs, out_specs=out_specs, check_vma=False
    )
```
